128 devices in a mesh: ctx: 64 (over x, z_lo, y, core), fsdp: 2 (over z_hi).
Axes of the slice: x: 4, y: 4, z: 4 (z_hi: 2, z_lo: 2; z = z_hi * 2 + z_lo), core: 2. Of those that a mesh axis runs over, the one named last changes fastest.
Arguments:
- hidden_in: bfloat16 [2, 8192, 768], P('fsdp', 'ctx'), may hold values from -6 to 6
- doc_lengths: int32 [2, 2, 8], P('fsdp'), may hold values from 1 to 2048, as said below
- norm_gain: bfloat16 [2, 2, 768], P(None, None, 'fsdp'), may hold values from 0.25 to 1.75
- norm_bias: bfloat16 [2, 2, 768], P(None, None, 'fsdp'), may hold values from -1.796875 to 1.796875
- qkv_weight: bfloat16 [2, 768, 2304], P(None, 'fsdp'), may hold values from -0.21875 to 0.21875
- qkv_bias: bfloat16 [2, 2304], P(None, 'fsdp'), may hold values from -3 to 3
- out_weight: bfloat16 [2, 768, 768], P(None, 'fsdp'), may hold values from -0.875 to 0.875
- out_bias: bfloat16 [2, 768], P(None, 'fsdp'), may hold values from -3 to 3
- up_weight: bfloat16 [2, 768, 3072], P(None, 'fsdp'), may hold values from -0.21875 to 0.21875
- up_bias: bfloat16 [2, 3072], P(None, 'fsdp'), may hold values from -3 to 3
- down_weight: bfloat16 [2, 3072, 768], P(None, 'fsdp'), may hold values from -0.109375 to 0.109375
- down_bias: bfloat16 [2, 768], P(None, 'fsdp'), may hold values from -3 to 3
- cotangent: bfloat16 [2, 8192, 768], P('fsdp', 'ctx'), may hold values from -6 to 6
Outputs:
- hidden_out: bfloat16 [2, 8192, 768], P('fsdp', 'ctx')
- hidden_grad: float32 [2, 8192, 768], P('fsdp', 'ctx')
- norm_gain_grad: float32 [2, 2, 768], P(None, None, 'fsdp')
- norm_bias_grad: float32 [2, 2, 768], P(None, None, 'fsdp')
- qkv_weight_grad: float32 [2, 768, 2304], P(None, 'fsdp')
- qkv_bias_grad: float32 [2, 2304], P(None, 'fsdp')
- out_weight_grad: float32 [2, 768, 768], P(None, 'fsdp')
- out_bias_grad: float32 [2, 768], P(None, 'fsdp')
- up_weight_grad: float32 [2, 768, 3072], P(None, 'fsdp')
- up_bias_grad: float32 [2, 3072], P(None, 'fsdp')
- down_weight_grad: float32 [2, 3072, 768], P(None, 'fsdp')
- down_bias_grad: float32 [2, 768], P(None, 'fsdp')
The draws below stay inside these ranges and needn't reach their ends.
Inputs may be any that keep to these rules, and one draw needn't show every extreme that they name: `doc_lengths`: row [g, s] holds the lengths of the 8 documents that fill sequence s of group g, in order; they sum to 4096, the last is end padding of 1 to 32 tokens, and the one before it is 2048 long, the largest of the row.
All inputs are finite; a program needn't handle non-finite values.
Results may differ from the reference program's by a relative error of at most 0.013.
Values may be sent and summed in bfloat16 or wider, within the bound.
No kernel may reach another device: no remote copies, remote signals or barrier semaphores. Data moves between devices by JAX's collectives and lax.ppermute only.
A program may use at most 384 MiB of HBM per device.

```python
import math
import jax
import jax.numpy as jnp
from jax import lax

D = 768
HEADS = 12
HEAD = 64
FF = 3072
ROT = 16
LAYERS = 2
WINDOW = 1024
DOCS = 8
BLOCK = 64
STREAM = 8192
SEQ_LEN = 4096
SEQS = 2
GROUPS = 2
N_CTX = 64


def draw_doc_lengths(key, part):
    key = jax.random.fold_in(key, 11)
    row_count = GROUPS * SEQS
    pad_key = jax.random.fold_in(key, 1)
    cut_key = jax.random.fold_in(key, 2)
    padding = jax.random.randint(pad_key, (row_count, 1), 1, max(1, BLOCK // 2) + 1).astype(jnp.int32)
    remain = SEQ_LEN - SEQ_LEN // 2 - padding
    spare = remain - (DOCS - 2)
    raw_cuts = jax.random.randint(cut_key, (row_count, DOCS - 3), 0, 65536).astype(jnp.int32)
    cuts = jnp.sort(raw_cuts * (spare + 1) // 65536, axis=-1)
    edges = jnp.concatenate([jnp.zeros((row_count, 1), jnp.int32), cuts, spare], axis=-1)
    pieces = edges[:, 1:] - edges[:, :-1] + 1
    longest = jnp.full((row_count, 1), SEQ_LEN // 2, jnp.int32)
    lengths = jnp.concatenate([pieces, longest, padding], axis=-1)
    return lengths.reshape(GROUPS, SEQS, DOCS).astype(jnp.int32)


def shard_levels(own_key, shape, split, least, top_value):
    def one(position, blocks):
        steps = jax.random.uniform(jax.random.fold_in(jax.random.fold_in(own_key, 6), position), (blocks,), jnp.float32, least / len(split), top_value / len(split))
        return jnp.repeat(jnp.exp(steps), shape[position] // blocks).reshape((-1,) + (1,) * (len(shape) - position - 1))

    level = one(*split[0])
    for cut in split[1:]:
        level = level * one(*cut)
    return level


def noise(key, shape, deviation, most, shards=(), kind=jnp.bfloat16):
    values = deviation * jax.random.normal(key, shape, jnp.float32)
    if shards:
        values = values * shard_levels(key, shape, shards, -0.22, 0.18)
    return jnp.clip(values, -most, most).astype(kind)


def setup_inputs(seed: int = 0) -> dict:
    arg_keys = jax.random.split(jax.random.key(seed), 14)
    return {
        "hidden_in": noise(arg_keys[0], (GROUPS, STREAM, D), 1.0, 6.0, ((0, 2), (1, 64))),
        "doc_lengths": draw_doc_lengths(jax.random.fold_in(arg_keys[13], 71), 0),
        "norm_gain": jnp.clip(1.0 + 0.15 * jax.random.normal(arg_keys[2], (LAYERS, 2, D), jnp.float32), 0.25, 1.75).astype(jnp.bfloat16),
        "norm_bias": noise(arg_keys[3], (LAYERS, 2, D), 0.3, 1.796875, ((2, 2),)),
        "qkv_weight": noise(arg_keys[4], (LAYERS, D, 3 * D), D ** -0.5, 0.21875, ((1, 2),)),
        "qkv_bias": noise(arg_keys[5], (LAYERS, 3 * D), 0.5, 3.0, ((1, 2),)),
        "out_weight": noise(arg_keys[6], (LAYERS, D, D), (D // 16) ** -0.5, 0.875, ((1, 2),)),
        "out_bias": noise(arg_keys[7], (LAYERS, D), 0.5, 3.0, ((1, 2),)),
        "up_weight": noise(arg_keys[8], (LAYERS, D, FF), D ** -0.5, 0.21875, ((1, 2),)),
        "up_bias": noise(arg_keys[9], (LAYERS, FF), 0.5, 3.0, ((1, 2),)),
        "down_weight": noise(arg_keys[10], (LAYERS, FF, D), FF ** -0.5, 0.109375, ((1, 2),)),
        "down_bias": noise(arg_keys[11], (LAYERS, D), 0.5, 3.0, ((1, 2),)),
        "cotangent": noise(arg_keys[12], (GROUPS, STREAM, D), 1.0, 6.0, ((0, 2), (1, 64))),
    }


@jax.custom_vjp
def low(v):
    return lax.optimization_barrier(v.astype(jnp.bfloat16)).astype(jnp.float32)

@jax.custom_vjp
def low_back(v):
    return v

def low_keep(v):
    return (low(v), None)

def low_pass(kept, grad):
    return (grad,)

def back_keep(v):
    return (v, None)

def back_low(kept, grad):
    return (low(grad),)
low.defvjp(low_keep, low_pass)
low_back.defvjp(back_keep, back_low)
highest = lax.Precision.HIGHEST
blocked_value = -1e+30
norm_epsilon = 1e-05

def layer_norm(values, scales, offsets):
    centered = values - lax.optimization_barrier(jnp.mean(values, axis=-1, keepdims=True))
    spread = lax.optimization_barrier(jnp.mean(centered * centered, axis=-1, keepdims=True))
    return centered * lax.rsqrt(spread + norm_epsilon) * scales + offsets

def rotate(values, cosine, sine_table):
    half_width = ROT // 2
    front_part = values[..., :ROT]
    turned = jnp.concatenate([-front_part[..., half_width:], front_part[..., :half_width]], axis=-1)
    return jnp.concatenate([front_part * cosine + turned * sine_table, values[..., ROT:]], axis=-1)

def rotary_tables(places):
    frequency = 1.0 / 10000.0 ** (jnp.arange(0, ROT, 2).astype(jnp.float32) / ROT)
    angles = places.astype(jnp.float32)[..., None] * frequency
    angles = jnp.concatenate([angles, angles], axis=-1)
    return (jnp.cos(angles), jnp.sin(angles))

def sequence_meta(doc_row):
    offsets = jnp.arange(SEQ_LEN, dtype=jnp.int32)
    doc_ends = jnp.cumsum(doc_row)
    before = doc_ends[None, :] <= offsets[:, None]
    segment = lax.optimization_barrier(jnp.sum(before.astype(jnp.int32), axis=-1))
    starts = lax.optimization_barrier(jnp.sum(jnp.where(before, doc_row[None, :], 0), axis=-1))
    return (segment, offsets - starts, segment == DOCS - 1)

def attention(queries, keys, vals, segment, padding):
    query_rows = min(512, SEQ_LEN)
    block_count = SEQ_LEN // query_rows
    score_scale = 1.0 / math.sqrt(HEAD)
    keys_padded = jnp.concatenate([jnp.zeros((WINDOW, HEADS, HEAD), keys.dtype), keys], axis=0)
    vals_padded = jnp.concatenate([jnp.zeros((WINDOW, HEADS, HEAD), vals.dtype), vals], axis=0)
    segment_padded = jnp.concatenate([jnp.full((WINDOW,), -1, jnp.int32), segment.astype(jnp.int32)])
    padding_padded = jnp.concatenate([jnp.zeros((WINDOW,), bool), padding])

    def one_block(block_index):
        start = (block_index * query_rows).astype(jnp.int32)
        query_part = lax.dynamic_slice_in_dim(queries, start, query_rows, 0)
        key_part = lax.dynamic_slice_in_dim(keys_padded, start, WINDOW + query_rows, 0)
        value_part = lax.dynamic_slice_in_dim(vals_padded, start, WINDOW + query_rows, 0)
        key_segment = lax.dynamic_slice_in_dim(segment_padded, start, WINDOW + query_rows, 0)
        key_padding = lax.dynamic_slice_in_dim(padding_padded, start, WINDOW + query_rows, 0)
        query_segment = lax.dynamic_slice_in_dim(segment.astype(jnp.int32), start, query_rows, 0)
        query_pos = start + jnp.arange(query_rows, dtype=jnp.int32)
        key_pos = start - WINDOW + jnp.arange(WINDOW + query_rows, dtype=jnp.int32)
        distance = query_pos[:, None] - key_pos[None, :]
        allowed = (query_segment[:, None] == key_segment[None, :]) & (distance >= 0) & (distance < WINDOW) & (jnp.logical_not(key_padding)[None, :] | (distance == 0))
        scores = low_back(jnp.einsum('qhd,khd->hqk', query_part, key_part, precision=highest) * score_scale)
        scores = jnp.where(allowed[None], scores, blocked_value)
        row_total = jax.nn.logsumexp(scores, axis=-1, keepdims=True)
        probs = jnp.exp(scores - row_total)
        return jnp.einsum('hqk,khd->qhd', low(probs), value_part, precision=highest)
    blocks = lax.map(jax.checkpoint(one_block), jnp.arange(block_count, dtype=jnp.int32))
    return blocks.reshape(SEQ_LEN, HEADS, HEAD)

def layer(stream, weight_set, segment, places, padding):
    scales, offsets, w_qkv, b_qkv, w_out, b_out, w_up, b_up, w_down, b_down = weight_set
    first_low = low(layer_norm(stream, scales[0], offsets[0]))
    second_low = low(layer_norm(stream, scales[1], offsets[1]))
    mixed_proj = low_back(jnp.dot(first_low, w_qkv, precision=highest) + b_qkv)
    cosine, sine_table = rotary_tables(places)
    cosine = cosine[:, None, :]
    sine_table = sine_table[:, None, :]
    queries = low(rotate(mixed_proj[:, :D].reshape(SEQ_LEN, HEADS, HEAD), cosine, sine_table))
    keys = low(rotate(mixed_proj[:, D:2 * D].reshape(SEQ_LEN, HEADS, HEAD), cosine, sine_table))
    vals = low(mixed_proj[:, 2 * D:].reshape(SEQ_LEN, HEADS, HEAD))
    context = low_back(low(attention(queries, keys, vals, segment, padding).reshape(SEQ_LEN, D)))
    attn_out = low_back(jnp.dot(context, w_out, precision=highest) + b_out)
    upward = low_back(jnp.dot(second_low, w_up, precision=highest) + b_up)
    hidden_low = low(jax.nn.gelu(upward, approximate=False))
    mlp_out = low_back(jnp.dot(hidden_low, w_down, precision=highest) + b_down)
    return stream + attn_out + mlp_out

def reference(hidden_in, doc_lengths, norm_gain, norm_bias, qkv_weight, qkv_bias, out_weight, out_bias, up_weight, up_bias, down_weight, down_bias, cotangent):
    params = tuple((item.astype(jnp.float32) for item in (norm_gain, norm_bias, qkv_weight, qkv_bias, out_weight, out_bias, up_weight, up_bias, down_weight, down_bias)))

    def natural(array):
        blocks = array.reshape(GROUPS, N_CTX, 2, BLOCK, D)
        ordered = jnp.concatenate([blocks[:, :, 0], jnp.flip(blocks[:, :, 1], axis=1)], axis=1)
        return ordered.reshape(GROUPS * SEQS, SEQ_LEN, D)

    def stored(array):
        blocks = array.reshape(GROUPS, 2 * N_CTX, BLOCK, D)
        paired = jnp.stack([blocks[:, :N_CTX], jnp.flip(blocks[:, N_CTX:], axis=1)], axis=2)
        return paired.reshape(GROUPS, STREAM, D)
    inputs_nat = natural(hidden_in.astype(jnp.float32))
    cotangent_nat = natural(cotangent.astype(jnp.float32))
    doc_rows = doc_lengths.reshape(GROUPS * SEQS, DOCS).astype(jnp.int32)

    def forward(stream, weight_all, doc_row):
        segment, places, padding = sequence_meta(doc_row)
        for layer_index in range(LAYERS):
            stream = layer(stream, tuple((item[layer_index] for item in weight_all)), segment, places, padding)
        return stream

    def per_sequence(totals, items):
        stream, stream_cot, doc_row = items
        result, pullback = jax.vjp(lambda first_arg, second_arg: forward(first_arg, second_arg, doc_row), stream, params)
        grad_stream, grad_weights = pullback(stream_cot)
        return (tuple((acc + extra for acc, extra in zip(totals, grad_weights))), (result, grad_stream))
    zero_grads = tuple((jnp.zeros_like(item) for item in params))
    totals, (results, grads) = lax.scan(per_sequence, zero_grads, (inputs_nat, cotangent_nat, doc_rows))
    return (stored(results).astype(jnp.bfloat16), stored(grads), totals[0], totals[1], totals[2], totals[3], totals[4], totals[5], totals[6], totals[7], totals[8], totals[9])
```

```python
import functools

import jax
import jax.numpy as jnp
from jax import lax
from jax.experimental import pallas as pl
from jax.experimental.pallas import tpu as pltpu
from jax.sharding import Mesh
from jax.sharding import PartitionSpec as P

D = 768
HALF = D // 2
HEADS = 12
HEAD = 64
FF = 3072
ROT = 16
LAYERS = 2
WINDOW = 1024
DOCS = 8
TILE = 128
TILES = 16
UNIT = TILE * TILES
SLOTS = 8
CORE_HEADS = HEADS // 2
QKV = 3 * HEAD
QKV_ROWS = CORE_HEADS * QKV
CORE_FF = FF // 2
QUARTER = FF // 4

CHUNK_UP = 96
CHUNK_DOWN = 48
CHUNK_OUT = 16
CHUNK = CHUNK_UP + 2 * CHUNK_DOWN + 2 * CHUNK_OUT
GRAD_UP = 4 * HALF
GRAD_DOWN = 2 * QUARTER
GRAD_OUT = HALF
GRAD_M = 32 * 112
GRAD_Q = 32 * 40

BLOCKED = -1e30
EPSILON = 1e-05
SWAP = [(0, 1), (1, 0)]
F32 = jnp.float32
BF16 = jnp.bfloat16

NN = (((1,), (0,)), ((), ()))
NT = (((1,), (1,)), ((), ()))
TN = (((0,), (0,)), ((), ()))


def dot(left, right, dims=NN):
    return lax.dot_general(left, right, dims, preferred_element_type=F32)


def shape(dims, kind):
    return jax.ShapeDtypeStruct(dims, kind)


def block(dims, *at):
    place = at[0] if at else (lambda s: (0,) * len(dims))
    return pl.BlockSpec(dims, lambda i, s: place(s))


def whole(array):
    return block(array.shape)


def run(kernel, scalars, inputs, outs, name, flops, moved, scratch=(), limit=40, aliases=None, exps=0, out_specs=None):
    arrays = [item[0] if isinstance(item, tuple) else item for item in inputs]
    specs = [item[1] if isinstance(item, tuple) else whole(item) for item in inputs]
    if out_specs is None:
        out_specs = [block(out.shape) for out in outs]
    return pl.pallas_call(
        kernel,
        grid_spec=pltpu.PrefetchScalarGridSpec(
            num_scalar_prefetch=1,
            grid=(1,),
            in_specs=specs,
            out_specs=out_specs,
            scratch_shapes=list(scratch),
        ),
        out_shape=outs,
        input_output_aliases=aliases or {},
        compiler_params=pltpu.CompilerParams(vmem_limit_bytes=limit * 1024 * 1024),
        cost_estimate=pl.CostEstimate(flops=flops, bytes_accessed=moved, transcendentals=exps),
        name=name,
    )(scalars, *arrays)


CORE, ZH, REVERSE, SWAPPED, FIRST_HALF, LAST_CHIP = range(6)


def half_at(index):
    return pl.ds(pl.multiple_of(index * HALF, HALF), HALF)


def turn_kernel(at, raw_ref, out_ref):
    def turn(core):
        for part in range(3):
            for z in range(2):
                start = part * D + z * HALF + core * QKV
                piece = raw_ref[0, :, start : start + QKV].T
                for head in range(3):
                    row = (z * 3 + head) * QKV + part * HEAD
                    out_ref[row : row + HEAD, :] = piece[head * HEAD : (head + 1) * HEAD]

    for core in range(2):
        pl.when(at[CORE] == core)(functools.partial(turn, core))


def turn_qkv(at, qkv_weight, layer):
    spec = block((1, HALF, 3 * D), lambda s: (layer, 0, 0))
    return run(
        turn_kernel, at, [(qkv_weight, spec)], [shape((QKV_ROWS, HALF), BF16)], "turn_qkv", 0, 2700000
    )[0]


def fill_up(z, up_ref, own0_ref, own1_ref, rest_ref):
    up_ref[half_at(z), 0:QUARTER] = own0_ref[0]
    up_ref[half_at(z), QUARTER:] = own1_ref[0]
    for chunk in range(16):
        x, y = chunk // 4, chunk % 4
        rows = pl.ds(pl.multiple_of((1 - z) * HALF + CHUNK_UP * x, 32), CHUNK_UP)
        up_ref[rows, y * HALF : (y + 1) * HALF] = rest_ref[chunk]


def fill_down(z, down_ref, own_ref, rest_ref):
    down_ref[pl.ds(pl.multiple_of(z * QUARTER, QUARTER), QUARTER), :] = own_ref[0]
    for chunk in range(16):
        rows = pl.ds(pl.multiple_of((1 - z) * QUARTER + CHUNK_DOWN * chunk, 16), CHUNK_DOWN)
        down_ref[rows, 0:HALF] = rest_ref[chunk, 0:CHUNK_DOWN]
        down_ref[rows, HALF:] = rest_ref[chunk, CHUNK_DOWN:]


def fill_out(z, out_ref, own_ref, rest_ref):
    out_ref[pl.ds(pl.multiple_of(z * QKV, QKV), QKV), :] = own_ref[0]
    for chunk in range(QKV // CHUNK_OUT):
        rows = pl.ds(pl.multiple_of((1 - z) * QKV + CHUNK_OUT * chunk, 16), CHUNK_OUT)
        out_ref[rows, 0:HALF] = rest_ref[chunk, 0:CHUNK_OUT]
        out_ref[rows, HALF:] = rest_ref[chunk, CHUNK_OUT:]


def up_inputs(weights, rest, layer):
    own = [
        (weights, block((1, HALF, QUARTER), lambda s, z=z: (layer, 0, 2 * z + s[CORE]))) for z in range(2)
    ]
    return own + [(rest, block((16, CHUNK_UP, HALF), lambda s: (0, 0, 0)))]


def down_inputs(weights, rest, layer):
    return [
        (weights, block((1, QUARTER, D), lambda s: (layer, s[CORE], 0))),
        (rest, block((16, 2 * CHUNK_DOWN, HALF), lambda s: (0, 1, 0))),
    ]


def out_inputs(weights, rest, layer):
    return [
        (weights, block((1, QKV, D), lambda s: (layer, s[CORE], 0))),
        (rest, block((16, 2 * CHUNK_OUT, HALF), lambda s: (0, 6, 0))),
    ]


def norm_kernel(at, *refs, first):
    if first:
        stream_ref, gain_ref, offset_ref, hat_ref, inverse_ref, act_ref = refs
        stream = stream_ref[...].astype(F32)
    else:
        stream_ref, keep_ref, got_ref, bias_ref, gain_ref, offset_ref, next_ref, hat_ref, inverse_ref, act_ref = refs
        stream = stream_ref[...].astype(F32) + (keep_ref[...] + got_ref[...] + bias_ref[...])
        next_ref[...] = stream
    centered = stream - jnp.mean(stream, axis=-1, keepdims=True)
    inverse = lax.rsqrt(jnp.mean(centered * centered, axis=-1, keepdims=True) + EPSILON)
    hat = centered * inverse
    hat_ref[...] = hat
    inverse_ref[...] = inverse
    act_ref[:, 0:D] = (hat * gain_ref[0:1] + offset_ref[0:1]).astype(BF16)
    act_ref[:, D:] = (hat * gain_ref[1:2] + offset_ref[1:2]).astype(BF16)


def norms(at, stream, added, gain, offset):
    outs = [shape((TILE, D), F32), shape((TILE, 1), F32), shape((TILE, 2 * D), BF16)]
    if added is None:
        kernel = functools.partial(norm_kernel, first=True)
        return [None, *run(kernel, at, [stream, gain, offset], outs, "norms", 1000000, 1200000)]
    kernel = functools.partial(norm_kernel, first=False)
    outs = [shape((TILE, D), F32)] + outs
    return run(kernel, at, [stream, *added, gain, offset], outs, "norms", 1000000, 2400000)


def assemble(target_ref, mine, theirs):
    rows = TILE // 2
    target_ref[0:rows] = mine[:rows]
    target_ref[rows : 2 * rows] = theirs[:rows]
    target_ref[2 * rows : 3 * rows] = mine[rows:]
    target_ref[3 * rows :] = theirs[rows:]


def qkv_kernel(at, mine_ref, theirs_ref, own_ref, other_ref, bias_ref, cos_ref, sin_ref, out_ref, tok_ref, act_t):
    z = at[ZH]
    assemble(tok_ref, mine_ref[...], theirs_ref[...])
    act_t[...] = tok_ref[...].T
    cosine, sine = cos_ref[...], sin_ref[...]

    def turned(part):
        low, high = part[:8], part[8:ROT]
        return jnp.concatenate(
            [low * cosine - high * sine, high * cosine + low * sine, part[ROT:]], axis=0
        )

    own_act, other_act = act_t[half_at(z), :], act_t[half_at(1 - z), :]
    for head in range(CORE_HEADS):
        rows = slice(head * QKV, (head + 1) * QKV)
        value = dot(own_ref[rows, :], own_act) + dot(other_ref[rows, :], other_act)
        bias = jnp.broadcast_to(bias_ref[head : head + 1, :], (8, QKV)).T
        value = value + bias[:, 0:1]
        query = (turned(value[:HEAD]).astype(BF16).astype(F32) * 0.125).astype(BF16)
        key = turned(value[HEAD : 2 * HEAD]).astype(BF16)
        val = value[2 * HEAD :].astype(BF16)
        for seq in range(2):
            lanes = slice(seq * TILE, (seq + 1) * TILE)
            out_ref[seq, head, 0:HEAD, :] = query[:, lanes]
            out_ref[seq, head, HEAD : 2 * HEAD, :] = key[:, lanes]
            out_ref[seq, head, 2 * HEAD :, :] = val[:, lanes]
    for seq in range(2):
        out_ref[seq, CORE_HEADS:] = jnp.zeros((SLOTS - CORE_HEADS, QKV, TILE), BF16)


def project_qkv(at, mine, theirs, own, other, bias, cosine, sine):
    left = block((TILE, D), lambda s: (0, 0))
    return run(
        qkv_kernel,
        at,
        [(mine, left), (theirs, left), own, other, bias, cosine, sine],
        [shape((2, SLOTS, QKV, TILE), BF16)],
        "qkv",
        4 * TILE * D * QKV_ROWS,
        3500000,
        [pltpu.VMEM((2 * TILE, D), BF16), pltpu.VMEM((D, 2 * TILE), BF16)],
        limit=24,
    )[0]


def mlp_kernel(
    at, mine_ref, theirs_ref, bias_ref, up0_ref, up1_ref, up_rest, down_own, down_rest, gate_ref, slope_ref, sum_ref, act, up, down
):
    z = at[ZH]
    act[0:TILE] = mine_ref[...]
    act[TILE:] = theirs_ref[...]
    fill_up(z, up, up0_ref, up1_ref, up_rest)
    fill_down(z, down, down_own, down_rest)
    total = jnp.zeros((2 * TILE, D), F32)
    for part in range(4):
        lanes = slice(part * HALF, (part + 1) * HALF)
        value = dot(act[...], up[:, lanes]) + bias_ref[:, lanes]
        normal = 0.5 * (1.0 + lax.erf(value * 0.7071067811865476))
        gate = (value * normal).astype(BF16)
        gate_ref[:, lanes] = gate
        slope_ref[:, lanes] = normal + value * (jnp.exp(-0.5 * value * value) * 0.3989422804014327)
        total = total + dot(gate, down[lanes, :])
    sum_ref[...] = total


def feed_forward(at, mine, theirs, bias, up, down, rest, layer):
    right = block((TILE, D), lambda s: (0, 1))
    tokens = 2 * TILE
    return run(
        mlp_kernel,
        at,
        [(mine, right), (theirs, right), bias, *up_inputs(up, rest, layer), *down_inputs(down, rest, layer)],
        [shape((tokens, CORE_FF), BF16), shape((tokens, CORE_FF), F32), shape((tokens, D), F32)],
        "mlp",
        4 * tokens * D * CORE_FF,
        8500000,
        [pltpu.VMEM((tokens, D), BF16), pltpu.VMEM((D, CORE_FF), BF16), pltpu.VMEM((CORE_FF, D), BF16)],
        limit=40,
        exps=2 * tokens * CORE_FF,
    )


def key_range(pair):
    first = max(-1, 2 * pair - WINDOW // TILE)
    return first, 2 * pair + 2


PAIRS_OF_TILES = sum(2 * (key_range(pair)[1] - key_range(pair)[0]) for pair in range(TILES // 2))


def allowed_mask(pair, first, last, low_row, pos_row, place):
    parts = []
    for tile in range(first, last):
        ok = place >= low_row - TILE * tile
        if tile >= 2 * pair:
            ok = ok & (place <= pos_row - TILE * tile)
        parts.append(ok)
    return jnp.concatenate(parts, axis=0)


def unturned(grads, cosine, sine):
    low, high = grads[:8], grads[8:ROT]
    return jnp.concatenate(
        [low * cosine + high * sine, high * cosine - low * sine, grads[ROT:]], axis=0
    ).astype(BF16)


def attention_kernel(at, *refs, forward, backward):
    refs = list(refs)
    take = lambda count: [refs.pop(0) for _ in range(count)]
    got_ref, halo_ref, low_ref, pos_ref = take(4)
    if backward:
        dctx_ref, cos_ref, sin_ref = take(3)
        if not forward:
            saved_ctx, saved_lse = take(2)
    if forward:
        (out_ref,) = take(1)
        if not backward:
            ctx_ref, lse_ref = take(2)
    if backward:
        packed_ref, edge_ref, tail_ref = take(3)
    key_tok, query_t = take(2)
    if forward:
        (val_t,) = take(1)
    if backward:
        val_tok, key_t, query_tok, dctx_t, dctx_tok, dkv = take(6)

    reverse = at[REVERSE]
    place = lax.broadcasted_iota(jnp.int32, (TILE, 2 * TILE), 0) ^ at[SWAPPED]

    def chip(tile):
        return jnp.where(reverse == 1, TILES - 1 - tile, tile)

    for tile in range(-1, TILES):
        here = slice(tile * TILE, (tile + 1) * TILE)
        after = slice((tile + 1) * TILE, (tile + 2) * TILE)
        if tile < 0:
            key, val = halo_ref[0:HEAD, :], halo_ref[HEAD:, :]
        else:
            source = chip(tile)
            query, key, val = (got_ref[source, part * HEAD : (part + 1) * HEAD, :] for part in range(3))
            query_t[:, here] = query
            if backward:
                query_tok[here, :] = query.T
                dctx = dctx_ref[source]
                dctx_t[:, here] = dctx
                dctx_tok[here, :] = dctx.T
        key_tok[after, :] = key.T
        if forward:
            val_t[:, after] = val
        if backward:
            key_t[:, after] = key
            val_tok[after, :] = val.T
    if backward:
        dkv[...] = jnp.zeros_like(dkv)
    for pair in range(TILES // 2):
        first, last = key_range(pair)
        rows = slice((first + 1) * TILE, (last + 1) * TILE)
        lanes = slice(pair * 2 * TILE, (pair + 1) * 2 * TILE)
        places = chip(2 * pair), chip(2 * pair + 1)
        scores = dot(key_tok[rows, :], query_t[:, lanes])
        ok = allowed_mask(pair, first, last, low_ref[:, lanes], pos_ref[:, lanes], place)
        scores = jnp.where(ok, scores, BLOCKED)
        if forward:
            peak = jnp.max(scores, axis=0, keepdims=True)
            probs = jnp.exp(scores - peak)
            total = jnp.sum(probs, axis=0, keepdims=True)
            inverse = 1.0 / total
            ctx = dot(val_t[:, rows], probs.astype(BF16)) * inverse
            low_ctx = ctx.astype(BF16)
            out_ref[places[0]] = low_ctx[:, :TILE]
            out_ref[places[1]] = low_ctx[:, TILE:]
            if backward:
                probs = probs * inverse
            else:
                ctx_ref[:, lanes] = ctx
                lse_ref[:, lanes] = peak + jnp.log(total)
        else:
            probs = jnp.exp(scores - saved_lse[:, lanes])
            ctx = saved_ctx[:, lanes]
        if backward:
            dctx = dctx_t[:, lanes]
            dprobs = dot(val_tok[rows, :], dctx)
            delta = jnp.sum(ctx * dctx.astype(F32), axis=0, keepdims=True)
            dscores = (probs * (dprobs - delta)).astype(BF16)
            dquery = dot(key_t[:, rows], dscores) * 0.125
            dquery = unturned(dquery, cos_ref[:, lanes], sin_ref[:, lanes])
            packed_ref[places[0], 0:HEAD, :] = dquery[:, :TILE]
            packed_ref[places[1], 0:HEAD, :] = dquery[:, TILE:]
            dkv[rows, 0:HEAD] += dot(dscores, query_tok[lanes, :])
            dkv[rows, HEAD:] += dot(probs.astype(BF16), dctx_tok[lanes, :])
    if backward:
        edge_ref[...] = dkv[0:TILE, :]
        tail_ref[...] = dkv[TILES * TILE :, :]
        for tile in range(TILES - 1):
            lanes = slice(tile * TILE, (tile + 1) * TILE)
            grads = dkv[(tile + 1) * TILE : (tile + 2) * TILE, :].T
            packed_ref[chip(tile), HEAD:, :] = unturned(grads, cos_ref[:, lanes], sin_ref[:, lanes])
        packed_ref[chip(TILES - 1), HEAD:, :] = jnp.zeros((2 * HEAD, TILE), BF16)


def attention(at, got, halo, low, pos, dctx=None, tables=None, saved=None):
    forward, backward = saved is None, dctx is not None
    keys = UNIT + TILE
    inputs = [got, halo, low, pos]
    outs = []
    scratch = [pltpu.VMEM((keys, HEAD), BF16), pltpu.VMEM((HEAD, UNIT), BF16)]
    if forward:
        scratch.append(pltpu.VMEM((HEAD, keys), BF16))
        outs.append(shape((TILES, HEAD, TILE), BF16))
        if not backward:
            outs += [shape((HEAD, UNIT), F32), shape((1, UNIT), F32)]
    if backward:
        inputs += [dctx, *tables]
        if saved is not None:
            inputs += list(saved)
        outs += [shape((TILES, QKV, TILE), BF16), shape((TILE, 2 * HEAD), F32), shape((TILE, 2 * HEAD), F32)]
        scratch += [
            pltpu.VMEM((keys, HEAD), BF16),
            pltpu.VMEM((HEAD, keys), BF16),
            pltpu.VMEM((UNIT, HEAD), BF16),
            pltpu.VMEM((HEAD, UNIT), BF16),
            pltpu.VMEM((UNIT, HEAD), BF16),
            pltpu.VMEM((keys, 2 * HEAD), F32),
        ]
    products = (2 if forward else 1) + (4 if backward else 0)
    return run(
        functools.partial(attention_kernel, forward=forward, backward=backward),
        at,
        inputs,
        outs,
        "attention" + ("_forward" if forward else "") + ("_backward" if backward else ""),
        2 * products * PAIRS_OF_TILES * TILE * TILE * HEAD * 4,
        4000000,
        scratch,
        exps=PAIRS_OF_TILES * TILE * TILE,
    )


def edge_kernel(at, packed_ref, tail_ref, edge_ref, cos_ref, sin_ref, out_ref):
    grads = tail_ref[...] + jnp.where(at[FIRST_HALF] == 1, edge_ref[...], 0.0)
    out_ref[0, 0:HEAD, :] = packed_ref[0, 0:HEAD, :]
    out_ref[0, HEAD:, :] = unturned(grads.T, cos_ref[...], sin_ref[...])


def add_edge(at, packed, tail, edge, cosine, sine):
    spec = block((1, QKV, TILE), lambda s: (s[LAST_CHIP], 0, 0))
    last = block((8, TILE), lambda s: (0, TILES - 1))
    return run(
        edge_kernel,
        at,
        [(packed, spec), tail, edge, (cosine, last), (sine, last)],
        [shape(packed.shape, BF16)],
        "attention_edge",
        100000,
        300000,
        limit=8,
        aliases={1: 0},
        out_specs=[spec],
    )[0]


def out_kernel(at, got_ref, own_ref, rest_ref, sum_ref, keep_ref, give_ref, weights):
    fill_out(at[ZH], weights, own_ref, rest_ref)
    rows = TILE // 2
    for seq in range(2):
        ctx = got_ref[seq * SLOTS : seq * SLOTS + CORE_HEADS].reshape(HALF, TILE)
        value = dot(ctx, weights[...], TN)
        here = slice(seq * rows, (seq + 1) * rows)
        there = slice(TILE + seq * rows, TILE + (seq + 1) * rows)
        keep_ref[here, :] = value[:rows] + sum_ref[here, :]
        give_ref[here, :] = value[rows:] + sum_ref[there, :]


def attention_out(at, got, weights, rest, total, layer):
    return run(
        out_kernel,
        at,
        [got, *out_inputs(weights, rest, layer), total],
        [shape((TILE, D), F32), shape((TILE, D), F32)],
        "attention_out",
        4 * TILE * HALF * D,
        2700000,
        [pltpu.VMEM((HALF, D), BF16)],
        limit=24,
    )


def dctx_kernel(at, mine_ref, theirs_ref, own_ref, rest_ref, out_ref, weights, tok):
    fill_out(at[ZH], weights, own_ref, rest_ref)
    assemble(tok, mine_ref[...], theirs_ref[...])
    value = dot(weights[...], tok[...], NT).astype(BF16)
    for seq in range(2):
        out_ref[seq, 0:CORE_HEADS] = value[:, seq * TILE : (seq + 1) * TILE].reshape(CORE_HEADS, HEAD, TILE)
        out_ref[seq, CORE_HEADS:] = jnp.zeros((SLOTS - CORE_HEADS, HEAD, TILE), BF16)


def grad_ctx(at, mine, theirs, weights, rest, layer):
    return run(
        dctx_kernel,
        at,
        [mine, theirs, *out_inputs(weights, rest, layer)],
        [shape((2, SLOTS, HEAD, TILE), BF16)],
        "grad_ctx",
        4 * TILE * HALF * D,
        1300000,
        [pltpu.VMEM((HALF, D), BF16), pltpu.VMEM((2 * TILE, D), BF16)],
        limit=24,
    )[0]


def mlp_back_kernel(
    at, mine_ref, theirs_ref, slope_ref, up0_ref, up1_ref, up_rest, down_own, down_rest, dup_ref, keep_ref, give_ref, bias_ref, dhid, up, down
):
    z = at[ZH]
    dhid[0:TILE] = mine_ref[...]
    dhid[TILE:] = theirs_ref[...]
    fill_up(z, up, up0_ref, up1_ref, up_rest)
    fill_down(z, down, down_own, down_rest)
    total = jnp.zeros((2 * TILE, D), F32)
    for part in range(4):
        lanes = slice(part * HALF, (part + 1) * HALF)
        value = dot(dhid[...], down[lanes, :], NT) * slope_ref[:, lanes]
        dup = value.astype(BF16)
        dup_ref[:, lanes] = dup
        bias_ref[part : part + 1, :] = jnp.sum(dup.astype(F32), axis=0, keepdims=True)
        total = total + dot(dup, up[:, lanes], NT)
    keep_ref[...] = total[:TILE]
    give_ref[...] = total[TILE:]


def mlp_back(at, mine, theirs, slope, up, down, rest, layer):
    tokens = 2 * TILE
    return run(
        mlp_back_kernel,
        at,
        [mine, theirs, slope, *up_inputs(up, rest, layer), *down_inputs(down, rest, layer)],
        [shape((tokens, CORE_FF), BF16), shape((TILE, D), F32), shape((TILE, D), F32), shape((4, HALF), F32)],
        "mlp_back",
        4 * tokens * D * CORE_FF,
        8500000,
        [pltpu.VMEM((tokens, D), BF16), pltpu.VMEM((D, CORE_FF), BF16), pltpu.VMEM((CORE_FF, D), BF16)],
        limit=40,
    )


def mlp_grads_kernel(
    at, act_mine, act_theirs, mine_ref, theirs_ref, gate_ref, dup_ref, ctx_ref, out_ref, act_t, dhid, tok, gate_t
):
    act_t[:, 0:TILE] = act_mine[...].T
    act_t[:, TILE:] = act_theirs[...].T
    dhid[0:TILE] = mine_ref[...]
    dhid[TILE:] = theirs_ref[...]
    assemble(tok, mine_ref[...], theirs_ref[...])
    gate_t[...] = gate_ref[...].T
    for z in range(2):
        for part in range(4):
            lanes = slice(part * HALF, (part + 1) * HALF)
            out_ref[z, lanes, :] = dot(act_t[z * HALF : (z + 1) * HALF, :], dup_ref[:, lanes]).astype(BF16)
        for side in range(2):
            lanes = slice(side * HALF, (side + 1) * HALF)
            start = GRAD_UP + side * QUARTER
            out_ref[z, start : start + QUARTER, :] = dot(
                gate_t[z * QUARTER : (z + 1) * QUARTER, :], dhid[:, lanes]
            ).astype(BF16)
            value = jnp.zeros((QKV, HALF), F32)
            for seq in range(2):
                ctx = ctx_ref[seq * SLOTS + 3 * z : seq * SLOTS + 3 * z + 3].reshape(QKV, TILE)
                value = value + dot(ctx, tok[seq * TILE : (seq + 1) * TILE, lanes])
            start = GRAD_UP + GRAD_DOWN + side * QKV
            out_ref[z, start : start + QKV, :] = value.astype(BF16)
        used = GRAD_UP + GRAD_DOWN + GRAD_OUT
        out_ref[z, used:, :] = jnp.zeros((GRAD_M - used, HALF), BF16)


def mlp_grads(at, mine, theirs, dmine, dtheirs, gate, dup, ctx):
    right = block((TILE, D), lambda s: (0, 1))
    tokens = 2 * TILE
    return run(
        mlp_grads_kernel,
        at,
        [(mine, right), (theirs, right), dmine, dtheirs, gate, dup, ctx],
        [shape((2, GRAD_M, HALF), BF16)],
        "mlp_grads",
        2 * tokens * 2 * GRAD_M * HALF,
        8000000,
        [
            pltpu.VMEM((D, tokens), BF16),
            pltpu.VMEM((tokens, D), BF16),
            pltpu.VMEM((tokens, D), BF16),
            pltpu.VMEM((CORE_FF, tokens), BF16),
        ],
        limit=40,
    )[0]


def qkv_back_kernel(at, got_ref, own_ref, other_ref, keep_ref, give_ref, bias_ref):
    z = at[ZH]
    rows = TILE // 2
    sums = jnp.zeros((8, QKV_ROWS), F32)
    for seq in range(2):
        tok = got_ref[seq * SLOTS : seq * SLOTS + CORE_HEADS].reshape(QKV_ROWS, TILE).T
        sums = sums + dot(jnp.ones((8, TILE), BF16), tok)
        here = slice(seq * rows, (seq + 1) * rows)
        for weights, at_z in ((own_ref, z), (other_ref, 1 - z)):
            value = dot(tok, weights[...])
            keep_ref[here, half_at(at_z)] = value[:rows]
            give_ref[here, half_at(at_z)] = value[rows:]
    bias_ref[...] = sums


def qkv_back(at, got, own, other):
    return run(
        qkv_back_kernel,
        at,
        [got, own, other],
        [shape((TILE, D), F32), shape((TILE, D), F32), shape((8, QKV_ROWS), F32)],
        "qkv_back",
        4 * TILE * D * QKV_ROWS,
        3500000,
        limit=24,
    )


def qkv_grads_kernel(at, got_ref, mine_ref, theirs_ref, out_ref, tok):
    assemble(tok, mine_ref[...], theirs_ref[...])
    for z in range(2):
        lanes = slice(z * HALF, (z + 1) * HALF)
        value = jnp.zeros((QKV_ROWS, HALF), F32)
        for seq in range(2):
            grads = got_ref[seq * SLOTS : seq * SLOTS + CORE_HEADS].reshape(QKV_ROWS, TILE)
            value = value + dot(grads, tok[seq * TILE : (seq + 1) * TILE, lanes])
        out_ref[z, 0:QKV_ROWS, :] = value.astype(BF16)
        out_ref[z, QKV_ROWS:, :] = jnp.zeros((GRAD_Q - QKV_ROWS, HALF), BF16)


def qkv_grads(at, got, mine, theirs):
    left = block((TILE, D), lambda s: (0, 0))
    return run(
        qkv_grads_kernel,
        at,
        [got, (mine, left), (theirs, left)],
        [shape((2, GRAD_Q, HALF), BF16)],
        "qkv_grads",
        4 * TILE * D * QKV_ROWS,
        3000000,
        [pltpu.VMEM((2 * TILE, D), BF16)],
        limit=24,
    )[0]


def norm_back_kernel(
    at, keep0, got0, keep1, got1, hat_ref, inverse_ref, gain_ref, dstream_ref, next_ref, low_ref, sums_ref
):
    first, second = keep0[...] + got0[...], keep1[...] + got1[...]
    hat = hat_ref[...]
    dstream = dstream_ref[...].astype(F32)
    dhat = first * gain_ref[0:1] + second * gain_ref[1:2]
    grad = inverse_ref[...] * (
        dhat
        - jnp.mean(dhat, axis=-1, keepdims=True)
        - hat * jnp.mean(dhat * hat, axis=-1, keepdims=True)
    )
    total = dstream + grad
    next_ref[...] = total
    low_ref[...] = total.astype(BF16)
    rows = (first * hat, second * hat, first, second, dstream.astype(BF16).astype(F32))
    for index, value in enumerate(rows):
        row = jnp.sum(value, axis=0, keepdims=True)
        sums_ref[2 * index : 2 * index + 1, :] = row[:, :HALF]
        sums_ref[2 * index + 1 : 2 * index + 2, :] = row[:, HALF:]


def norm_back(at, first, second, hat, inverse, gain, dstream):
    return run(
        norm_back_kernel,
        at,
        [*first, *second, hat, inverse, gain, dstream],
        [shape((TILE, D), F32), shape((TILE, D), BF16), shape((10, HALF), F32)],
        "norm_back",
        2000000,
        3400000,
        limit=24,
    )


def place_mlp_kernel(at, *refs):
    mine_ref, theirs_ref = refs[:2]
    up_ref, down_ref, out_ref = refs[-3:]
    for mine, source in ((True, mine_ref), (False, theirs_ref)):
        def put(core, source=source):
            for z in range(2):
                for side in range(2):
                    column = z * CORE_FF + core * QUARTER + side * HALF
                    row = (2 * z + side) * HALF
                    up_ref[0, :, column : column + HALF] = source[row : row + HALF, :].astype(F32)
            for side in range(2):
                lanes = slice(side * HALF, (side + 1) * HALF)
                row = GRAD_UP + side * QUARTER
                down_ref[0, core * QUARTER : (core + 1) * QUARTER, lanes] = source[row : row + QUARTER, :].astype(F32)
                row = GRAD_UP + GRAD_DOWN + side * QKV
                out_ref[0, core * QKV : (core + 1) * QKV, lanes] = source[row : row + QKV, :].astype(F32)

        for core in range(2):
            pl.when((at[CORE] == core) == mine)(functools.partial(put, core))


def place_mlp(at, mine, theirs, layer, filled):
    outs = [shape((LAYERS, HALF, FF), F32), shape((LAYERS, FF // 2, D), F32), shape((LAYERS, HALF, D), F32)]
    specs = [block((1,) + out.shape[1:], lambda s: (layer, 0, 0)) for out in outs]
    inputs = [mine, theirs]
    aliases = {}
    if filled is not None:
        inputs += [(array, pl.BlockSpec(memory_space=pl.ANY)) for array in filled]
        aliases = {3: 0, 4: 1, 5: 2}
    return run(
        place_mlp_kernel, at, inputs, outs, "place_mlp", 0, 16000000, limit=40, aliases=aliases, out_specs=specs
    )


def place_qkv_kernel(at, *refs):
    mine_ref, theirs_ref = refs[:2]
    out_ref, rows_ref = refs[-2:]
    for part in range(3):
        for z in range(2):
            for mine, source in ((True, mine_ref), (False, theirs_ref)):
                def put(core, source=source):
                    for head in range(3):
                        row = (z * 3 + head) * QKV + part * HEAD
                        to = core * QKV + head * HEAD
                        rows_ref[to : to + HEAD, :] = source[row : row + HEAD, :].astype(F32)

                for core in range(2):
                    pl.when((at[CORE] == core) == mine)(functools.partial(put, core))
            column = part * D + z * HALF
            out_ref[0, :, column : column + HALF] = rows_ref[...].T


def place_qkv(at, mine, theirs, layer, filled):
    out = shape((LAYERS, HALF, 3 * D), F32)
    inputs = [mine, theirs]
    aliases = {}
    if filled is not None:
        inputs.append((filled, pl.BlockSpec(memory_space=pl.ANY)))
        aliases = {3: 0}
    return run(
        place_qkv_kernel,
        at,
        inputs,
        [out],
        "place_qkv",
        0,
        6000000,
        [pltpu.VMEM((HALF, HALF), F32)],
        limit=40,
        aliases=aliases,
        out_specs=[block((1, HALF, 3 * D), lambda s: (layer, 0, 0))],
    )[0]


ROW_GAIN, ROW_OFFSET, ROW_QKV, ROW_OUT, ROW_UP, ROW_DOWN, SMALL_ROWS = 0, 4, 8, 14, 16, 24, 32


def gather_small_kernel(at, gain_ref, offset_ref, qkv_ref, out_ref, up_ref, down_ref, rows_ref):
    rows_ref[...] = jnp.zeros((SMALL_ROWS, HALF), F32)
    rows_ref[ROW_GAIN : ROW_GAIN + 4] = gain_ref[...].astype(F32).reshape(4, HALF)
    rows_ref[ROW_OFFSET : ROW_OFFSET + 4] = offset_ref[...].astype(F32).reshape(4, HALF)
    rows_ref[ROW_OUT : ROW_OUT + LAYERS] = out_ref[...].astype(F32)
    rows_ref[ROW_DOWN : ROW_DOWN + LAYERS] = down_ref[...].astype(F32)
    for ref, start, count in ((qkv_ref, ROW_QKV, 3), (up_ref, ROW_UP, 4)):
        values = ref[...].astype(F32)
        for layer in range(LAYERS):
            for part in range(count):
                row = start + layer * count + part
                rows_ref[row : row + 1] = values[layer : layer + 1, part * HALF : (part + 1) * HALF]


def spread_small_kernel(at, own_ref, other_ref, gain_ref, offset_ref, qkv_ref, rest_ref, up_ref):
    own, other = own_ref[...], other_ref[...]
    swap = at[ZH] == 1
    halves = jnp.where(swap, other, own), jnp.where(swap, own, other)

    def row(index, z):
        return halves[z][index : index + 1]

    def by_core(core):
        for layer in range(LAYERS):
            for part in range(3):
                for z in range(2):
                    place = part * 2 + z
                    values = row(ROW_QKV + layer * 3 + place % 3, place // 3)
                    for head in range(3):
                        lane = core * QKV + head * HEAD
                        qkv_ref[layer, 3 * z + head : 3 * z + head + 1, part * HEAD : (part + 1) * HEAD] = values[
                            :, lane : lane + HEAD
                        ]
            for z in range(2):
                for side in range(2):
                    lane = z * QUARTER + side * HALF
                    up_ref[layer, :, lane : lane + HALF] = row(ROW_UP + 4 * layer + 2 * core + side, z)

    for core in range(2):
        pl.when(at[CORE] == core)(functools.partial(by_core, core))
    for layer in range(LAYERS):
        for z in range(2):
            lanes = slice(z * HALF, (z + 1) * HALF)
            for index in range(2):
                gain_ref[layer, index : index + 1, lanes] = row(ROW_GAIN + 2 * layer + index, z)
                offset_ref[layer, index : index + 1, lanes] = row(ROW_OFFSET + 2 * layer + index, z)
            rest_ref[layer, :, lanes] = row(ROW_OUT + layer, z) + row(ROW_DOWN + layer, z)


def small_parameters(at, arrays):
    rows = run(gather_small_kernel, at, list(arrays), [shape((SMALL_ROWS, HALF), F32)], "small_rows", 0, 80000, limit=8)[0]
    other = lax.ppermute(rows, "zh", SWAP)
    outs = [
        shape((LAYERS, 2, D), F32),
        shape((LAYERS, 2, D), F32),
        shape((LAYERS, CORE_HEADS, QKV), F32),
        shape((LAYERS, 1, D), F32),
        shape((LAYERS, 1, CORE_FF), F32),
    ]
    return run(spread_small_kernel, at, [rows, other], outs, "small_spread", 0, 160000, limit=8)


SUM_ROWS = 18


def pack_sums_kernel(at, *refs):
    out_ref = refs[-1]
    out_ref[...] = jnp.zeros((64, HALF), F32)
    for layer in range(LAYERS):
        norm_ref, up_ref, qkv_ref = refs[3 * layer : 3 * layer + 3]
        start = layer * SUM_ROWS
        out_ref[start : start + 10] = norm_ref[...]
        out_ref[start + 10 : start + 14] = up_ref[...]
        for part in range(3):
            out_ref[start + 14 + part : start + 15 + part] = qkv_ref[0:1, part * HALF : (part + 1) * HALF]


def reduce_small(at, sums):
    rows = run(pack_sums_kernel, at, sums, [shape((64, HALF), F32)], "pack_sums", 0, 200000, limit=8)[0]
    parts = lax.all_to_all(rows.reshape(64, 1, HALF), EVERY, 0, 0, tiled=True)
    total = jnp.sum(parts, axis=0, keepdims=True)
    mine = lax.all_to_all(jnp.broadcast_to(total, (64, 1, HALF)), EVERY, 0, 0, tiled=True).reshape(64, HALF)
    return mine, lax.ppermute(mine, "core", SWAP)


def place_small(mine, theirs, core, zh):
    both = mine + theirs
    cores = jnp.stack([jnp.where(core == 0, mine, theirs), jnp.where(core == 0, theirs, mine)])
    gain, offset, hidden, up, qkv = [], [], [], [], []
    for layer in range(LAYERS):
        start = layer * SUM_ROWS

        def rows(first, count):
            pairs = both[start + first : start + first + 2 * count].reshape(count, 2, HALF)
            return lax.dynamic_index_in_dim(pairs, zh, 1, keepdims=False)

        gain.append(rows(0, 2))
        offset.append(rows(4, 2))
        hidden.append(rows(8, 1)[0])
        values = cores[:, start + 10 : start + 14].reshape(2, 2, QUARTER)
        up.append(lax.dynamic_index_in_dim(values, zh, 1, keepdims=False).reshape(FF // 2))
        values = cores[:, start + 14 : start + 17].reshape(2, 2, 3, 3, HEAD)
        values = values.transpose(3, 1, 0, 2, 4).reshape(2, 3 * D // 2)
        qkv.append(lax.dynamic_index_in_dim(values, zh, 0, keepdims=False))
    return tuple(jnp.stack(pieces) for pieces in (gain, offset, qkv, hidden, up))


EVERY = ("zh", "xh", "xl", "y", "zl")
ACROSS = ("xh", "xl", "y")
CHIPS = ("xl", "zl", "y")


def exchange(values):
    return lax.ppermute(values, "core", SWAP)


def scatter_sum(grads):
    parts = grads.reshape(64, -1, HALF)
    parts = lax.all_to_all(parts, EVERY, 0, 0, tiled=True)
    return jnp.sum(parts.astype(F32), axis=0).astype(BF16)


def gather_long(part, zl):
    other = lax.ppermute(part, "zl", SWAP)
    pair = jnp.concatenate([jnp.where(zl == 0, part, other), jnp.where(zl == 0, other, part)])
    return lax.all_gather(pair, ACROSS, axis=0, tiled=True)


def gather_short(part):
    copies = jnp.broadcast_to(part[None], (32,) + part.shape)
    return lax.all_to_all(copies, EVERY[1:], 0, 0, tiled=True).reshape(-1, HALF)


def token_places(offsets, lengths):
    ends = jnp.cumsum(lengths)
    before = ends[:, None] <= offsets[None, :]
    start = jnp.max(jnp.where(before, ends[:, None], 0), axis=0)
    return start, offsets >= ends[DOCS - 2]


def rotary(places):
    frequency = 1.0 / 10000.0 ** (jnp.arange(0, ROT, 2).astype(F32) / ROT)
    angles = frequency[:, None] * places.astype(F32)[None, :]
    return jnp.cos(angles), jnp.sin(angles)


def local(
    hidden_in,
    doc_lengths,
    norm_gain,
    norm_bias,
    qkv_weight,
    qkv_bias,
    out_weight,
    out_bias,
    up_weight,
    up_bias,
    down_weight,
    down_bias,
    cotangent,
):
    zh, core, xh, xl, zl, y = (lax.axis_index(name) for name in ("zh", "core", "xh", "xl", "zl", "y"))
    chip = (xl * 2 + zl) * 4 + y
    x = xh * 2 + xl
    spot = x * 4 + y
    lengths = doc_lengths[0]

    unit_seq = xl
    unit_half = jnp.where(unit_seq == 0, xh, 1 - xh)
    unit_swap = jnp.where(unit_seq == core, 0, TILE // 2)
    last_chip = jnp.where(unit_seq == 0, TILES - 1, 0)
    at = jnp.stack([core, zh, unit_seq, unit_swap, 1 - unit_half, last_chip]).astype(jnp.int32)

    gain, offset, b_qkv, b_rest, b_up = small_parameters(
        at, (norm_gain, norm_bias, qkv_bias, out_bias, up_bias, down_bias)
    )
    own_qkv = [turn_qkv(at, qkv_weight, layer) for layer in range(LAYERS)]
    other_qkv = [lax.ppermute(weights, "zh", SWAP) for weights in own_qkv]

    def chunk(layer):
        column = (y // 2) * CORE_FF + core * QUARTER + (y % 2) * HALF
        up = lax.dynamic_slice(up_weight, (layer, x * CHUNK_UP, column), (1, CHUNK_UP, HALF))[0]
        down = lax.dynamic_slice(
            down_weight, (layer, core * QUARTER + spot * CHUNK_DOWN, 0), (1, CHUNK_DOWN, D)
        )[0]
        row = core * QKV + jnp.minimum(spot, QKV // CHUNK_OUT - 1) * CHUNK_OUT
        out = lax.dynamic_slice(out_weight, (layer, row, 0), (1, CHUNK_OUT, D))[0]
        return jnp.concatenate([up, down[:, :HALF], down[:, HALF:], out[:, :HALF], out[:, HALF:]])

    rest = [
        lax.all_gather(lax.ppermute(chunk(layer), "zh", SWAP), ACROSS, axis=0, tiled=True).reshape(
            16, CHUNK, HALF
        )
        for layer in range(LAYERS)
    ]

    lane = jnp.arange(TILE, dtype=jnp.int32)
    seq0_tile = xh * TILES + chip
    places = []
    for seq, tile in ((0, seq0_tile), (1, 2 * TILES - 1 - seq0_tile)):
        offsets = tile * TILE + (lane ^ jnp.where(seq == core, 0, TILE // 2))
        places.append(offsets - token_places(offsets, lengths[seq])[0])
    own_tables = rotary(jnp.concatenate(places))
    unit_lengths = lax.dynamic_index_in_dim(lengths, unit_seq, 0, keepdims=False)
    relative = (jnp.arange(TILES, dtype=jnp.int32)[:, None] * TILE + (lane ^ unit_swap)[None, :]).reshape(-1)
    offsets = unit_half * UNIT + relative
    start, padding = token_places(offsets, unit_lengths)
    unit_tables = rotary(offsets - start)
    low = jnp.where(padding, offsets, jnp.maximum(start, offsets - (WINDOW - 1)))
    low = (low - unit_half * UNIT).reshape(1, UNIT)
    pos = relative.reshape(1, UNIT)

    def to_units(values):
        return lax.all_to_all(values.reshape(TILES, -1, TILE), CHIPS, 0, 0, tiled=True)

    def halo_of(got):
        last = lax.dynamic_index_in_dim(got, last_chip, 0, keepdims=False)
        return lax.ppermute(last[HEAD:], "xh", SWAP)

    def finish_attention(packed, edge, tail):
        edge = lax.ppermute(edge, "xh", SWAP)
        return to_units(add_edge(at, packed, tail, edge, *unit_tables))

    tokens = cotangent[0]
    dhid = [None, (tokens, exchange(tokens))]
    stream, added = hidden_in[0], None
    kept = []
    for layer in range(LAYERS):
        following, hat, inverse, act = norms(at, stream, added, gain[layer], offset[layer])
        stream = stream if following is None else following
        acts = (act, exchange(act))
        got = to_units(project_qkv(at, *acts, own_qkv[layer], other_qkv[layer], b_qkv[layer], *own_tables))
        gate, slope, total = feed_forward(at, *acts, b_up[layer], up_weight, down_weight, rest[layer], layer)
        halo = halo_of(got)
        if layer == LAYERS - 1:
            dctx = to_units(grad_ctx(at, *dhid[layer], out_weight, rest[layer], layer))
            ctx, *packed = attention(at, got, halo, low, pos, dctx, unit_tables)
            saved = None
        else:
            ctx, *saved = attention(at, got, halo, low, pos)
        ctx = to_units(ctx)
        keep, give = attention_out(at, ctx, out_weight, rest[layer], total, layer)
        added = (keep, exchange(give), b_rest[layer])
        kept.append((hat, inverse, acts, got, halo, gate, slope, ctx, saved))
    hidden_out = (stream.astype(F32) + (added[0] + added[1] + added[2])).astype(BF16)[None]

    dstream = tokens
    big, sums = [None] * LAYERS, [None] * LAYERS
    for layer in reversed(range(LAYERS)):
        hat, inverse, acts, got, halo, gate, slope, ctx, saved = kept[layer]
        if layer < LAYERS - 1:
            dhid[layer] = (low_stream, exchange(low_stream))
            dctx = to_units(grad_ctx(at, *dhid[layer], out_weight, rest[layer], layer))
        dup, keep, give, sum_up = mlp_back(
            at, *dhid[layer], slope, up_weight, down_weight, rest[layer], layer
        )
        second = (keep, exchange(give))
        part_m = scatter_sum(mlp_grads(at, *acts, *dhid[layer], gate, dup, ctx))
        if layer < LAYERS - 1:
            packed = attention(at, got, halo, low, pos, dctx, unit_tables, saved)
        dqkv = finish_attention(*packed)
        keep, give, sum_qkv = qkv_back(at, dqkv, own_qkv[layer], other_qkv[layer])
        first = (keep, exchange(give))
        part_q = scatter_sum(qkv_grads(at, dqkv, *acts))
        dstream, low_stream, sum_norm = norm_back(at, first, second, hat, inverse, gain[layer], dstream)
        sums[layer] = (sum_norm, sum_up, sum_qkv)
        mlp = gather_long(part_m, zl)
        qkv = gather_short(part_q)
        big[layer] = (mlp, exchange(mlp), qkv, exchange(qkv))
    hidden_grad = dstream[None]

    totals = reduce_small(at, [item for layer in range(LAYERS) for item in sums[layer]])
    g_gain, g_offset, g_bqkv, g_hidden, g_bup = place_small(*totals, core, zh)
    filled_mlp, filled_qkv = None, None
    for layer in reversed(range(LAYERS)):
        mlp, mlp_theirs, qkv, qkv_theirs = big[layer]
        filled_mlp = place_mlp(at, mlp, mlp_theirs, layer, filled_mlp)
        filled_qkv = place_qkv(at, qkv, qkv_theirs, layer, filled_qkv)
    g_up, g_down, g_out = filled_mlp
    return (
        hidden_out,
        hidden_grad,
        g_gain,
        g_offset,
        filled_qkv,
        g_bqkv,
        g_out,
        g_hidden,
        g_up,
        g_bup,
        g_down,
        g_hidden,
    )


def solution(mesh):
    fine = Mesh(
        mesh.devices.reshape(2, 2, 2, 4, 2, 2), ("xh", "xl", "zl", "y", "core", "zh")
    )
    ctx = ("xh", "xl", "zl", "y", "core")
    rows = P(None, "zh", None)
    tokens = P("zh", ctx, None)
    last = P(None, None, "zh")
    bias = P(None, "zh")
    return jax.shard_map(
        local,
        mesh=fine,
        in_specs=(tokens, P("zh", None, None), last, last, rows, bias, rows, bias, rows, bias, rows, bias, tokens),
        out_specs=(tokens, tokens, last, last, rows, bias, rows, bias, rows, bias, rows, bias),
        check_vma=False,
    )
```

```python
import functools

import jax
import jax.numpy as jnp
from jax import lax
from jax.experimental import pallas as pl
from jax.experimental.pallas import tpu as pltpu
from jax.sharding import Mesh
from jax.sharding import PartitionSpec as P

D = 768
HALF = D // 2
HEADS = 12
HEAD = 64
FF = 3072
ROT = 16
LAYERS = 2
WINDOW = 1024
DOCS = 8
TILE = 128
TILES = 16
UNIT = TILE * TILES
SLOTS = 8
CORE_HEADS = HEADS // 2
QKV = 3 * HEAD
QKV_ROWS = CORE_HEADS * QKV
CORE_FF = FF // 2
QUARTER = FF // 4

CHUNK_UP = 96
CHUNK_DOWN = 48
CHUNK = CHUNK_UP + 2 * CHUNK_DOWN
QKV_PART = QKV_ROWS // 4
OUT_PART = QKV // 2
PART_SECOND = 2 * HALF
PART_FIRST = 2 * HALF + OUT_PART + 32
PART_QKV = QKV_PART + OUT_PART
CHUNK_SECOND, CHUNK_FIRST, CHUNK_QKV = PART_SECOND // 4, PART_FIRST // 4, PART_QKV // 4
SENT_GATE, SENT_CTX = HALF, HALF + QUARTER
SENT_EARLY = SENT_CTX + QKV + HEAD
SENT_LATE = CORE_FF + D
QKV_FIRST = 32 * 40
SMALL = 12

BLOCKED = -1e30
EPSILON = 1e-05
SWAP = [(0, 1), (1, 0)]
F32 = jnp.float32
BF16 = jnp.bfloat16

NN = (((1,), (0,)), ((), ()))
NT = (((1,), (1,)), ((), ()))
TN = (((0,), (0,)), ((), ()))


def dot(left, right, dims=NN):
    return lax.dot_general(left, right, dims, preferred_element_type=F32)


def shape(dims, kind):
    return jax.ShapeDtypeStruct(dims, kind)


def block(dims, *at):
    place = at[0] if at else (lambda s: (0,) * len(dims))
    return pl.BlockSpec(dims, lambda i, s: place(s))


def whole(array):
    return block(array.shape)


LATEST = []


def run(
    kernel, scalars, inputs, outs, name, flops, moved, scratch=(), limit=40, aliases=None, exps=0, out_specs=None, after=(), token=False
):
    after = list(after) + LATEST
    arrays = [item[0] if isinstance(item, tuple) else item for item in inputs] + after
    specs = [item[1] if isinstance(item, tuple) else whole(item) for item in inputs]
    specs += [pl.BlockSpec(memory_space=pl.ANY)] * len(after)
    if out_specs is None:
        out_specs = [block(out.shape) for out in outs]
    count = len(inputs)

    def body(at, *refs):
        kernel(at, *refs[:count], *refs[count + len(after) :])

    results = pl.pallas_call(
        body,
        grid_spec=pltpu.PrefetchScalarGridSpec(
            num_scalar_prefetch=1,
            grid=(1,),
            in_specs=specs,
            out_specs=out_specs,
            scratch_shapes=list(scratch),
        ),
        out_shape=outs,
        input_output_aliases=aliases or {},
        compiler_params=pltpu.CompilerParams(vmem_limit_bytes=60 * 1024 * 1024),
        cost_estimate=pl.CostEstimate(flops=1, bytes_accessed=1, transcendentals=0),
        name=name,
    )(scalars, *arrays)
    LATEST[:] = [results[-1] if token else min(results, key=lambda result: result.size)]
    return results


def held(at, values, after=()):
    anywhere = pl.BlockSpec(memory_space=pl.ANY)

    def kernel(at, *refs):
        refs[-1][...] = jnp.zeros_like(refs[-1])

    outs = [shape(value.shape, value.dtype) for value in values] + [shape((8, 128), F32)]
    specs = [anywhere] * len(values) + [block((8, 128))]
    aliases = {1 + index: index for index in range(len(values))}
    inputs = [(value, anywhere) for value in values]
    return run(kernel, at, inputs, outs, "held", 0, 0, aliases=aliases, out_specs=specs, after=after, token=True)[:-1]


CORE, ZH, REVERSE, SWAPPED, FIRST_HALF, LAST_CHIP, RING_X, RING_Y, SPOT = range(9)


def half_at(index):
    return pl.ds(pl.multiple_of(index * HALF, HALF), HALF)


def turn(at, raw_ref, out_ref):
    def by_core(core):
        for part in range(3):
            for z in range(2):
                start = part * D + z * HALF + core * QKV
                piece = raw_ref[0, :, start : start + QKV].T
                for head in range(3):
                    row = (z * 3 + head) * QKV + part * HEAD
                    out_ref[row : row + HEAD, :] = piece[head * HEAD : (head + 1) * HEAD]

    for core in range(2):
        pl.when(at[CORE] == core)(functools.partial(by_core, core))


def put_chunk(up_ref, down_ref, out_ref):
    out_ref[0:CHUNK_UP] = up_ref[0]
    out_ref[CHUNK_UP : CHUNK_UP + CHUNK_DOWN] = down_ref[0, :, :HALF]
    out_ref[CHUNK_UP + CHUNK_DOWN :] = down_ref[0, :, HALF:]


SMALL_AT, CHUNK_AT = QKV_ROWS, QKV_ROWS + 32


def begin_kernel(at, qkv_ref, up_ref, down_ref, *refs):
    small, out_ref = refs[:-1], refs[-1]
    turn(at, qkv_ref, out_ref)
    out_ref[SMALL_AT:CHUNK_AT] = gather_small(small).astype(BF16)
    put_chunk(up_ref, down_ref, out_ref.at[CHUNK_AT:])


def begin(at, qkv_weight, up_weight, down_weight, small):
    return run(
        begin_kernel,
        at,
        [
            (qkv_weight, block((1, HALF, 3 * D), lambda s: (0, 0, 0))),
            *chunk_inputs(up_weight, down_weight, 0),
            *small,
        ],
        [shape((CHUNK_AT + CHUNK, HALF), BF16)],
        "begin",
        0,
        2700000,
    )[0]


def chunk_inputs(up_weight, down_weight, layer):
    column = lambda s: (s[RING_Y] // 2) * 4 + s[CORE] * 2 + s[RING_Y] % 2
    return [
        (up_weight, block((1, CHUNK_UP, HALF), lambda s: (layer, s[RING_X], column(s)))),
        (down_weight, block((1, CHUNK_DOWN, D), lambda s: (layer, s[CORE] * 16 + s[SPOT], 0))),
    ]


REST_CHUNK = LAYERS * HALF


def begin_rest_kernel(at, qkv_ref, up_ref, down_ref, out_ref, rows_ref, turned_ref):
    for layer in range(LAYERS):
        for side in range(2):
            row = layer * HALF + side * QKV
            rows_ref[row : row + QKV] = out_ref[layer, :, side * HALF : (side + 1) * HALF]
    put_chunk(up_ref, down_ref, rows_ref.at[REST_CHUNK:])
    turn(at, qkv_ref, turned_ref)


def begin_rest(at, qkv_weight, up_weight, down_weight, out_weight):
    return run(
        begin_rest_kernel,
        at,
        [
            (qkv_weight, block((1, HALF, 3 * D), lambda s: (1, 0, 0))),
            *chunk_inputs(up_weight, down_weight, 1),
            (out_weight, block((LAYERS, QKV, D), lambda s: (0, s[CORE], 0))),
        ],
        [shape((REST_CHUNK + CHUNK, HALF), BF16), shape((QKV_ROWS, HALF), BF16)],
        "begin_rest",
        0,
        1500000,
    )


def fill_up(z, up_ref, own0_ref, own1_ref, rest_ref):
    up_ref[half_at(z), 0:QUARTER] = own0_ref[0]
    up_ref[half_at(z), QUARTER:] = own1_ref[0]
    for chunk in range(16):
        x, y = chunk // 4, chunk % 4
        rows = pl.ds(pl.multiple_of((1 - z) * HALF + CHUNK_UP * x, 32), CHUNK_UP)
        up_ref[rows, y * HALF : (y + 1) * HALF] = rest_ref[chunk]


def fill_down(z, down_ref, own_ref, rest_ref):
    down_ref[pl.ds(pl.multiple_of(z * QUARTER, QUARTER), QUARTER), :] = own_ref[0]
    for chunk in range(16):
        rows = pl.ds(pl.multiple_of((1 - z) * QUARTER + CHUNK_DOWN * chunk, 16), CHUNK_DOWN)
        down_ref[rows, 0:HALF] = rest_ref[chunk, 0:CHUNK_DOWN]
        down_ref[rows, HALF:] = rest_ref[chunk, CHUNK_DOWN:]


def fill_out(z, out_ref, own_ref, other_ref):
    out_ref[pl.ds(pl.multiple_of(z * QKV, QKV), QKV), :] = own_ref[0]
    for side in range(2):
        rows = slice(side * QKV, (side + 1) * QKV)
        out_ref[pl.ds(pl.multiple_of((1 - z) * QKV, QKV), QKV), side * HALF : (side + 1) * HALF] = other_ref[rows, :]


def up_inputs(weights, rest, layer):
    own = [
        (weights, block((1, HALF, QUARTER), lambda s, z=z: (layer, 0, 2 * z + s[CORE]))) for z in range(2)
    ]
    return own + [(rest[layer], block((16, CHUNK_UP, HALF), lambda s: (0, 0, 0)))]


def down_inputs(weights, rest, layer):
    return [
        (weights, block((1, QUARTER, D), lambda s: (layer, s[CORE], 0))),
        (rest[layer], block((16, 2 * CHUNK_DOWN, HALF), lambda s: (0, 1, 0))),
    ]


def out_inputs(own, other, layer):
    return [
        (own, block((1, QKV, D), lambda s: (layer, s[CORE], 0))),
        (other, block((HALF, HALF), lambda s: (layer, 0))),
    ]


def norm_kernel(at, *refs, first):
    if first:
        stream_ref, gain_ref, offset_ref, hat_ref, inverse_ref, act_ref = refs
        stream = stream_ref[...].astype(F32)
    else:
        stream_ref, keep_ref, got_ref, bias_ref, gain_ref, offset_ref, next_ref, hat_ref, inverse_ref, act_ref = refs
        stream = stream_ref[...].astype(F32) + (keep_ref[...] + got_ref[...] + bias_ref[...])
        next_ref[...] = stream
    centered = stream - jnp.mean(stream, axis=-1, keepdims=True)
    inverse = lax.rsqrt(jnp.mean(centered * centered, axis=-1, keepdims=True) + EPSILON)
    hat = centered * inverse
    hat_ref[...] = hat
    inverse_ref[...] = inverse
    act_ref[:, 0:D] = (hat * gain_ref[0:1] + offset_ref[0:1]).astype(BF16)
    act_ref[:, D:] = (hat * gain_ref[1:2] + offset_ref[1:2]).astype(BF16)


def norms(at, stream, added, gain, offset):
    outs = [shape((TILE, D), F32), shape((TILE, 1), F32), shape((TILE, 2 * D), BF16)]
    if added is None:
        kernel = functools.partial(norm_kernel, first=True)
        return [None, *run(kernel, at, [stream, gain, offset], outs, "norms", 1000000, 1200000)]
    kernel = functools.partial(norm_kernel, first=False)
    outs = [shape((TILE, D), F32)] + outs
    return run(kernel, at, [stream, *added, gain, offset], outs, "norms", 1000000, 2400000)


def assemble(target_ref, mine, theirs):
    rows = TILE // 2
    target_ref[0:rows] = mine[:rows]
    target_ref[rows : 2 * rows] = theirs[:rows]
    target_ref[2 * rows : 3 * rows] = mine[rows:]
    target_ref[3 * rows :] = theirs[rows:]


def qkv_kernel(at, mine_ref, theirs_ref, own_ref, other_ref, bias_ref, cos_ref, sin_ref, *refs):
    along, (out_ref, tok_ref, act_t) = refs[:-3], refs[-3:]
    z = at[ZH]
    assemble(tok_ref, mine_ref[...], theirs_ref[...])
    act_t[...] = tok_ref[...].T
    cosine, sine = cos_ref[...], sin_ref[...]

    def rotated(part):
        low, high = part[:8], part[8:ROT]
        return jnp.concatenate(
            [low * cosine - high * sine, high * cosine + low * sine, part[ROT:]], axis=0
        )

    own_act, other_act = act_t[half_at(z), :], act_t[half_at(1 - z), :]
    for head in range(CORE_HEADS):
        rows = slice(head * QKV, (head + 1) * QKV)
        value = dot(own_ref[rows, :], own_act) + dot(other_ref[rows, :], other_act)
        bias = jnp.broadcast_to(bias_ref[head : head + 1, :], (8, QKV)).T
        value = value + bias[:, 0:1]
        query = (rotated(value[:HEAD]).astype(BF16).astype(F32) * 0.125).astype(BF16)
        key = rotated(value[HEAD : 2 * HEAD]).astype(BF16)
        val = value[2 * HEAD :].astype(BF16)
        for seq in range(2):
            lanes = slice(seq * TILE, (seq + 1) * TILE)
            out_ref[seq, head, 0:HEAD, :] = query[:, lanes]
            out_ref[seq, head, HEAD : 2 * HEAD, :] = key[:, lanes]
            out_ref[seq, head, 2 * HEAD : QKV, :] = val[:, lanes]
    for seq in range(2):
        out_ref[seq, CORE_HEADS:, 0:QKV, :] = jnp.zeros((SLOTS - CORE_HEADS, QKV, TILE), BF16)
        if along:
            out_ref[seq, :, QKV:, :] = along[0][seq * SLOTS : (seq + 1) * SLOTS]


def turned(weights):
    return weights, block((QKV_ROWS, HALF), lambda s: (0, 0))


def project_qkv(at, mine, theirs, own, other, bias, cosine, sine, along=None):
    left = block((TILE, D), lambda s: (0, 0))
    return run(
        qkv_kernel,
        at,
        [(mine, left), (theirs, left), turned(own), turned(other), bias, cosine, sine]
        + ([] if along is None else [along]),
        [shape((2, SLOTS, QKV if along is None else QKV + HEAD, TILE), BF16)],
        "qkv",
        4 * TILE * D * QKV_ROWS,
        3500000,
        [pltpu.VMEM((2 * TILE, D), BF16), pltpu.VMEM((D, 2 * TILE), BF16)],
        limit=24,
    )[0]


def mlp_kernel(
    at, mine_ref, theirs_ref, bias_ref, up0_ref, up1_ref, up_rest, down_own, down_rest, gate_ref, slope_ref, sum_ref, act, up, down
):
    z = at[ZH]
    act[0:TILE] = mine_ref[...]
    act[TILE:] = theirs_ref[...]
    fill_up(z, up, up0_ref, up1_ref, up_rest)
    fill_down(z, down, down_own, down_rest)
    total = jnp.zeros((2 * TILE, D), F32)
    for part in range(4):
        lanes = slice(part * HALF, (part + 1) * HALF)
        value = dot(act[...], up[:, lanes]) + bias_ref[:, lanes]
        normal = 0.5 * (1.0 + lax.erf(value * 0.7071067811865476))
        gate = (value * normal).astype(BF16)
        gate_ref[:, lanes] = gate
        slope_ref[:, lanes] = normal + value * (jnp.exp(-0.5 * value * value) * 0.3989422804014327)
        total = total + dot(gate, down[lanes, :])
    sum_ref[...] = total


def feed_forward(at, mine, theirs, bias, up, down, rest, layer, after=()):
    right = block((TILE, D), lambda s: (0, 1))
    tokens = 2 * TILE
    return run(
        mlp_kernel,
        at,
        [(mine, right), (theirs, right), bias, *up_inputs(up, rest, layer), *down_inputs(down, rest, layer)],
        [shape((tokens, CORE_FF), BF16), shape((tokens, CORE_FF), F32), shape((tokens, D), F32)],
        "mlp",
        4 * tokens * D * CORE_FF,
        8500000,
        [pltpu.VMEM((tokens, D), BF16), pltpu.VMEM((D, CORE_FF), BF16), pltpu.VMEM((CORE_FF, D), BF16)],
        limit=40,
        exps=2 * tokens * CORE_FF,
        after=after,
    )


def key_range(pair):
    first = max(-1, 2 * pair - WINDOW // TILE)
    return first, 2 * pair + 2


PAIRS_OF_TILES = sum(2 * (key_range(pair)[1] - key_range(pair)[0]) for pair in range(TILES // 2))


def allowed_mask(pair, first, last, low_row, pos_row, place):
    parts = []
    for tile in range(first, last):
        ok = place >= low_row - TILE * tile
        if tile >= 2 * pair:
            ok = ok & (place <= pos_row - TILE * tile)
        parts.append(ok)
    return jnp.concatenate(parts, axis=0)


def unturned(grads, cosine, sine):
    low, high = grads[:8], grads[8:ROT]
    return jnp.concatenate(
        [low * cosine + high * sine, high * cosine - low * sine, grads[ROT:]], axis=0
    ).astype(BF16)


def attention_kernel(at, *refs, forward, backward):
    refs = list(refs)
    take = lambda count: [refs.pop(0) for _ in range(count)]
    got_ref, halo_ref, low_ref, pos_ref = take(4)
    if backward:
        cos_ref, sin_ref = take(2)
        if not forward:
            dctx_ref, saved_ctx, saved_lse = take(3)
    if forward and not backward:
        out_ref, ctx_ref, lse_ref = take(3)
    if backward:
        packed_ref, edge_ref, tail_ref = take(3)
    key_tok, query_t = take(2)
    if forward:
        (val_t,) = take(1)
    if backward:
        val_tok, key_t, query_tok, dctx_t, dctx_tok, dkv = take(6)

    reverse = at[REVERSE]
    place = lax.broadcasted_iota(jnp.int32, (TILE, 2 * TILE), 0) ^ at[SWAPPED]

    def chip(tile):
        return jnp.where(reverse == 1, TILES - 1 - tile, tile)

    for tile in range(-1, TILES):
        here = slice(tile * TILE, (tile + 1) * TILE)
        after = slice((tile + 1) * TILE, (tile + 2) * TILE)
        if tile < 0:
            key, val = halo_ref[0:HEAD, :], halo_ref[HEAD:, :]
        else:
            source = chip(tile)
            query, key, val = (got_ref[source, part * HEAD : (part + 1) * HEAD, :] for part in range(3))
            query_t[:, here] = query
            if backward:
                query_tok[here, :] = query.T
                dctx = got_ref[source, QKV:, :] if forward else dctx_ref[source]
                dctx_t[:, here] = dctx
                dctx_tok[here, :] = dctx.T
        key_tok[after, :] = key.T
        if forward:
            val_t[:, after] = val
        if backward:
            key_t[:, after] = key
            val_tok[after, :] = val.T
    if backward:
        dkv[...] = jnp.zeros_like(dkv)
    for pair in range(TILES // 2):
        first, last = key_range(pair)
        rows = slice((first + 1) * TILE, (last + 1) * TILE)
        lanes = slice(pair * 2 * TILE, (pair + 1) * 2 * TILE)
        places = chip(2 * pair), chip(2 * pair + 1)
        scores = dot(key_tok[rows, :], query_t[:, lanes])
        ok = allowed_mask(pair, first, last, low_ref[:, lanes], pos_ref[:, lanes], place)
        scores = jnp.where(ok, scores, BLOCKED)
        if forward:
            peak = jnp.max(scores, axis=0, keepdims=True)
            probs = jnp.exp(scores - peak)
            total = jnp.sum(probs, axis=0, keepdims=True)
            inverse = 1.0 / total
            ctx = dot(val_t[:, rows], probs.astype(BF16)) * inverse
            low_ctx = ctx.astype(BF16)
            for index in range(2):
                lanes_here = slice(index * TILE, (index + 1) * TILE)
                if backward:
                    packed_ref[places[index], QKV:, :] = low_ctx[:, lanes_here]
                else:
                    out_ref[places[index]] = low_ctx[:, lanes_here]
            if backward:
                probs = probs * inverse
            else:
                ctx_ref[:, lanes] = ctx
                lse_ref[:, lanes] = peak + jnp.log(total)
        else:
            probs = jnp.exp(scores - saved_lse[:, lanes])
            ctx = saved_ctx[:, lanes]
        if backward:
            dctx = dctx_t[:, lanes]
            dprobs = dot(val_tok[rows, :], dctx)
            delta = jnp.sum(ctx * dctx.astype(F32), axis=0, keepdims=True)
            dscores = (probs * (dprobs - delta)).astype(BF16)
            dquery = dot(key_t[:, rows], dscores) * 0.125
            dquery = unturned(dquery, cos_ref[:, lanes], sin_ref[:, lanes])
            packed_ref[places[0], 0:HEAD, :] = dquery[:, :TILE]
            packed_ref[places[1], 0:HEAD, :] = dquery[:, TILE:]
            dkv[rows, 0:HEAD] += dot(dscores, query_tok[lanes, :])
            dkv[rows, HEAD:] += dot(probs.astype(BF16), dctx_tok[lanes, :])
    if backward:
        edge_ref[...] = dkv[0:TILE, :]
        tail_ref[...] = dkv[TILES * TILE :, :]
        for tile in range(TILES - 1):
            lanes = slice(tile * TILE, (tile + 1) * TILE)
            grads = dkv[(tile + 1) * TILE : (tile + 2) * TILE, :].T
            packed_ref[chip(tile), HEAD:QKV, :] = unturned(grads, cos_ref[:, lanes], sin_ref[:, lanes])
        packed_ref[chip(TILES - 1), HEAD:QKV, :] = jnp.zeros((2 * HEAD, TILE), BF16)


def attention(at, got, halo, low, pos, tables=None, dctx=None, saved=None):
    forward, backward = saved is None, tables is not None
    keys = UNIT + TILE
    inputs = [got, halo, low, pos]
    outs = []
    scratch = [pltpu.VMEM((keys, HEAD), BF16), pltpu.VMEM((HEAD, UNIT), BF16)]
    if forward:
        scratch.append(pltpu.VMEM((HEAD, keys), BF16))
        if not backward:
            outs += [shape((TILES, HEAD, TILE), BF16), shape((HEAD, UNIT), F32), shape((1, UNIT), F32)]
    if backward:
        inputs += list(tables)
        if saved is not None:
            inputs += [dctx, *saved]
        rows = QKV + HEAD if forward else QKV
        outs += [shape((TILES, rows, TILE), BF16), shape((TILE, 2 * HEAD), F32), shape((TILE, 2 * HEAD), F32)]
        scratch += [
            pltpu.VMEM((keys, HEAD), BF16),
            pltpu.VMEM((HEAD, keys), BF16),
            pltpu.VMEM((UNIT, HEAD), BF16),
            pltpu.VMEM((HEAD, UNIT), BF16),
            pltpu.VMEM((UNIT, HEAD), BF16),
            pltpu.VMEM((keys, 2 * HEAD), F32),
        ]
    products = (2 if forward else 1) + (4 if backward else 0)
    return run(
        functools.partial(attention_kernel, forward=forward, backward=backward),
        at,
        inputs,
        outs,
        "attention" + ("_forward" if forward else "") + ("_backward" if backward else ""),
        2 * products * PAIRS_OF_TILES * TILE * TILE * HEAD * 4,
        4000000,
        scratch,
        exps=PAIRS_OF_TILES * TILE * TILE,
    )


def edge_kernel(at, packed_ref, tail_ref, edge_ref, cos_ref, sin_ref, out_ref):
    grads = tail_ref[...] + jnp.where(at[FIRST_HALF] == 1, edge_ref[...], 0.0)
    out_ref[0, 0:HEAD, :] = packed_ref[0, 0:HEAD, :]
    out_ref[0, HEAD:QKV, :] = unturned(grads.T, cos_ref[...], sin_ref[...])
    if out_ref.shape[1] > QKV:
        out_ref[0, QKV:, :] = packed_ref[0, QKV:, :]


def add_edge(at, packed, tail, edge, cosine, sine):
    spec = block((1,) + packed.shape[1:], lambda s: (s[LAST_CHIP], 0, 0))
    last = block((8, TILE), lambda s: (0, TILES - 1))
    return run(
        edge_kernel,
        at,
        [(packed, spec), tail, edge, (cosine, last), (sine, last)],
        [shape(packed.shape, BF16)],
        "attention_edge",
        100000,
        300000,
        limit=8,
        aliases={1: 0},
        out_specs=[spec],
    )[0]


def out_kernel(at, got_ref, own_ref, other_ref, sum_ref, keep_ref, give_ref, weights):
    fill_out(at[ZH], weights, own_ref, other_ref)
    rows = TILE // 2
    for seq in range(2):
        ctx = got_ref[seq * SLOTS : seq * SLOTS + CORE_HEADS].reshape(HALF, TILE)
        value = dot(ctx, weights[...], TN)
        here = slice(seq * rows, (seq + 1) * rows)
        there = slice(TILE + seq * rows, TILE + (seq + 1) * rows)
        keep_ref[here, :] = value[:rows] + sum_ref[here, :]
        give_ref[here, :] = value[rows:] + sum_ref[there, :]


def ctx_of(got):
    return got, block((TILES, HEAD, TILE), lambda s: (0, got.shape[1] // HEAD - 1, 0))


def attention_out(at, got, outs, total, layer, after=()):
    return run(
        out_kernel,
        at,
        [ctx_of(got), *out_inputs(*outs, layer), total],
        [shape((TILE, D), F32), shape((TILE, D), F32)],
        "attention_out",
        4 * TILE * HALF * D,
        2700000,
        [pltpu.VMEM((HALF, D), BF16)],
        after=after,
    )


def dctx_kernel(at, mine_ref, theirs_ref, own_ref, other_ref, out_ref, weights, tok):
    fill_out(at[ZH], weights, own_ref, other_ref)
    assemble(tok, mine_ref[...], theirs_ref[...])
    value = dot(weights[...], tok[...], NT).astype(BF16)
    for seq in range(2):
        part = value[:, seq * TILE : (seq + 1) * TILE].reshape(CORE_HEADS, HEAD, TILE)
        start = seq * SLOTS
        out_ref[start : start + CORE_HEADS] = part
        out_ref[start + CORE_HEADS : start + SLOTS] = jnp.zeros((SLOTS - CORE_HEADS, HEAD, TILE), BF16)


def grad_ctx(at, mine, theirs, outs, layer):
    return run(
        dctx_kernel,
        at,
        [mine, theirs, *out_inputs(*outs, layer)],
        [shape((TILES, HEAD, TILE), BF16)],
        "grad_ctx",
        4 * TILE * HALF * D,
        1300000,
        [pltpu.VMEM((HALF, D), BF16), pltpu.VMEM((2 * TILE, D), BF16)],
    )[0]


def put_early(z, act_mine, act_theirs, gate_ref, sent_ref):
    sent_ref[0:TILE, 0:HALF] = act_mine[:, half_at(1 - z)]
    sent_ref[TILE:, 0:HALF] = act_theirs[:, half_at(1 - z)]
    lanes = pl.ds(pl.multiple_of((1 - z) * QUARTER, QUARTER), QUARTER)
    sent_ref[:, SENT_GATE:SENT_CTX] = gate_ref[:, lanes]


def mlp_back_kernel(at, *refs, early):
    refs = list(refs)
    take = lambda count: [refs.pop(0) for _ in range(count)]
    mine_ref, theirs_ref, slope_ref, up0_ref, up1_ref, up_rest, down_own, down_rest = take(8)
    if early:
        act_mine, act_theirs, gate_ref = take(3)
    dup_ref, keep_ref, give_ref, bias_ref, sent_ref, dhid, up, down = refs
    z = at[ZH]
    dhid[0:TILE] = mine_ref[...]
    dhid[TILE:] = theirs_ref[...]
    fill_up(z, up, up0_ref, up1_ref, up_rest)
    fill_down(z, down, down_own, down_rest)
    total = jnp.zeros((2 * TILE, D), F32)
    start = SENT_CTX if early else 0
    for part in range(4):
        lanes = slice(part * HALF, (part + 1) * HALF)
        value = dot(dhid[...], down[lanes, :], NT) * slope_ref[:, lanes]
        dup = value.astype(BF16)
        dup_ref[:, lanes] = dup
        sent_ref[:, start + part * HALF : start + (part + 1) * HALF] = dup
        bias_ref[part : part + 1, :] = jnp.sum(dup.astype(F32), axis=0, keepdims=True)
        total = total + dot(dup, up[:, lanes], NT)
    keep_ref[...] = total[:TILE]
    give_ref[...] = total[TILE:]
    sent_ref[:, start + CORE_FF :] = dhid[...]
    if early:
        put_early(z, act_mine, act_theirs, gate_ref, sent_ref)


def mlp_back(at, mine, theirs, slope, up, down, rest, layer, early=None):
    right = block((TILE, D), lambda s: (0, 1))
    tokens = 2 * TILE
    extra = [] if early is None else [(early[0], right), (early[1], right), early[2]]
    width = SENT_LATE + (0 if early is None else SENT_CTX)
    return run(
        functools.partial(mlp_back_kernel, early=early is not None),
        at,
        [mine, theirs, slope, *up_inputs(up, rest, layer), *down_inputs(down, rest, layer), *extra],
        [
            shape((tokens, CORE_FF), BF16),
            shape((TILE, D), F32),
            shape((TILE, D), F32),
            shape((4, HALF), F32),
            shape((tokens, width), BF16),
        ],
        "mlp_back",
        4 * tokens * D * CORE_FF,
        8500000,
        [pltpu.VMEM((tokens, D), BF16), pltpu.VMEM((D, CORE_FF), BF16), pltpu.VMEM((CORE_FF, D), BF16)],
    )


def early_kernel(at, act_mine, act_theirs, gate_ref, ctx_ref, sent_ref):
    z = at[ZH]
    put_early(z, act_mine, act_theirs, gate_ref, sent_ref)
    for seq in range(2):
        ctx = ctx_ref[pl.ds(seq * SLOTS + 3 * (1 - z), 3)].reshape(QKV, TILE)
        sent_ref[seq * TILE : (seq + 1) * TILE, SENT_CTX : SENT_CTX + QKV] = ctx.T
    sent_ref[:, SENT_CTX + QKV :] = jnp.zeros((2 * TILE, HEAD), BF16)


def pack_early(at, mine, theirs, gate, ctx):
    right = block((TILE, D), lambda s: (0, 1))
    outs = [shape((2 * TILE, SENT_EARLY), BF16)]
    return run(early_kernel, at, [(mine, right), (theirs, right), gate, ctx], outs, "pack_early", 0, 0)[0]


def put_out_grads(grads, ctx_ref, tok, z, offset, length):
    for side in range(2):
        lanes = slice(side * HALF, (side + 1) * HALF)
        value = jnp.zeros((QKV, HALF), F32)
        for seq in range(2):
            ctx = ctx_ref[seq * SLOTS + 3 * z : seq * SLOTS + 3 * z + 3].reshape(QKV, TILE)
            value = value + dot(ctx, tok[seq * TILE : (seq + 1) * TILE, lanes])
        value = value.astype(BF16)
        for index in range(2):
            start = (2 * side + index) * length + offset
            grads[start : start + OUT_PART, :] = value[index * OUT_PART : (index + 1) * OUT_PART]


def by_chunks(grads, out_ref, length):
    out_ref[...] = grads[...].reshape(16, length // 4, HALF)


def own_grads_kernel(at, act_mine, act_theirs, mine_ref, theirs_ref, gate_ref, dup_ref, *refs, with_ctx):
    refs = list(refs)
    if with_ctx:
        ctx_ref, early_ref, late_ref, out_ref, done_ref, act, dhid, grads, tok, tok_other = refs
        length, start = PART_FIRST, 0
    else:
        late_ref, out_ref, done_ref, act, dhid, grads = refs
        early_ref = late_ref
        length, start = PART_SECOND, SENT_CTX
    z = at[ZH]
    done_ref[...] = jnp.zeros_like(done_ref)
    act[0:TILE] = act_mine[:, half_at(z)]
    act[TILE:] = act_theirs[:, half_at(z)]
    dhid[0:TILE] = mine_ref[...]
    dhid[TILE:] = theirs_ref[...]
    act_t, act_other = act[...].T, early_ref[:, 0:HALF].T
    for part in range(4):
        lanes = slice(part * HALF, (part + 1) * HALF)
        other = slice(start + part * HALF, start + (part + 1) * HALF)
        value = dot(act_t, dup_ref[:, lanes]) + dot(act_other, late_ref[:, other])
        grads[part * length : part * length + HALF, :] = value.astype(BF16)
    start += CORE_FF
    gate_t = gate_ref[:, pl.ds(pl.multiple_of(z * QUARTER, QUARTER), QUARTER)].T
    gate_other = early_ref[:, SENT_GATE:SENT_CTX].T
    for side in range(2):
        lanes = slice(side * HALF, (side + 1) * HALF)
        other = slice(start + side * HALF, start + (side + 1) * HALF)
        value = (dot(gate_t, dhid[:, lanes]) + dot(gate_other, late_ref[:, other])).astype(BF16)
        for index in range(2):
            row = (2 * side + index) * length + HALF
            grads[row : row + HALF, :] = value[index * HALF : (index + 1) * HALF]
    if with_ctx:
        assemble(tok, mine_ref[...], theirs_ref[...])
        assemble(tok_other, late_ref[0:TILE, start:], late_ref[TILE:, start:])
        ctx_other = early_ref[:, SENT_CTX : SENT_CTX + QKV].T
        for side in range(2):
            lanes = slice(side * HALF, (side + 1) * HALF)
            value = dot(ctx_other, tok_other[:, lanes])
            for seq in range(2):
                ctx = ctx_ref[pl.ds(seq * SLOTS + 3 * z, 3)].reshape(QKV, TILE)
                value = value + dot(ctx, tok[seq * TILE : (seq + 1) * TILE, lanes])
            value = value.astype(BF16)
            for index in range(2):
                row = (2 * side + index) * length + 2 * HALF
                grads[row : row + OUT_PART, :] = value[index * OUT_PART : (index + 1) * OUT_PART]
                grads[row + OUT_PART : row + OUT_PART + 32, :] = jnp.zeros((32, HALF), BF16)
    by_chunks(grads, out_ref, length)


def own_grads(at, mine, theirs, dmine, dtheirs, gate, dup, late, early=None, ctx=None):
    right = block((TILE, D), lambda s: (0, 1))
    tokens = 2 * TILE
    length = PART_SECOND if ctx is None else PART_FIRST
    inputs = [(mine, right), (theirs, right), dmine, dtheirs, gate, dup]
    inputs += [late] if ctx is None else [ctx, early, late]
    scratch = [pltpu.VMEM((tokens, HALF), BF16), pltpu.VMEM((tokens, D), BF16), pltpu.VMEM((4 * length, HALF), BF16)]
    if ctx is not None:
        scratch += [pltpu.VMEM((tokens, D), BF16)] * 2
    return run(
        functools.partial(own_grads_kernel, with_ctx=ctx is not None),
        at,
        inputs,
        [shape((16, length // 4, HALF), BF16), shape((8, 128), F32)],
        "own_grads",
        4 * tokens * 4 * length * HALF,
        8000000,
        scratch,
        token=True,
    )[0]


def grads_qkv_kernel(
    at, got_ref, mine_ref, theirs_ref, dmine_ref, dtheirs_ref, ctx_ref, out_ref, done_ref, act, tok, grads
):
    done_ref[...] = jnp.zeros_like(done_ref)
    assemble(act, mine_ref[...], theirs_ref[...])
    assemble(tok, dmine_ref[...], dtheirs_ref[...])
    for z in range(2):
        put_out_grads(grads, ctx_ref, tok, z, QKV_PART, PART_QKV)
        lanes = slice(z * HALF, (z + 1) * HALF)
        value = jnp.zeros((QKV_ROWS, HALF), F32)
        for seq in range(2):
            rows = got_ref[seq * SLOTS : seq * SLOTS + CORE_HEADS, 0:QKV, :].reshape(QKV_ROWS, TILE)
            value = value + dot(rows, act[seq * TILE : (seq + 1) * TILE, lanes])
        value = value.astype(BF16)
        for part in range(4):
            start = part * PART_QKV
            grads[start : start + QKV_PART, :] = value[part * QKV_PART : (part + 1) * QKV_PART]
        out_ref[:, z] = grads[...].reshape(16, CHUNK_QKV, HALF)


def grads_qkv(at, got, mine, theirs, dmine, dtheirs):
    left = block((TILE, D), lambda s: (0, 0))
    return run(
        grads_qkv_kernel,
        at,
        [got, (mine, left), (theirs, left), dmine, dtheirs, ctx_of(got)],
        [shape((16, 2, CHUNK_QKV, HALF), BF16), shape((8, 128), F32)],
        "grads_qkv",
        4 * TILE * D * 4 * PART_QKV,
        3800000,
        [pltpu.VMEM((2 * TILE, D), BF16)] * 2 + [pltpu.VMEM((4 * PART_QKV, HALF), BF16)],
        token=True,
    )[0]


def spread_kernel(at, *refs):
    outs = refs[8:]
    rows = outs[0].shape[0] // 4
    for index, axis in ((0, RING_Y), (1, RING_X)):
        for step in range(4):
            place = (at[axis] + 4 - step) % 4
            outs[index][pl.ds(pl.multiple_of(place * rows, 32), rows), :] = refs[4 * index + step][...]


def spread(at, pieces, after):
    rows = pieces[0].shape[0]
    outs = [shape((4 * rows, HALF), BF16)] * 2
    return run(spread_kernel, at, pieces, outs, "ring_spread", 0, 32 * rows * HALF, after=after)


def collect_kernel(at, *refs):
    out_ref = refs[8]
    rows = refs[0].shape[0] // 4
    for step in range(4):
        x = (at[RING_X] + 4 - step) % 4
        for y in range(4):
            to = pl.ds(pl.multiple_of((x * 4 + y) * 2 * rows, 32), rows)
            out_ref[to, :] = refs[step][y * rows : (y + 1) * rows, :]
        y = (at[RING_Y] + 4 - step) % 4
        for x in range(4):
            to = pl.ds(pl.multiple_of((x * 4 + y) * 2 * rows + rows, 32), rows)
            out_ref[to, :] = refs[4 + step][x * rows : (x + 1) * rows, :]


def collect(at, pieces, after):
    rows = pieces[0].shape[0]
    outs = [shape((8 * rows, HALF), BF16)]
    return run(collect_kernel, at, pieces, outs, "ring_collect", 0, 32 * rows * HALF, after=after)[0]


def qkv_back_kernel(at, got_ref, own_ref, other_ref, keep_ref, give_ref, bias_ref):
    z = at[ZH]
    rows = TILE // 2
    sums = jnp.zeros((8, QKV_ROWS), F32)
    for seq in range(2):
        tok = got_ref[seq * SLOTS : seq * SLOTS + CORE_HEADS, 0:QKV, :].reshape(QKV_ROWS, TILE).T
        sums = sums + dot(jnp.ones((8, TILE), BF16), tok)
        here = slice(seq * rows, (seq + 1) * rows)
        for weights, at_z in ((own_ref, z), (other_ref, 1 - z)):
            value = dot(tok, weights[...])
            keep_ref[here, half_at(at_z)] = value[:rows]
            give_ref[here, half_at(at_z)] = value[rows:]
    bias_ref[...] = sums


def qkv_back(at, got, own, other):
    return run(
        qkv_back_kernel,
        at,
        [got, turned(own), turned(other)],
        [shape((TILE, D), F32), shape((TILE, D), F32), shape((8, QKV_ROWS), F32)],
        "qkv_back",
        4 * TILE * D * QKV_ROWS,
        3500000,
        limit=24,
    )


def qkv_rows(got_ref, tok, out_ref):
    for z in range(2):
        lanes = slice(z * HALF, (z + 1) * HALF)
        value = jnp.zeros((QKV_ROWS, HALF), F32)
        for seq in range(2):
            grads = got_ref[seq * SLOTS : seq * SLOTS + CORE_HEADS].reshape(QKV_ROWS, TILE)
            value = value + dot(grads, tok[seq * TILE : (seq + 1) * TILE, lanes])
        out_ref[z, 0:QKV_ROWS, :] = value.astype(BF16)


def qkv_grads_first_kernel(at, got_ref, mine_ref, theirs_ref, *refs):
    sums, (out_ref, tok, small) = refs[:6], refs[6:]
    assemble(tok, mine_ref[...], theirs_ref[...])
    qkv_rows(got_ref, tok, out_ref)

    def by_core(core):
        for z in range(2):
            small[...] = jnp.zeros((4 * SMALL, HALF), F32)
            for layer in range(LAYERS):
                norm_ref, up_ref, qkv_ref = sums[3 * layer : 3 * layer + 3]
                start = layer * SMALL
                for index in range(5):
                    small[start + index : start + index + 1] = norm_ref[2 * index + z : 2 * index + z + 1]
                for index in range(3):
                    part, half = (3 * z + index) // 2, (3 * z + index) % 2
                    for head in range(3):
                        lane = core * QKV + head * HEAD
                        source = (3 * half + head) * QKV + part * HEAD
                        small[start + 5 + index : start + 6 + index, lane : lane + HEAD] = qkv_ref[
                            0:1, source : source + HEAD
                        ]
                for side in range(2):
                    row = start + 8 + 2 * core + side
                    small[row : row + 1] = up_ref[2 * z + side : 2 * z + side + 1]
            out_ref[z, QKV_ROWS : QKV_ROWS + 4 * SMALL, :] = small[...].astype(BF16)
            used = QKV_ROWS + 4 * SMALL
            out_ref[z, used:, :] = jnp.zeros((QKV_FIRST - used, HALF), BF16)

    for core in range(2):
        pl.when(at[CORE] == core)(functools.partial(by_core, core))


def qkv_grads_first(at, got, mine, theirs, sums, after):
    left = block((TILE, D), lambda s: (0, 0))
    return run(
        qkv_grads_first_kernel,
        at,
        [got, (mine, left), (theirs, left), *sums],
        [shape((2, QKV_FIRST, HALF), BF16)],
        "qkv_grads_first",
        4 * TILE * D * QKV_ROWS,
        3300000,
        [pltpu.VMEM((2 * TILE, D), BF16), pltpu.VMEM((4 * SMALL, HALF), F32)],
        after=after,
    )[0]


def norm_back_kernel(
    at, keep0, got0, keep1, got1, hat_ref, inverse_ref, gain_ref, dstream_ref, next_ref, low_ref, sums_ref
):
    first, second = keep0[...] + got0[...], keep1[...] + got1[...]
    hat = hat_ref[...]
    dstream = dstream_ref[...].astype(F32)
    dhat = first * gain_ref[0:1] + second * gain_ref[1:2]
    grad = inverse_ref[...] * (
        dhat
        - jnp.mean(dhat, axis=-1, keepdims=True)
        - hat * jnp.mean(dhat * hat, axis=-1, keepdims=True)
    )
    total = dstream + grad
    next_ref[...] = total
    low_ref[...] = total.astype(BF16)
    rows = (first * hat, second * hat, first, second, dstream.astype(BF16).astype(F32))
    for index, value in enumerate(rows):
        row = jnp.sum(value, axis=0, keepdims=True)
        sums_ref[2 * index : 2 * index + 1, :] = row[:, :HALF]
        sums_ref[2 * index + 1 : 2 * index + 2, :] = row[:, HALF:]


def norm_back(at, first, second, hat, inverse, gain, dstream):
    return run(
        norm_back_kernel,
        at,
        [*first, *second, hat, inverse, gain, dstream],
        [shape((TILE, D), F32), shape((TILE, D), BF16), shape((10, HALF), F32)],
        "norm_back",
        2000000,
        3400000,
        limit=24,
    )


def rows_of(part, start, count, chunk, length, offset=0):
    at = start
    while at < start + count:
        step = min(chunk - at % chunk, start + count - at)
        yield (4 * part + at // chunk) * length + offset + at % chunk, at - start, step
        at += step


def place_mlp(source, core, up_ref, down_ref, chunk, length):
    for part in range(4):
        z, side = part // 2, part % 2
        column = z * CORE_FF + core * QUARTER + side * HALF
        for source_row, row, count in rows_of(part, 0, HALF, chunk, length):
            up_ref[0, row : row + count, column : column + HALF] = source[source_row : source_row + count, :].astype(F32)
        side, index = part // 2, part % 2
        lanes = slice(side * HALF, (side + 1) * HALF)
        first = core * QUARTER + index * HALF
        for source_row, row, count in rows_of(part, HALF, HALF, chunk, length):
            row += first
            down_ref[0, row : row + count, lanes] = source[source_row : source_row + count, :].astype(F32)


def for_cores(at, mine, theirs, put):
    for here, source in ((True, mine), (False, theirs)):
        for core in range(2):
            pl.when((at[CORE] == core) == here)(functools.partial(put, core, source))


UP_SHAPE, DOWN_SHAPE, OUT_SHAPE = (LAYERS, HALF, FF), (LAYERS, FF // 2, D), (LAYERS, HALF, D)
QKV_SHAPE = (LAYERS, HALF, 3 * D)
PLACED = (UP_SHAPE, DOWN_SHAPE, OUT_SHAPE)


def place_out(source, core, out_ref, first, chunk, length, offset):
    for part in range(4):
        lanes = slice((part // 2) * HALF, (part // 2 + 1) * HALF)
        start = core * QKV + (part % 2) * OUT_PART
        for source_row, row, count in rows_of(part, first, OUT_PART, chunk, length, offset):
            row += start
            out_ref[0, row : row + count, lanes] = source[source_row : source_row + count, :].astype(F32)


def place_turned(rows_ref, out_ref, part, z):
    column = part * D + z * HALF
    out_ref[0, :, column : column + HALF] = rows_ref[...].T


def place_second_kernel(at, mine_ref, theirs_ref, up_ref, down_ref, done_ref):
    done_ref[...] = jnp.zeros_like(done_ref)
    for_cores(
        at,
        mine_ref,
        theirs_ref,
        lambda core, source: place_mlp(source, core, up_ref, down_ref, CHUNK_SECOND, CHUNK_SECOND),
    )


def place_second(at, mine, theirs):
    outs = PLACED[:2]
    return run(
        place_second_kernel,
        at,
        [mine, theirs],
        [shape(dims, F32) for dims in outs] + [shape((8, 128), F32)],
        "place_second",
        0,
        14000000,
        out_specs=[block((1,) + dims[1:], lambda s: (1, 0, 0)) for dims in outs] + [block((8, 128))],
        token=True,
    )[:-1]


def place_first_kernel(
    at, mine_ref, theirs_ref, up_in, down_in, qkv_in, up_ref, down_ref, out_ref, qkv_ref, done_ref, rows_ref
):
    length = CHUNK_FIRST + CHUNK_QKV
    done_ref[...] = jnp.zeros_like(done_ref)

    def put(core, source):
        place_mlp(source, core, up_ref, down_ref, CHUNK_FIRST, length)
        place_out(source, core, out_ref.at[0:1], 2 * HALF, CHUNK_FIRST, length, 0)
        place_out(source, core, out_ref.at[1:2], QKV_PART, CHUNK_QKV, length, CHUNK_FIRST)

    for_cores(at, mine_ref, theirs_ref, put)
    for part in range(3):
        for z in range(2):

            def put_rows(core, source):
                for head in range(3):
                    row = (z * 3 + head) * QKV + part * HEAD
                    to = core * QKV + head * HEAD
                    for first in range(row, row + HEAD, 32):
                        pieces = rows_of(first // QKV_PART, first % QKV_PART, 32, CHUNK_QKV, length, CHUNK_FIRST)
                        for source_row, more, count in pieces:
                            here = to + first - row + more
                            rows_ref[here : here + count, :] = source[source_row : source_row + count, :].astype(F32)

            for_cores(at, mine_ref, theirs_ref, put_rows)
            place_turned(rows_ref, qkv_ref, part, z)


def place_first(at, mine, theirs, up, down, qkv):
    anywhere = pl.BlockSpec(memory_space=pl.ANY)
    return run(
        place_first_kernel,
        at,
        [mine, theirs, (up, anywhere), (down, anywhere), (qkv, anywhere)],
        [shape(dims, F32) for dims in (*PLACED, QKV_SHAPE)] + [shape((8, 128), F32)],
        "place_first",
        0,
        24000000,
        [pltpu.VMEM((HALF, HALF), F32)],
        aliases={3: 0, 4: 1, 5: 3},
        out_specs=[
            block((1,) + UP_SHAPE[1:], lambda s: (0, 0, 0)),
            block((1,) + DOWN_SHAPE[1:], lambda s: (0, 0, 0)),
            block(OUT_SHAPE),
            block((1,) + QKV_SHAPE[1:], lambda s: (1, 0, 0)),
            block((8, 128)),
        ],
        token=True,
    )[:-1]


def place_qkv_kernel(
    at, mine_ref, theirs_ref, out_ref, gain_ref, offset_ref, hidden_ref, again_ref, qkv_ref, up_ref, rows_ref
):
    for part in range(3):
        for z in range(2):

            def put(core, source):
                for head in range(3):
                    row = (z * 3 + head) * QKV + part * HEAD
                    to = core * QKV + head * HEAD
                    rows_ref[to : to + HEAD, :] = source[row : row + HEAD, :].astype(F32)

            for_cores(at, mine_ref, theirs_ref, put)
            place_turned(rows_ref, out_ref, part, z)
    rows = slice(QKV_ROWS, QKV_ROWS + 2 * SMALL + 8)
    small = mine_ref[rows, :].astype(F32) + theirs_ref[rows, :].astype(F32)
    for layer in range(LAYERS):
        start = layer * SMALL
        gain_ref[layer] = small[start : start + 2]
        offset_ref[layer] = small[start + 2 : start + 4]
        hidden_ref[layer : layer + 1] = small[start + 4 : start + 5]
        again_ref[layer : layer + 1] = small[start + 4 : start + 5]
        for index in range(3):
            lanes = slice(index * HALF, (index + 1) * HALF)
            qkv_ref[layer : layer + 1, lanes] = small[start + 5 + index : start + 6 + index]
        for index in range(4):
            lanes = slice(index * HALF, (index + 1) * HALF)
            up_ref[layer : layer + 1, lanes] = small[start + 8 + index : start + 9 + index]


def place_qkv(at, mine, theirs):
    outs = [shape((LAYERS, HALF, 3 * D), F32)]
    specs = [block((1, HALF, 3 * D), lambda s: (0, 0, 0))]
    for dims in ((2, HALF), (2, HALF), (HALF,), (HALF,), (3 * HALF,), (4 * HALF,)):
        outs.append(shape((LAYERS,) + dims, F32))
        specs.append(block((LAYERS,) + dims))
    return run(
        place_qkv_kernel,
        at,
        [mine, theirs],
        outs,
        "place_qkv",
        0,
        6000000,
        [pltpu.VMEM((HALF, HALF), F32)],
        limit=40,
        out_specs=specs,
    )


ROW_GAIN, ROW_OFFSET, ROW_QKV, ROW_OUT, ROW_UP, ROW_DOWN, SMALL_ROWS = 0, 4, 8, 14, 16, 24, 32


def gather_small(refs):
    gain, offset, qkv, out, up, down = (ref[...].astype(F32) for ref in refs)
    rows = [gain.reshape(4, HALF), offset.reshape(4, HALF)]
    rows += [qkv[layer : layer + 1, part * HALF : (part + 1) * HALF] for layer in range(LAYERS) for part in range(3)]
    rows.append(out)
    rows += [up[layer : layer + 1, part * HALF : (part + 1) * HALF] for layer in range(LAYERS) for part in range(4)]
    rows += [down, jnp.zeros((SMALL_ROWS - ROW_DOWN - LAYERS, HALF), F32)]
    return jnp.concatenate(rows, axis=0)


def spread_small_kernel(at, own_ref, other_ref, *outs):
    own, other = own_ref[...].astype(F32), other_ref[...].astype(F32)
    swap = at[ZH] == 1
    halves = jnp.where(swap, other, own), jnp.where(swap, own, other)

    def row(index, z):
        return halves[z][index : index + 1]

    def by_core(core):
        for layer in range(LAYERS):
            qkv_ref, up_ref = outs[5 * layer + 2], outs[5 * layer + 4]
            for part in range(3):
                for z in range(2):
                    place = part * 2 + z
                    values = row(ROW_QKV + layer * 3 + place % 3, place // 3)
                    for head in range(3):
                        lane = core * QKV + head * HEAD
                        qkv_ref[3 * z + head : 3 * z + head + 1, part * HEAD : (part + 1) * HEAD] = values[
                            :, lane : lane + HEAD
                        ]
            for z in range(2):
                for side in range(2):
                    lane = z * QUARTER + side * HALF
                    up_ref[:, lane : lane + HALF] = row(ROW_UP + 4 * layer + 2 * core + side, z)

    for core in range(2):
        pl.when(at[CORE] == core)(functools.partial(by_core, core))
    for layer in range(LAYERS):
        gain_ref, offset_ref, _, rest_ref, _ = outs[5 * layer : 5 * layer + 5]
        for z in range(2):
            lanes = slice(z * HALF, (z + 1) * HALF)
            for index in range(2):
                gain_ref[index : index + 1, lanes] = row(ROW_GAIN + 2 * layer + index, z)
                offset_ref[index : index + 1, lanes] = row(ROW_OFFSET + 2 * layer + index, z)
            rest_ref[:, lanes] = row(ROW_OUT + layer, z) + row(ROW_DOWN + layer, z)


def spread_small(at, rows, other):
    outs = [shape((2, D), F32), shape((2, D), F32), shape((8, QKV), F32), shape((1, D), F32), shape((1, CORE_FF), F32)]
    spec = block((SMALL_ROWS, HALF), lambda s: (QKV_ROWS // SMALL_ROWS, 0))
    values = run(spread_small_kernel, at, [(rows, spec), (other, spec)], outs * LAYERS, "small_spread", 0, 0)
    return zip(values[:5], values[5:])


EVERY = ("zh", "xh", "xl", "y", "zl")
ACROSS = ("xh", "xl", "y")
CHIPS = ("xl", "zl", "y")


def exchange(values):
    return lax.ppermute(values, "core", SWAP)


def scatter_sum(grads):
    parts = grads.reshape(64, -1, HALF)
    parts = lax.all_to_all(parts, EVERY, 0, 0, tiled=True)
    return jnp.sum(parts.astype(F32), axis=0).astype(BF16)


def add_from(part, other):
    return (part.astype(F32) + other.astype(F32)).astype(BF16)


def ring(values, axis, by):
    return lax.ppermute(values, axis, [(place, (place + by) % 4) for place in range(4)])


X_RING, Y_RING = ("xh", "xl"), "y"


def around(pieces, first, second):
    return [
        (ring(piece, first if index < 4 else second, index % 4) if index % 4 else piece)
        for index, piece in enumerate(pieces)
    ]


def sum_x(grads):
    return lax.psum_scatter(grads.reshape(-1, HALF), X_RING, scatter_dimension=0, tiled=True)


def sum_y(part):
    return lax.psum_scatter(part, Y_RING, scatter_dimension=0, tiled=True)


def sum_grid(grads):
    parts = lax.all_to_all(grads, ACROSS, 0, 0, tiled=True)
    return jnp.sum(parts.astype(F32), axis=0).astype(BF16)


def sum_near(part):
    return add_from(part, lax.ppermute(part, "zl", SWAP))


def sum_depth(zh, part):
    part = part.reshape(2, -1, HALF)
    keep = jnp.where(zh == 0, part[0], part[1])
    give = jnp.where(zh == 0, part[1], part[0])
    near = lax.ppermute(keep, "zl", SWAP)
    far = lax.ppermute(give, "zh", SWAP)
    across = lax.ppermute(give, ("zl", "zh"), [(0, 3), (3, 0), (1, 2), (2, 1)])
    total = (keep.astype(F32) + near.astype(F32)) + (far.astype(F32) + across.astype(F32))
    return total.astype(BF16)


def gather_half(at, total, after):
    rows = total.shape[0] // 2
    halves = total[:rows], total[rows:]
    return spread(at, around([halves[0]] * 4 + [halves[1]] * 4, Y_RING, X_RING), after)


def gather_rest(at, long, after):
    return collect(at, around([long[0]] * 4 + [long[1]] * 4, X_RING, Y_RING), after)


def gather_short(part):
    copies = jnp.broadcast_to(part[None], (32,) + part.shape)
    return lax.all_to_all(copies, EVERY[1:], 0, 0, tiled=True).reshape(-1, HALF)


def token_places(offsets, lengths):
    ends = jnp.cumsum(lengths)
    before = ends[:, None] <= offsets[None, :]
    start = jnp.max(jnp.where(before, ends[:, None], 0), axis=0)
    return start, offsets >= ends[DOCS - 2]


def rotary(places):
    frequency = 1.0 / 10000.0 ** (jnp.arange(0, ROT, 2).astype(F32) / ROT)
    angles = frequency[:, None] * places.astype(F32)[None, :]
    return jnp.cos(angles), jnp.sin(angles)


def local(
    hidden_in,
    doc_lengths,
    norm_gain,
    norm_bias,
    qkv_weight,
    qkv_bias,
    out_weight,
    out_bias,
    up_weight,
    up_bias,
    down_weight,
    down_bias,
    cotangent,
):
    LATEST.clear()
    zh, core, xh, xl, zl, y = (lax.axis_index(name) for name in ("zh", "core", "xh", "xl", "zl", "y"))
    chip = (xl * 2 + zl) * 4 + y
    x = xh * 2 + xl
    lengths = doc_lengths[0]

    unit_seq = xl
    unit_half = jnp.where(unit_seq == 0, xh, 1 - xh)
    unit_swap = jnp.where(unit_seq == core, 0, TILE // 2)
    last_chip = jnp.where(unit_seq == 0, TILES - 1, 0)
    at = jnp.stack(
        [core, zh, unit_seq, unit_swap, 1 - unit_half, last_chip, x, y, x * 4 + y]
    ).astype(jnp.int32)

    lane = jnp.arange(TILE, dtype=jnp.int32)
    seq0_tile = xh * TILES + chip
    places = []
    for seq, tile in ((0, seq0_tile), (1, 2 * TILES - 1 - seq0_tile)):
        offsets = tile * TILE + (lane ^ jnp.where(seq == core, 0, TILE // 2))
        places.append(offsets - token_places(offsets, lengths[seq])[0])
    own_tables = rotary(jnp.concatenate(places))
    unit_lengths = lax.dynamic_index_in_dim(lengths, unit_seq, 0, keepdims=False)
    relative = (jnp.arange(TILES, dtype=jnp.int32)[:, None] * TILE + (lane ^ unit_swap)[None, :]).reshape(-1)
    offsets = unit_half * UNIT + relative
    start, padding = token_places(offsets, unit_lengths)
    unit_tables = rotary(offsets - start)
    low = jnp.where(padding, offsets, jnp.maximum(start, offsets - (WINDOW - 1)))
    low = (low - unit_half * UNIT).reshape(1, UNIT)
    pos = relative.reshape(1, UNIT)

    def to_units(values):
        return lax.all_to_all(values.reshape(TILES, -1, TILE), CHIPS, 0, 0, tiled=True)

    def halo_of(got):
        last = lax.dynamic_index_in_dim(got, last_chip, 0, keepdims=False)
        return lax.ppermute(last[HEAD:QKV], "xh", SWAP)

    def finish_attention(packed, edge, tail):
        edge = lax.ppermute(edge, "xh", SWAP)
        return to_units(add_edge(at, packed, tail, edge, *unit_tables))

    small = (norm_gain, norm_bias, qkv_bias, out_bias, up_bias, down_bias)

    def gather_chunks(chunk):
        return lax.all_gather(chunk, ACROSS, axis=0, tiled=True).reshape(16, CHUNK, HALF)

    weights = begin(at, qkv_weight, up_weight, down_weight, small)
    own_qkv, other_qkv = [weights], [lax.ppermute(weights, "zh", SWAP)]
    rest = [gather_chunks(other_qkv[0][CHUNK_AT:])]
    tokens = cotangent[0]
    dhid1 = (tokens, exchange(tokens))
    gain, offset, b_qkv, b_rest, b_up = spread_small(at, weights, other_qkv[0])
    _, hat0, inverse0, act = norms(at, hidden_in[0], None, gain[0], offset[0])
    acts0 = (act, exchange(act))
    got0 = to_units(project_qkv(at, *acts0, own_qkv[0], other_qkv[0], b_qkv[0], *own_tables))
    rows, weights = begin_rest(at, qkv_weight, up_weight, down_weight, out_weight)
    rows, weights = held(at, [rows, weights], (got0,))
    rows = lax.ppermute(rows, "zh", SWAP)
    own_qkv.append(weights)
    other_qkv.append(lax.ppermute(weights, "zh", SWAP))
    outs = (out_weight, rows)
    halo0 = halo_of(got0)
    ctx0, *saved0 = attention(at, got0, halo0, low, pos)
    rest.append(gather_chunks(held(at, [rows[REST_CHUNK:]])[0]))
    ctx0 = to_units(ctx0)
    gate0, slope0, total = feed_forward(at, *acts0, b_up[0], up_weight, down_weight, rest, 0)
    dctx1 = grad_ctx(at, *dhid1, outs, 1)
    keep, give = attention_out(at, ctx0, outs, total, 0)
    added = (keep, exchange(give), b_rest[0])

    stream, hat1, inverse1, act = norms(at, hidden_in[0], added, gain[1], offset[1])
    acts1 = (act, exchange(act))
    got1 = to_units(project_qkv(at, *acts1, own_qkv[1], other_qkv[1], b_qkv[1], *own_tables, dctx1))
    gate1, slope1, total = feed_forward(at, *acts1, b_up[1], up_weight, down_weight, rest, 1)
    dup1, keep, give, sum_up1, sent = mlp_back(
        at, *dhid1, slope1, up_weight, down_weight, rest, 1, (*acts1, gate1)
    )
    second1 = (keep, exchange(give))
    late1 = lax.ppermute(held(at, [sent], (got1,))[0], "zh", SWAP)
    halo1 = halo_of(got1)
    packed = attention(at, got1, halo1, low, pos, unit_tables)
    dqkv1 = finish_attention(*packed)
    grads1 = own_grads(at, *acts1, *dhid1, gate1, dup1, late1)
    part1 = sum_x(held(at, [grads1], (dqkv1,))[0])
    keep, give, sum_qkv1 = qkv_back(at, dqkv1, own_qkv[1], other_qkv[1])
    first1 = (keep, exchange(give))
    early0 = lax.ppermute(pack_early(at, *acts0, gate0, ctx0), "zh", SWAP)
    dstream, low_stream, sum_norm1 = norm_back(at, first1, second1, hat1, inverse1, gain[1], tokens)

    dhid0 = (low_stream, exchange(low_stream))
    dctx0 = to_units(grad_ctx(at, *dhid0, outs, 0))
    dup0, keep, give, sum_up0, sent = mlp_back(at, *dhid0, slope0, up_weight, down_weight, rest, 0)
    second0 = (keep, exchange(give))
    gradsq = grads_qkv(at, dqkv1, *acts1, *dhid1)
    gradsq, sent, part1 = held(at, [gradsq, sent, part1], (dctx0, early0))
    late0 = lax.ppermute(sent, "zh", SWAP)
    part1 = sum_y(part1)
    partq = sum_x(gradsq)
    packed = attention(at, got0, halo0, low, pos, unit_tables, dctx0, saved0)
    dqkv0 = finish_attention(*packed)
    grads0 = own_grads(at, *acts0, *dhid0, gate0, dup0, late0, early0, ctx0)
    part0 = sum_grid(held(at, [grads0], (dqkv0,))[0])
    keep, give, sum_qkv0 = qkv_back(at, dqkv0, own_qkv[0], other_qkv[0])
    first0 = (keep, exchange(give))
    dstream, _, sum_norm0 = norm_back(at, first0, second0, hat0, inverse0, gain[0], dstream)
    hidden_grad = dstream[None]
    partq, part1 = held(at, [partq, part1])
    partq = sum_y(partq)

    sums = (sum_norm0, sum_up0, sum_qkv0, sum_norm1, sum_up1, sum_qkv1)
    part_qkv = scatter_sum(qkv_grads_first(at, dqkv0, *acts0, sums, (part0,)))
    keep, give = attention_out(at, dqkv1, outs, total, 1)
    partq, part1 = held(at, [partq, part1])
    long1 = lax.all_gather(sum_near(part1), ACROSS, axis=0, tiled=True)
    hidden_out = (stream + (keep + exchange(give) + b_rest[1])).astype(BF16)[None]
    total0 = jnp.concatenate([sum_near(part0), sum_depth(zh, partq)])
    half0 = gather_half(at, total0, (part_qkv,))
    long1 = held(at, [long1])[0]
    qkv0 = gather_short(part_qkv)
    g_up, g_down = place_second(at, long1, exchange(long1))
    long0 = gather_rest(at, half0, (qkv0,))
    g_qkv, g_gain, g_offset, g_hidden, g_again, g_bqkv, g_bup = place_qkv(at, qkv0, exchange(qkv0))
    g_up, g_down, g_out, g_qkv = place_first(at, long0, exchange(long0), g_up, g_down, g_qkv)
    return (
        hidden_out,
        hidden_grad,
        g_gain,
        g_offset,
        g_qkv,
        g_bqkv,
        g_out,
        g_hidden,
        g_up,
        g_bup,
        g_down,
        g_again,
    )


def solution(mesh):
    fine = Mesh(
        mesh.devices.reshape(2, 2, 2, 4, 2, 2), ("xh", "xl", "zl", "y", "core", "zh")
    )
    ctx = ("xh", "xl", "zl", "y", "core")
    rows = P(None, "zh", None)
    tokens = P("zh", ctx, None)
    last = P(None, None, "zh")
    bias = P(None, "zh")
    return jax.shard_map(
        local,
        mesh=fine,
        in_specs=(tokens, P("zh", None, None), last, last, rows, bias, rows, bias, rows, bias, rows, bias, tokens),
        out_specs=(tokens, tokens, last, last, rows, bias, rows, bias, rows, bias, rows, bias),
        check_vma=False,
    )
```

```python
import functools

import jax
import jax.numpy as jnp
from jax import lax
from jax.experimental import pallas as pl
from jax.experimental.pallas import tpu as pltpu
from jax.sharding import Mesh
from jax.sharding import PartitionSpec as P

D = 768
HALF = D // 2
HEADS = 12
HEAD = 64
FF = 3072
ROT = 16
LAYERS = 2
WINDOW = 1024
DOCS = 8
TILE = 128
TILES = 16
UNIT = TILE * TILES
SLOTS = 8
CORE_HEADS = HEADS // 2
QKV = 3 * HEAD
QKV_ROWS = CORE_HEADS * QKV
CORE_FF = FF // 2
QUARTER = FF // 4

CHUNK_UP = 96
CHUNK_DOWN = 48
CHUNK = CHUNK_UP + 2 * CHUNK_DOWN
QKV_PART = QKV_ROWS // 4
OUT_PART = QKV // 2
PART_SECOND = 2 * HALF
PART_FIRST = 2 * HALF + OUT_PART + 32
PART_QKV = QKV_PART + OUT_PART
CHUNK_SECOND, CHUNK_FIRST, CHUNK_QKV = PART_SECOND // 4, PART_FIRST // 4, PART_QKV // 4
SENT_GATE, SENT_CTX = HALF, HALF + QUARTER
SENT_EARLY = SENT_CTX + QKV + HEAD
SENT_LATE = CORE_FF + D
QKV_FIRST = 32 * 40
SMALL = 12

BLOCKED = -1e30
EPSILON = 1e-05
SWAP = [(0, 1), (1, 0)]
F32 = jnp.float32
BF16 = jnp.bfloat16

NN = (((1,), (0,)), ((), ()))
NT = (((1,), (1,)), ((), ()))
TN = (((0,), (0,)), ((), ()))


def dot(left, right, dims=NN):
    return lax.dot_general(left, right, dims, preferred_element_type=F32)


def shape(dims, kind):
    return jax.ShapeDtypeStruct(dims, kind)


def block(dims, *at):
    place = at[0] if at else (lambda s: (0,) * len(dims))
    return pl.BlockSpec(dims, lambda i, s: place(s))


def whole(array):
    return block(array.shape)


LATEST = []


def run(
    kernel, scalars, inputs, outs, name, flops, moved, scratch=(), limit=40, aliases=None, exps=0, out_specs=None, after=(), token=False
):
    after = list(after) + LATEST
    arrays = [item[0] if isinstance(item, tuple) else item for item in inputs] + after
    specs = [item[1] if isinstance(item, tuple) else whole(item) for item in inputs]
    specs += [pl.BlockSpec(memory_space=pl.ANY)] * len(after)
    if out_specs is None:
        out_specs = [block(out.shape) for out in outs]
    count = len(inputs)

    def body(at, *refs):
        kernel(at, *refs[:count], *refs[count + len(after) :])

    results = pl.pallas_call(
        body,
        grid_spec=pltpu.PrefetchScalarGridSpec(
            num_scalar_prefetch=1,
            grid=(1,),
            in_specs=specs,
            out_specs=out_specs,
            scratch_shapes=list(scratch),
        ),
        out_shape=outs,
        input_output_aliases=aliases or {},
        compiler_params=pltpu.CompilerParams(vmem_limit_bytes=60 * 1024 * 1024),
        cost_estimate=pl.CostEstimate(flops=1, bytes_accessed=1, transcendentals=0),
        name=name,
    )(scalars, *arrays)
    LATEST[:] = [results[-1] if token else min(results, key=lambda result: result.size)]
    return results


def held(at, values, after=()):
    anywhere = pl.BlockSpec(memory_space=pl.ANY)

    def kernel(at, *refs):
        refs[-1][...] = jnp.zeros_like(refs[-1])

    outs = [shape(value.shape, value.dtype) for value in values] + [shape((8, 128), F32)]
    specs = [anywhere] * len(values) + [block((8, 128))]
    aliases = {1 + index: index for index in range(len(values))}
    inputs = [(value, anywhere) for value in values]
    return run(kernel, at, inputs, outs, "held", 0, 0, aliases=aliases, out_specs=specs, after=after, token=True)[:-1]


CORE, ZH, REVERSE, SWAPPED, FIRST_HALF, LAST_CHIP, RING_X, RING_Y, SPOT = range(9)


def half_at(index):
    return pl.ds(pl.multiple_of(index * HALF, HALF), HALF)


def turn(at, raw_ref, out_ref):
    def by_core(core):
        for part in range(3):
            for z in range(2):
                start = part * D + z * HALF + core * QKV
                piece = raw_ref[0, :, start : start + QKV].T
                for head in range(3):
                    row = (z * 3 + head) * QKV + part * HEAD
                    out_ref[row : row + HEAD, :] = piece[head * HEAD : (head + 1) * HEAD]

    for core in range(2):
        pl.when(at[CORE] == core)(functools.partial(by_core, core))


def put_chunk(up_ref, down_ref, out_ref):
    out_ref[0:CHUNK_UP] = up_ref[0]
    out_ref[CHUNK_UP : CHUNK_UP + CHUNK_DOWN] = down_ref[0, :, :HALF]
    out_ref[CHUNK_UP + CHUNK_DOWN :] = down_ref[0, :, HALF:]


SMALL_AT, CHUNK_AT = QKV_ROWS, QKV_ROWS + 32


def begin_kernel(at, qkv_ref, up_ref, down_ref, *refs):
    small, out_ref = refs[:-1], refs[-1]
    turn(at, qkv_ref, out_ref)
    out_ref[SMALL_AT:CHUNK_AT] = gather_small(small).astype(BF16)
    put_chunk(up_ref, down_ref, out_ref.at[CHUNK_AT:])


def begin(at, qkv_weight, up_weight, down_weight, small):
    return run(
        begin_kernel,
        at,
        [
            (qkv_weight, block((1, HALF, 3 * D), lambda s: (0, 0, 0))),
            *chunk_inputs(up_weight, down_weight, 0),
            *small,
        ],
        [shape((CHUNK_AT + CHUNK, HALF), BF16)],
        "begin",
        0,
        2700000,
    )[0]


def chunk_inputs(up_weight, down_weight, layer):
    column = lambda s: (s[RING_Y] // 2) * 4 + s[CORE] * 2 + s[RING_Y] % 2
    return [
        (up_weight, block((1, CHUNK_UP, HALF), lambda s: (layer, s[RING_X], column(s)))),
        (down_weight, block((1, CHUNK_DOWN, D), lambda s: (layer, s[CORE] * 16 + s[SPOT], 0))),
    ]


REST_CHUNK = LAYERS * HALF


def begin_rest_kernel(at, qkv_ref, up_ref, down_ref, out_ref, rows_ref, turned_ref):
    for layer in range(LAYERS):
        for side in range(2):
            row = layer * HALF + side * QKV
            rows_ref[row : row + QKV] = out_ref[layer, :, side * HALF : (side + 1) * HALF]
    put_chunk(up_ref, down_ref, rows_ref.at[REST_CHUNK:])
    turn(at, qkv_ref, turned_ref)


def begin_rest(at, qkv_weight, up_weight, down_weight, out_weight):
    return run(
        begin_rest_kernel,
        at,
        [
            (qkv_weight, block((1, HALF, 3 * D), lambda s: (1, 0, 0))),
            *chunk_inputs(up_weight, down_weight, 1),
            (out_weight, block((LAYERS, QKV, D), lambda s: (0, s[CORE], 0))),
        ],
        [shape((REST_CHUNK + CHUNK, HALF), BF16), shape((QKV_ROWS, HALF), BF16)],
        "begin_rest",
        0,
        1500000,
    )


def fill_up(z, up_ref, own0_ref, own1_ref, rest_ref):
    up_ref[half_at(z), 0:QUARTER] = own0_ref[0]
    up_ref[half_at(z), QUARTER:] = own1_ref[0]
    for chunk in range(16):
        x, y = chunk // 4, chunk % 4
        rows = pl.ds(pl.multiple_of((1 - z) * HALF + CHUNK_UP * x, 32), CHUNK_UP)
        up_ref[rows, y * HALF : (y + 1) * HALF] = rest_ref[chunk]


def fill_down(z, down_ref, own_ref, rest_ref):
    down_ref[pl.ds(pl.multiple_of(z * QUARTER, QUARTER), QUARTER), :] = own_ref[0]
    for chunk in range(16):
        rows = pl.ds(pl.multiple_of((1 - z) * QUARTER + CHUNK_DOWN * chunk, 16), CHUNK_DOWN)
        down_ref[rows, 0:HALF] = rest_ref[chunk, 0:CHUNK_DOWN]
        down_ref[rows, HALF:] = rest_ref[chunk, CHUNK_DOWN:]


def fill_out(z, out_ref, own_ref, other_ref):
    out_ref[pl.ds(pl.multiple_of(z * QKV, QKV), QKV), :] = own_ref[0]
    for side in range(2):
        rows = slice(side * QKV, (side + 1) * QKV)
        out_ref[pl.ds(pl.multiple_of((1 - z) * QKV, QKV), QKV), side * HALF : (side + 1) * HALF] = other_ref[rows, :]


def up_inputs(weights, rest, layer):
    own = [
        (weights, block((1, HALF, QUARTER), lambda s, z=z: (layer, 0, 2 * z + s[CORE]))) for z in range(2)
    ]
    return own + [(rest[layer], block((16, CHUNK_UP, HALF), lambda s: (0, 0, 0)))]


def down_inputs(weights, rest, layer):
    return [
        (weights, block((1, QUARTER, D), lambda s: (layer, s[CORE], 0))),
        (rest[layer], block((16, 2 * CHUNK_DOWN, HALF), lambda s: (0, 1, 0))),
    ]


def out_inputs(own, other, layer):
    return [
        (own, block((1, QKV, D), lambda s: (layer, s[CORE], 0))),
        (other, block((HALF, HALF), lambda s: (layer, 0))),
    ]


def norm_kernel(at, *refs, first):
    if first:
        stream_ref, gain_ref, offset_ref, hat_ref, inverse_ref, act_ref = refs
        stream = stream_ref[...].astype(F32)
    else:
        stream_ref, keep_ref, got_ref, bias_ref, gain_ref, offset_ref, next_ref, hat_ref, inverse_ref, act_ref = refs
        stream = stream_ref[...].astype(F32) + (keep_ref[...] + got_ref[...] + bias_ref[...])
        next_ref[...] = stream
    centered = stream - jnp.mean(stream, axis=-1, keepdims=True)
    inverse = lax.rsqrt(jnp.mean(centered * centered, axis=-1, keepdims=True) + EPSILON)
    hat = centered * inverse
    hat_ref[...] = hat
    inverse_ref[...] = inverse
    act_ref[:, 0:D] = (hat * gain_ref[0:1] + offset_ref[0:1]).astype(BF16)
    act_ref[:, D:] = (hat * gain_ref[1:2] + offset_ref[1:2]).astype(BF16)


def norms(at, stream, added, gain, offset):
    outs = [shape((TILE, D), F32), shape((TILE, 1), F32), shape((TILE, 2 * D), BF16)]
    if added is None:
        kernel = functools.partial(norm_kernel, first=True)
        return [None, *run(kernel, at, [stream, gain, offset], outs, "norms", 1000000, 1200000)]
    kernel = functools.partial(norm_kernel, first=False)
    outs = [shape((TILE, D), F32)] + outs
    return run(kernel, at, [stream, *added, gain, offset], outs, "norms", 1000000, 2400000)


def assemble(target_ref, mine, theirs):
    rows = TILE // 2
    target_ref[0:rows] = mine[:rows]
    target_ref[rows : 2 * rows] = theirs[:rows]
    target_ref[2 * rows : 3 * rows] = mine[rows:]
    target_ref[3 * rows :] = theirs[rows:]


def qkv_kernel(at, mine_ref, theirs_ref, own_ref, other_ref, bias_ref, cos_ref, sin_ref, *refs):
    along, (out_ref, tok_ref, act_t) = refs[:-3], refs[-3:]
    z = at[ZH]
    assemble(tok_ref, mine_ref[...], theirs_ref[...])
    act_t[...] = tok_ref[...].T
    cosine, sine = cos_ref[...], sin_ref[...]

    def rotated(part):
        low, high = part[:8], part[8:ROT]
        return jnp.concatenate(
            [low * cosine - high * sine, high * cosine + low * sine, part[ROT:]], axis=0
        )

    own_act, other_act = act_t[half_at(z), :], act_t[half_at(1 - z), :]
    for head in range(CORE_HEADS):
        rows = slice(head * QKV, (head + 1) * QKV)
        value = dot(own_ref[rows, :], own_act) + dot(other_ref[rows, :], other_act)
        bias = jnp.broadcast_to(bias_ref[head : head + 1, :], (8, QKV)).T
        value = value + bias[:, 0:1]
        query = (rotated(value[:HEAD]).astype(BF16).astype(F32) * 0.125).astype(BF16)
        key = rotated(value[HEAD : 2 * HEAD]).astype(BF16)
        val = value[2 * HEAD :].astype(BF16)
        for seq in range(2):
            lanes = slice(seq * TILE, (seq + 1) * TILE)
            out_ref[seq, head, 0:HEAD, :] = query[:, lanes]
            out_ref[seq, head, HEAD : 2 * HEAD, :] = key[:, lanes]
            out_ref[seq, head, 2 * HEAD : QKV, :] = val[:, lanes]
    for seq in range(2):
        out_ref[seq, CORE_HEADS:, 0:QKV, :] = jnp.zeros((SLOTS - CORE_HEADS, QKV, TILE), BF16)
        if along:
            out_ref[seq, :, QKV:, :] = along[0][seq * SLOTS : (seq + 1) * SLOTS]


def turned(weights):
    return weights, block((QKV_ROWS, HALF), lambda s: (0, 0))


def project_qkv(at, mine, theirs, own, other, bias, cosine, sine, along=None):
    left = block((TILE, D), lambda s: (0, 0))
    return run(
        qkv_kernel,
        at,
        [(mine, left), (theirs, left), turned(own), turned(other), bias, cosine, sine]
        + ([] if along is None else [along]),
        [shape((2, SLOTS, QKV if along is None else QKV + HEAD, TILE), BF16)],
        "qkv",
        4 * TILE * D * QKV_ROWS,
        3500000,
        [pltpu.VMEM((2 * TILE, D), BF16), pltpu.VMEM((D, 2 * TILE), BF16)],
        limit=24,
    )[0]


def mlp_kernel(
    at, mine_ref, theirs_ref, bias_ref, up0_ref, up1_ref, up_rest, down_own, down_rest, gate_ref, slope_ref, sum_ref, act, up, down
):
    z = at[ZH]
    act[0:TILE] = mine_ref[...]
    act[TILE:] = theirs_ref[...]
    fill_up(z, up, up0_ref, up1_ref, up_rest)
    fill_down(z, down, down_own, down_rest)
    total = jnp.zeros((2 * TILE, D), F32)
    for part in range(4):
        lanes = slice(part * HALF, (part + 1) * HALF)
        value = dot(act[...], up[:, lanes]) + bias_ref[:, lanes]
        normal = 0.5 * (1.0 + lax.erf(value * 0.7071067811865476))
        gate = (value * normal).astype(BF16)
        gate_ref[:, lanes] = gate
        slope_ref[:, lanes] = normal + value * (jnp.exp(-0.5 * value * value) * 0.3989422804014327)
        total = total + dot(gate, down[lanes, :])
    sum_ref[...] = total


def feed_forward(at, mine, theirs, bias, up, down, rest, layer, after=()):
    right = block((TILE, D), lambda s: (0, 1))
    tokens = 2 * TILE
    return run(
        mlp_kernel,
        at,
        [(mine, right), (theirs, right), bias, *up_inputs(up, rest, layer), *down_inputs(down, rest, layer)],
        [shape((tokens, CORE_FF), BF16), shape((tokens, CORE_FF), F32), shape((tokens, D), F32)],
        "mlp",
        4 * tokens * D * CORE_FF,
        8500000,
        [pltpu.VMEM((tokens, D), BF16), pltpu.VMEM((D, CORE_FF), BF16), pltpu.VMEM((CORE_FF, D), BF16)],
        limit=40,
        exps=2 * tokens * CORE_FF,
        after=after,
    )


def key_range(pair):
    first = max(-1, 2 * pair - WINDOW // TILE)
    return first, 2 * pair + 2


PAIRS_OF_TILES = sum(2 * (key_range(pair)[1] - key_range(pair)[0]) for pair in range(TILES // 2))


def allowed_mask(pair, first, last, low_row, pos_row, place):
    parts = []
    for tile in range(first, last):
        ok = place >= low_row - TILE * tile
        if tile >= 2 * pair:
            ok = ok & (place <= pos_row - TILE * tile)
        parts.append(ok)
    return jnp.concatenate(parts, axis=0)


def unturned(grads, cosine, sine):
    low, high = grads[:8], grads[8:ROT]
    return jnp.concatenate(
        [low * cosine + high * sine, high * cosine - low * sine, grads[ROT:]], axis=0
    ).astype(BF16)


def attention_kernel(at, *refs, forward, backward):
    refs = list(refs)
    take = lambda count: [refs.pop(0) for _ in range(count)]
    got_ref, halo_ref, low_ref, pos_ref = take(4)
    if backward:
        cos_ref, sin_ref = take(2)
        if not forward:
            dctx_ref, saved_ctx, saved_lse = take(3)
    if forward and not backward:
        out_ref, ctx_ref, lse_ref = take(3)
    if backward:
        packed_ref, edge_ref, tail_ref = take(3)
    key_tok, query_t = take(2)
    if forward:
        (val_t,) = take(1)
    if backward:
        val_tok, key_t, query_tok, dctx_t, dctx_tok, dkv = take(6)

    reverse = at[REVERSE]
    place = lax.broadcasted_iota(jnp.int32, (TILE, 2 * TILE), 0) ^ at[SWAPPED]

    def chip(tile):
        return jnp.where(reverse == 1, TILES - 1 - tile, tile)

    for tile in range(-1, TILES):
        here = slice(tile * TILE, (tile + 1) * TILE)
        after = slice((tile + 1) * TILE, (tile + 2) * TILE)
        if tile < 0:
            key, val = halo_ref[0:HEAD, :], halo_ref[HEAD:, :]
        else:
            source = chip(tile)
            query, key, val = (got_ref[source, part * HEAD : (part + 1) * HEAD, :] for part in range(3))
            query_t[:, here] = query
            if backward:
                query_tok[here, :] = query.T
                dctx = got_ref[source, QKV:, :] if forward else dctx_ref[source]
                dctx_t[:, here] = dctx
                dctx_tok[here, :] = dctx.T
        key_tok[after, :] = key.T
        if forward:
            val_t[:, after] = val
        if backward:
            key_t[:, after] = key
            val_tok[after, :] = val.T
    if backward:
        dkv[...] = jnp.zeros_like(dkv)
    for pair in range(TILES // 2):
        first, last = key_range(pair)
        rows = slice((first + 1) * TILE, (last + 1) * TILE)
        lanes = slice(pair * 2 * TILE, (pair + 1) * 2 * TILE)
        places = chip(2 * pair), chip(2 * pair + 1)
        scores = dot(key_tok[rows, :], query_t[:, lanes])
        ok = allowed_mask(pair, first, last, low_ref[:, lanes], pos_ref[:, lanes], place)
        scores = jnp.where(ok, scores, BLOCKED)
        if forward:
            peak = jnp.max(scores, axis=0, keepdims=True)
            probs = jnp.exp(scores - peak)
            total = jnp.sum(probs, axis=0, keepdims=True)
            inverse = 1.0 / total
            ctx = dot(val_t[:, rows], probs.astype(BF16)) * inverse
            low_ctx = ctx.astype(BF16)
            for index in range(2):
                lanes_here = slice(index * TILE, (index + 1) * TILE)
                if backward:
                    packed_ref[places[index], QKV:, :] = low_ctx[:, lanes_here]
                else:
                    out_ref[places[index]] = low_ctx[:, lanes_here]
            if backward:
                probs = probs * inverse
            else:
                ctx_ref[:, lanes] = ctx
                lse_ref[:, lanes] = peak + jnp.log(total)
        else:
            probs = jnp.exp(scores - saved_lse[:, lanes])
            ctx = saved_ctx[:, lanes]
        if backward:
            dctx = dctx_t[:, lanes]
            dprobs = dot(val_tok[rows, :], dctx)
            delta = jnp.sum(ctx * dctx.astype(F32), axis=0, keepdims=True)
            dscores = (probs * (dprobs - delta)).astype(BF16)
            dquery = dot(key_t[:, rows], dscores) * 0.125
            dquery = unturned(dquery, cos_ref[:, lanes], sin_ref[:, lanes])
            packed_ref[places[0], 0:HEAD, :] = dquery[:, :TILE]
            packed_ref[places[1], 0:HEAD, :] = dquery[:, TILE:]
            dkv[rows, 0:HEAD] += dot(dscores, query_tok[lanes, :])
            dkv[rows, HEAD:] += dot(probs.astype(BF16), dctx_tok[lanes, :])
    if backward:
        edge_ref[...] = dkv[0:TILE, :]
        tail_ref[...] = dkv[TILES * TILE :, :]
        for tile in range(TILES - 1):
            lanes = slice(tile * TILE, (tile + 1) * TILE)
            grads = dkv[(tile + 1) * TILE : (tile + 2) * TILE, :].T
            packed_ref[chip(tile), HEAD:QKV, :] = unturned(grads, cos_ref[:, lanes], sin_ref[:, lanes])
        packed_ref[chip(TILES - 1), HEAD:QKV, :] = jnp.zeros((2 * HEAD, TILE), BF16)


def attention(at, got, halo, low, pos, tables=None, dctx=None, saved=None):
    forward, backward = saved is None, tables is not None
    keys = UNIT + TILE
    inputs = [got, halo, low, pos]
    outs = []
    scratch = [pltpu.VMEM((keys, HEAD), BF16), pltpu.VMEM((HEAD, UNIT), BF16)]
    if forward:
        scratch.append(pltpu.VMEM((HEAD, keys), BF16))
        if not backward:
            outs += [shape((TILES, HEAD, TILE), BF16), shape((HEAD, UNIT), F32), shape((1, UNIT), F32)]
    if backward:
        inputs += list(tables)
        if saved is not None:
            inputs += [dctx, *saved]
        rows = QKV + HEAD if forward else QKV
        outs += [shape((TILES, rows, TILE), BF16), shape((TILE, 2 * HEAD), F32), shape((TILE, 2 * HEAD), F32)]
        scratch += [
            pltpu.VMEM((keys, HEAD), BF16),
            pltpu.VMEM((HEAD, keys), BF16),
            pltpu.VMEM((UNIT, HEAD), BF16),
            pltpu.VMEM((HEAD, UNIT), BF16),
            pltpu.VMEM((UNIT, HEAD), BF16),
            pltpu.VMEM((keys, 2 * HEAD), F32),
        ]
    products = (2 if forward else 1) + (4 if backward else 0)
    return run(
        functools.partial(attention_kernel, forward=forward, backward=backward),
        at,
        inputs,
        outs,
        "attention" + ("_forward" if forward else "") + ("_backward" if backward else ""),
        2 * products * PAIRS_OF_TILES * TILE * TILE * HEAD * 4,
        4000000,
        scratch,
        exps=PAIRS_OF_TILES * TILE * TILE,
    )


def edge_kernel(at, packed_ref, tail_ref, edge_ref, cos_ref, sin_ref, out_ref):
    grads = tail_ref[...] + jnp.where(at[FIRST_HALF] == 1, edge_ref[...], 0.0)
    out_ref[0, 0:HEAD, :] = packed_ref[0, 0:HEAD, :]
    out_ref[0, HEAD:QKV, :] = unturned(grads.T, cos_ref[...], sin_ref[...])
    if out_ref.shape[1] > QKV:
        out_ref[0, QKV:, :] = packed_ref[0, QKV:, :]


def add_edge(at, packed, tail, edge, cosine, sine):
    spec = block((1,) + packed.shape[1:], lambda s: (s[LAST_CHIP], 0, 0))
    last = block((8, TILE), lambda s: (0, TILES - 1))
    return run(
        edge_kernel,
        at,
        [(packed, spec), tail, edge, (cosine, last), (sine, last)],
        [shape(packed.shape, BF16)],
        "attention_edge",
        100000,
        300000,
        limit=8,
        aliases={1: 0},
        out_specs=[spec],
    )[0]


def out_kernel(at, got_ref, own_ref, other_ref, sum_ref, keep_ref, give_ref, weights):
    fill_out(at[ZH], weights, own_ref, other_ref)
    rows = TILE // 2
    for seq in range(2):
        ctx = got_ref[seq * SLOTS : seq * SLOTS + CORE_HEADS].reshape(HALF, TILE)
        value = dot(ctx, weights[...], TN)
        here = slice(seq * rows, (seq + 1) * rows)
        there = slice(TILE + seq * rows, TILE + (seq + 1) * rows)
        keep_ref[here, :] = value[:rows] + sum_ref[here, :]
        give_ref[here, :] = value[rows:] + sum_ref[there, :]


def ctx_of(got):
    return got, block((TILES, HEAD, TILE), lambda s: (0, got.shape[1] // HEAD - 1, 0))


def attention_out(at, got, outs, total, layer, after=()):
    return run(
        out_kernel,
        at,
        [ctx_of(got), *out_inputs(*outs, layer), total],
        [shape((TILE, D), F32), shape((TILE, D), F32)],
        "attention_out",
        4 * TILE * HALF * D,
        2700000,
        [pltpu.VMEM((HALF, D), BF16)],
        after=after,
    )


def dctx_kernel(at, mine_ref, theirs_ref, own_ref, other_ref, out_ref, weights, tok):
    fill_out(at[ZH], weights, own_ref, other_ref)
    assemble(tok, mine_ref[...], theirs_ref[...])
    value = dot(weights[...], tok[...], NT).astype(BF16)
    for seq in range(2):
        part = value[:, seq * TILE : (seq + 1) * TILE].reshape(CORE_HEADS, HEAD, TILE)
        start = seq * SLOTS
        out_ref[start : start + CORE_HEADS] = part
        out_ref[start + CORE_HEADS : start + SLOTS] = jnp.zeros((SLOTS - CORE_HEADS, HEAD, TILE), BF16)


def grad_ctx(at, mine, theirs, outs, layer):
    return run(
        dctx_kernel,
        at,
        [mine, theirs, *out_inputs(*outs, layer)],
        [shape((TILES, HEAD, TILE), BF16)],
        "grad_ctx",
        4 * TILE * HALF * D,
        1300000,
        [pltpu.VMEM((HALF, D), BF16), pltpu.VMEM((2 * TILE, D), BF16)],
    )[0]


def put_early(z, act_mine, act_theirs, gate_ref, sent_ref):
    sent_ref[0:TILE, 0:HALF] = act_mine[:, half_at(1 - z)]
    sent_ref[TILE:, 0:HALF] = act_theirs[:, half_at(1 - z)]
    lanes = pl.ds(pl.multiple_of((1 - z) * QUARTER, QUARTER), QUARTER)
    sent_ref[:, SENT_GATE:SENT_CTX] = gate_ref[:, lanes]


def mlp_back_kernel(at, *refs, early):
    refs = list(refs)
    take = lambda count: [refs.pop(0) for _ in range(count)]
    mine_ref, theirs_ref, slope_ref, up0_ref, up1_ref, up_rest, down_own, down_rest = take(8)
    if early:
        act_mine, act_theirs, gate_ref = take(3)
    dup_ref, keep_ref, give_ref, bias_ref, sent_ref, dhid, up, down = refs
    z = at[ZH]
    dhid[0:TILE] = mine_ref[...]
    dhid[TILE:] = theirs_ref[...]
    fill_up(z, up, up0_ref, up1_ref, up_rest)
    fill_down(z, down, down_own, down_rest)
    total = jnp.zeros((2 * TILE, D), F32)
    start = SENT_CTX if early else 0
    for part in range(4):
        lanes = slice(part * HALF, (part + 1) * HALF)
        value = dot(dhid[...], down[lanes, :], NT) * slope_ref[:, lanes]
        dup = value.astype(BF16)
        dup_ref[:, lanes] = dup
        sent_ref[:, start + part * HALF : start + (part + 1) * HALF] = dup
        bias_ref[part : part + 1, :] = jnp.sum(dup.astype(F32), axis=0, keepdims=True)
        total = total + dot(dup, up[:, lanes], NT)
    keep_ref[...] = total[:TILE]
    give_ref[...] = total[TILE:]
    sent_ref[:, start + CORE_FF :] = dhid[...]
    if early:
        put_early(z, act_mine, act_theirs, gate_ref, sent_ref)


def mlp_back(at, mine, theirs, slope, up, down, rest, layer, early=None):
    right = block((TILE, D), lambda s: (0, 1))
    tokens = 2 * TILE
    extra = [] if early is None else [(early[0], right), (early[1], right), early[2]]
    width = SENT_LATE + (0 if early is None else SENT_CTX)
    return run(
        functools.partial(mlp_back_kernel, early=early is not None),
        at,
        [mine, theirs, slope, *up_inputs(up, rest, layer), *down_inputs(down, rest, layer), *extra],
        [
            shape((tokens, CORE_FF), BF16),
            shape((TILE, D), F32),
            shape((TILE, D), F32),
            shape((4, HALF), F32),
            shape((tokens, width), BF16),
        ],
        "mlp_back",
        4 * tokens * D * CORE_FF,
        8500000,
        [pltpu.VMEM((tokens, D), BF16), pltpu.VMEM((D, CORE_FF), BF16), pltpu.VMEM((CORE_FF, D), BF16)],
    )


def early_kernel(at, act_mine, act_theirs, gate_ref, ctx_ref, sent_ref):
    z = at[ZH]
    put_early(z, act_mine, act_theirs, gate_ref, sent_ref)
    for seq in range(2):
        ctx = ctx_ref[pl.ds(seq * SLOTS + 3 * (1 - z), 3)].reshape(QKV, TILE)
        sent_ref[seq * TILE : (seq + 1) * TILE, SENT_CTX : SENT_CTX + QKV] = ctx.T
    sent_ref[:, SENT_CTX + QKV :] = jnp.zeros((2 * TILE, HEAD), BF16)


def pack_early(at, mine, theirs, gate, ctx):
    right = block((TILE, D), lambda s: (0, 1))
    outs = [shape((2 * TILE, SENT_EARLY), BF16)]
    return run(early_kernel, at, [(mine, right), (theirs, right), gate, ctx], outs, "pack_early", 0, 0)[0]


def put_out_grads(grads, ctx_ref, tok, z, offset, length):
    for side in range(2):
        lanes = slice(side * HALF, (side + 1) * HALF)
        value = jnp.zeros((QKV, HALF), F32)
        for seq in range(2):
            ctx = ctx_ref[seq * SLOTS + 3 * z : seq * SLOTS + 3 * z + 3].reshape(QKV, TILE)
            value = value + dot(ctx, tok[seq * TILE : (seq + 1) * TILE, lanes])
        value = value.astype(BF16)
        for index in range(2):
            start = (2 * side + index) * length + offset
            grads[start : start + OUT_PART, :] = value[index * OUT_PART : (index + 1) * OUT_PART]


def by_chunks(grads, out_ref, length):
    out_ref[...] = grads[...].reshape(16, length // 4, HALF)


def own_grads_kernel(at, act_mine, act_theirs, mine_ref, theirs_ref, gate_ref, dup_ref, *refs, with_ctx):
    refs = list(refs)
    if with_ctx:
        ctx_ref, early_ref, late_ref, out_ref, done_ref, act, dhid, grads, tok, tok_other = refs
        length, start = PART_FIRST, 0
    else:
        late_ref, out_ref, done_ref, act, dhid, grads = refs
        early_ref = late_ref
        length, start = PART_SECOND, SENT_CTX
    z = at[ZH]
    done_ref[...] = jnp.zeros_like(done_ref)
    act[0:TILE] = act_mine[:, half_at(z)]
    act[TILE:] = act_theirs[:, half_at(z)]
    dhid[0:TILE] = mine_ref[...]
    dhid[TILE:] = theirs_ref[...]
    act_t, act_other = act[...].T, early_ref[:, 0:HALF].T
    for part in range(4):
        lanes = slice(part * HALF, (part + 1) * HALF)
        other = slice(start + part * HALF, start + (part + 1) * HALF)
        value = dot(act_t, dup_ref[:, lanes]) + dot(act_other, late_ref[:, other])
        grads[part * length : part * length + HALF, :] = value.astype(BF16)
    start += CORE_FF
    gate_t = gate_ref[:, pl.ds(pl.multiple_of(z * QUARTER, QUARTER), QUARTER)].T
    gate_other = early_ref[:, SENT_GATE:SENT_CTX].T
    for side in range(2):
        lanes = slice(side * HALF, (side + 1) * HALF)
        other = slice(start + side * HALF, start + (side + 1) * HALF)
        value = (dot(gate_t, dhid[:, lanes]) + dot(gate_other, late_ref[:, other])).astype(BF16)
        for index in range(2):
            row = (2 * side + index) * length + HALF
            grads[row : row + HALF, :] = value[index * HALF : (index + 1) * HALF]
    if with_ctx:
        assemble(tok, mine_ref[...], theirs_ref[...])
        assemble(tok_other, late_ref[0:TILE, start:], late_ref[TILE:, start:])
        ctx_other = early_ref[:, SENT_CTX : SENT_CTX + QKV].T
        for side in range(2):
            lanes = slice(side * HALF, (side + 1) * HALF)
            value = dot(ctx_other, tok_other[:, lanes])
            for seq in range(2):
                ctx = ctx_ref[pl.ds(seq * SLOTS + 3 * z, 3)].reshape(QKV, TILE)
                value = value + dot(ctx, tok[seq * TILE : (seq + 1) * TILE, lanes])
            value = value.astype(BF16)
            for index in range(2):
                row = (2 * side + index) * length + 2 * HALF
                grads[row : row + OUT_PART, :] = value[index * OUT_PART : (index + 1) * OUT_PART]
                grads[row + OUT_PART : row + OUT_PART + 32, :] = jnp.zeros((32, HALF), BF16)
    by_chunks(grads, out_ref, length)


def own_grads(at, mine, theirs, dmine, dtheirs, gate, dup, late, early=None, ctx=None):
    right = block((TILE, D), lambda s: (0, 1))
    tokens = 2 * TILE
    length = PART_SECOND if ctx is None else PART_FIRST
    inputs = [(mine, right), (theirs, right), dmine, dtheirs, gate, dup]
    inputs += [late] if ctx is None else [ctx, early, late]
    scratch = [pltpu.VMEM((tokens, HALF), BF16), pltpu.VMEM((tokens, D), BF16), pltpu.VMEM((4 * length, HALF), BF16)]
    if ctx is not None:
        scratch += [pltpu.VMEM((tokens, D), BF16)] * 2
    return run(
        functools.partial(own_grads_kernel, with_ctx=ctx is not None),
        at,
        inputs,
        [shape((16, length // 4, HALF), BF16), shape((8, 128), F32)],
        "own_grads",
        4 * tokens * 4 * length * HALF,
        8000000,
        scratch,
        token=True,
    )[0]


def grads_qkv_kernel(
    at, got_ref, mine_ref, theirs_ref, dmine_ref, dtheirs_ref, ctx_ref, out_ref, done_ref, act, tok, grads
):
    done_ref[...] = jnp.zeros_like(done_ref)
    assemble(act, mine_ref[...], theirs_ref[...])
    assemble(tok, dmine_ref[...], dtheirs_ref[...])
    for z in range(2):
        put_out_grads(grads, ctx_ref, tok, z, QKV_PART, PART_QKV)
        lanes = slice(z * HALF, (z + 1) * HALF)
        value = jnp.zeros((QKV_ROWS, HALF), F32)
        for seq in range(2):
            rows = got_ref[seq * SLOTS : seq * SLOTS + CORE_HEADS, 0:QKV, :].reshape(QKV_ROWS, TILE)
            value = value + dot(rows, act[seq * TILE : (seq + 1) * TILE, lanes])
        value = value.astype(BF16)
        for part in range(4):
            start = part * PART_QKV
            grads[start : start + QKV_PART, :] = value[part * QKV_PART : (part + 1) * QKV_PART]
        out_ref[:, z] = grads[...].reshape(16, CHUNK_QKV, HALF)


def grads_qkv(at, got, mine, theirs, dmine, dtheirs):
    left = block((TILE, D), lambda s: (0, 0))
    return run(
        grads_qkv_kernel,
        at,
        [got, (mine, left), (theirs, left), dmine, dtheirs, ctx_of(got)],
        [shape((16, 2, CHUNK_QKV, HALF), BF16), shape((8, 128), F32)],
        "grads_qkv",
        4 * TILE * D * 4 * PART_QKV,
        3800000,
        [pltpu.VMEM((2 * TILE, D), BF16)] * 2 + [pltpu.VMEM((4 * PART_QKV, HALF), BF16)],
        token=True,
    )[0]


def qkv_back_kernel(at, got_ref, own_ref, other_ref, keep_ref, give_ref, bias_ref):
    z = at[ZH]
    rows = TILE // 2
    sums = jnp.zeros((8, QKV_ROWS), F32)
    for seq in range(2):
        tok = got_ref[seq * SLOTS : seq * SLOTS + CORE_HEADS, 0:QKV, :].reshape(QKV_ROWS, TILE).T
        sums = sums + dot(jnp.ones((8, TILE), BF16), tok)
        here = slice(seq * rows, (seq + 1) * rows)
        for weights, at_z in ((own_ref, z), (other_ref, 1 - z)):
            value = dot(tok, weights[...])
            keep_ref[here, half_at(at_z)] = value[:rows]
            give_ref[here, half_at(at_z)] = value[rows:]
    bias_ref[...] = sums


def qkv_back(at, got, own, other):
    return run(
        qkv_back_kernel,
        at,
        [got, turned(own), turned(other)],
        [shape((TILE, D), F32), shape((TILE, D), F32), shape((8, QKV_ROWS), F32)],
        "qkv_back",
        4 * TILE * D * QKV_ROWS,
        3500000,
        limit=24,
    )


def qkv_rows(got_ref, tok, out_ref):
    for z in range(2):
        lanes = slice(z * HALF, (z + 1) * HALF)
        value = jnp.zeros((QKV_ROWS, HALF), F32)
        for seq in range(2):
            grads = got_ref[seq * SLOTS : seq * SLOTS + CORE_HEADS].reshape(QKV_ROWS, TILE)
            value = value + dot(grads, tok[seq * TILE : (seq + 1) * TILE, lanes])
        out_ref[z, 0:QKV_ROWS, :] = value.astype(BF16)


def qkv_grads_first_kernel(at, got_ref, mine_ref, theirs_ref, *refs):
    sums, (out_ref, tok, small) = refs[:6], refs[6:]
    assemble(tok, mine_ref[...], theirs_ref[...])
    qkv_rows(got_ref, tok, out_ref)

    def by_core(core):
        for z in range(2):
            small[...] = jnp.zeros((4 * SMALL, HALF), F32)
            for layer in range(LAYERS):
                norm_ref, up_ref, qkv_ref = sums[3 * layer : 3 * layer + 3]
                start = layer * SMALL
                for index in range(5):
                    small[start + index : start + index + 1] = norm_ref[2 * index + z : 2 * index + z + 1]
                for index in range(3):
                    part, half = (3 * z + index) // 2, (3 * z + index) % 2
                    for head in range(3):
                        lane = core * QKV + head * HEAD
                        source = (3 * half + head) * QKV + part * HEAD
                        small[start + 5 + index : start + 6 + index, lane : lane + HEAD] = qkv_ref[
                            0:1, source : source + HEAD
                        ]
                for side in range(2):
                    row = start + 8 + 2 * core + side
                    small[row : row + 1] = up_ref[2 * z + side : 2 * z + side + 1]
            out_ref[z, QKV_ROWS : QKV_ROWS + 4 * SMALL, :] = small[...].astype(BF16)
            used = QKV_ROWS + 4 * SMALL
            out_ref[z, used:, :] = jnp.zeros((QKV_FIRST - used, HALF), BF16)

    for core in range(2):
        pl.when(at[CORE] == core)(functools.partial(by_core, core))


def qkv_grads_first(at, got, mine, theirs, sums, after):
    left = block((TILE, D), lambda s: (0, 0))
    return run(
        qkv_grads_first_kernel,
        at,
        [got, (mine, left), (theirs, left), *sums],
        [shape((2, QKV_FIRST, HALF), BF16)],
        "qkv_grads_first",
        4 * TILE * D * QKV_ROWS,
        3300000,
        [pltpu.VMEM((2 * TILE, D), BF16), pltpu.VMEM((4 * SMALL, HALF), F32)],
        after=after,
    )[0]


def norm_back_kernel(
    at, keep0, got0, keep1, got1, hat_ref, inverse_ref, gain_ref, dstream_ref, next_ref, low_ref, sums_ref
):
    first, second = keep0[...] + got0[...], keep1[...] + got1[...]
    hat = hat_ref[...]
    dstream = dstream_ref[...].astype(F32)
    dhat = first * gain_ref[0:1] + second * gain_ref[1:2]
    grad = inverse_ref[...] * (
        dhat
        - jnp.mean(dhat, axis=-1, keepdims=True)
        - hat * jnp.mean(dhat * hat, axis=-1, keepdims=True)
    )
    total = dstream + grad
    next_ref[...] = total
    low_ref[...] = total.astype(BF16)
    rows = (first * hat, second * hat, first, second, dstream.astype(BF16).astype(F32))
    for index, value in enumerate(rows):
        row = jnp.sum(value, axis=0, keepdims=True)
        sums_ref[2 * index : 2 * index + 1, :] = row[:, :HALF]
        sums_ref[2 * index + 1 : 2 * index + 2, :] = row[:, HALF:]


def norm_back(at, first, second, hat, inverse, gain, dstream):
    return run(
        norm_back_kernel,
        at,
        [*first, *second, hat, inverse, gain, dstream],
        [shape((TILE, D), F32), shape((TILE, D), BF16), shape((10, HALF), F32)],
        "norm_back",
        2000000,
        3400000,
        limit=24,
    )


def rows_of(part, start, count, chunk, length, offset=0):
    at = start
    while at < start + count:
        step = min(chunk - at % chunk, start + count - at)
        yield (4 * part + at // chunk) * length + offset + at % chunk, at - start, step
        at += step


def place_mlp(source, core, up_ref, down_ref, chunk, length, offset=0):
    for part in range(4):
        z, side = part // 2, part % 2
        column = z * CORE_FF + core * QUARTER + side * HALF
        for source_row, row, count in rows_of(part, 0, HALF, chunk, length, offset):
            up_ref[0, row : row + count, column : column + HALF] = source[source_row : source_row + count, :].astype(F32)
        side, index = part // 2, part % 2
        lanes = slice(side * HALF, (side + 1) * HALF)
        first = core * QUARTER + index * HALF
        for source_row, row, count in rows_of(part, HALF, HALF, chunk, length, offset):
            row += first
            down_ref[0, row : row + count, lanes] = source[source_row : source_row + count, :].astype(F32)


def for_cores(at, mine, theirs, put):
    for here, source in ((True, mine), (False, theirs)):
        for core in range(2):
            pl.when((at[CORE] == core) == here)(functools.partial(put, core, source))


UP_SHAPE, DOWN_SHAPE, OUT_SHAPE = (LAYERS, HALF, FF), (LAYERS, FF // 2, D), (LAYERS, HALF, D)
QKV_SHAPE = (LAYERS, HALF, 3 * D)
PLACED = (UP_SHAPE, DOWN_SHAPE, OUT_SHAPE)


def place_out(source, core, out_ref, first, chunk, length, offset):
    for part in range(4):
        lanes = slice((part // 2) * HALF, (part // 2 + 1) * HALF)
        start = core * QKV + (part % 2) * OUT_PART
        for source_row, row, count in rows_of(part, first, OUT_PART, chunk, length, offset):
            row += start
            out_ref[0, row : row + count, lanes] = source[source_row : source_row + count, :].astype(F32)


def place_turned(rows_ref, out_ref, part, z):
    column = part * D + z * HALF
    out_ref[0, :, column : column + HALF] = rows_ref[...].T


LENGTH = CHUNK_FIRST + CHUNK_QKV + CHUNK_SECOND


def place_long_kernel(at, mine_ref, theirs_ref, qkv_in, token, up_ref, down_ref, out_ref, qkv_ref, rows_ref):
    def first(core, source):
        place_mlp(source, core, up_ref, down_ref, CHUNK_FIRST, LENGTH)
        place_out(source, core, out_ref, 2 * HALF, CHUNK_FIRST, LENGTH, 0)

    def second(core, source):
        place_mlp(source, core, up_ref, down_ref, CHUNK_SECOND, LENGTH, CHUNK_FIRST + CHUNK_QKV)
        place_out(source, core, out_ref, QKV_PART, CHUNK_QKV, LENGTH, CHUNK_FIRST)

    @pl.when(pl.program_id(0) == 0)
    def _():
        for_cores(at, mine_ref, theirs_ref, first)
        for part in range(3):
            for z in range(2):

                def put_rows(core, source):
                    for head in range(3):
                        row = (z * 3 + head) * QKV + part * HEAD
                        to = core * QKV + head * HEAD
                        for start in range(row, row + HEAD, 32):
                            pieces = rows_of(start // QKV_PART, start % QKV_PART, 32, CHUNK_QKV, LENGTH, CHUNK_FIRST)
                            for source_row, more, count in pieces:
                                here = to + start - row + more
                                rows_ref[here : here + count, :] = source[source_row : source_row + count, :].astype(F32)

                for_cores(at, mine_ref, theirs_ref, put_rows)
                place_turned(rows_ref, qkv_ref, part, z)

    @pl.when(pl.program_id(0) == 1)
    def _():
        for_cores(at, mine_ref, theirs_ref, second)


def place_long(at, mine, theirs, qkv):
    anywhere = pl.BlockSpec(memory_space=pl.ANY)
    once = pl.BlockSpec(mine.shape, lambda i, s: (0, 0), pipeline_mode=pl.Buffered(1))
    return pl.pallas_call(
        place_long_kernel,
        grid_spec=pltpu.PrefetchScalarGridSpec(
            num_scalar_prefetch=1,
            grid=(LAYERS,),
            in_specs=[once, once, anywhere, anywhere],
            out_specs=[pl.BlockSpec((1,) + dims[1:], lambda i, s: (i, 0, 0)) for dims in PLACED]
            + [pl.BlockSpec((1,) + QKV_SHAPE[1:], lambda i, s: (1, 0, 0))],
            scratch_shapes=[pltpu.VMEM((HALF, HALF), F32)],
        ),
        out_shape=[shape(dims, F32) for dims in (*PLACED, QKV_SHAPE)],
        input_output_aliases={3: 3},
        compiler_params=pltpu.CompilerParams(vmem_limit_bytes=60 * 1024 * 1024),
        cost_estimate=pl.CostEstimate(flops=1, bytes_accessed=1, transcendentals=0),
        name="place_long",
    )(at, mine, theirs, qkv, *LATEST)


def place_qkv_kernel(
    at, mine_ref, theirs_ref, out_ref, gain_ref, offset_ref, hidden_ref, again_ref, qkv_ref, up_ref, rows_ref
):
    for part in range(3):
        for z in range(2):

            def put(core, source):
                for head in range(3):
                    row = (z * 3 + head) * QKV + part * HEAD
                    to = core * QKV + head * HEAD
                    rows_ref[to : to + HEAD, :] = source[row : row + HEAD, :].astype(F32)

            for_cores(at, mine_ref, theirs_ref, put)
            place_turned(rows_ref, out_ref, part, z)
    rows = slice(QKV_ROWS, QKV_ROWS + 2 * SMALL + 8)
    small = mine_ref[rows, :].astype(F32) + theirs_ref[rows, :].astype(F32)
    for layer in range(LAYERS):
        start = layer * SMALL
        gain_ref[layer] = small[start : start + 2]
        offset_ref[layer] = small[start + 2 : start + 4]
        hidden_ref[layer : layer + 1] = small[start + 4 : start + 5]
        again_ref[layer : layer + 1] = small[start + 4 : start + 5]
        for index in range(3):
            lanes = slice(index * HALF, (index + 1) * HALF)
            qkv_ref[layer : layer + 1, lanes] = small[start + 5 + index : start + 6 + index]
        for index in range(4):
            lanes = slice(index * HALF, (index + 1) * HALF)
            up_ref[layer : layer + 1, lanes] = small[start + 8 + index : start + 9 + index]


def place_qkv(at, mine, theirs):
    outs = [shape((LAYERS, HALF, 3 * D), F32)]
    specs = [block((1, HALF, 3 * D), lambda s: (0, 0, 0))]
    for dims in ((2, HALF), (2, HALF), (HALF,), (HALF,), (3 * HALF,), (4 * HALF,)):
        outs.append(shape((LAYERS,) + dims, F32))
        specs.append(block((LAYERS,) + dims))
    return run(
        place_qkv_kernel,
        at,
        [mine, theirs],
        outs,
        "place_qkv",
        0,
        6000000,
        [pltpu.VMEM((HALF, HALF), F32)],
        limit=40,
        out_specs=specs,
    )


ROW_GAIN, ROW_OFFSET, ROW_QKV, ROW_OUT, ROW_UP, ROW_DOWN, SMALL_ROWS = 0, 4, 8, 14, 16, 24, 32


def gather_small(refs):
    gain, offset, qkv, out, up, down = (ref[...].astype(F32) for ref in refs)
    rows = [gain.reshape(4, HALF), offset.reshape(4, HALF)]
    rows += [qkv[layer : layer + 1, part * HALF : (part + 1) * HALF] for layer in range(LAYERS) for part in range(3)]
    rows.append(out)
    rows += [up[layer : layer + 1, part * HALF : (part + 1) * HALF] for layer in range(LAYERS) for part in range(4)]
    rows += [down, jnp.zeros((SMALL_ROWS - ROW_DOWN - LAYERS, HALF), F32)]
    return jnp.concatenate(rows, axis=0)


def spread_small_kernel(at, own_ref, other_ref, *outs):
    own, other = own_ref[...].astype(F32), other_ref[...].astype(F32)
    swap = at[ZH] == 1
    halves = jnp.where(swap, other, own), jnp.where(swap, own, other)

    def row(index, z):
        return halves[z][index : index + 1]

    def by_core(core):
        for layer in range(LAYERS):
            qkv_ref, up_ref = outs[5 * layer + 2], outs[5 * layer + 4]
            for part in range(3):
                for z in range(2):
                    place = part * 2 + z
                    values = row(ROW_QKV + layer * 3 + place % 3, place // 3)
                    for head in range(3):
                        lane = core * QKV + head * HEAD
                        qkv_ref[3 * z + head : 3 * z + head + 1, part * HEAD : (part + 1) * HEAD] = values[
                            :, lane : lane + HEAD
                        ]
            for z in range(2):
                for side in range(2):
                    lane = z * QUARTER + side * HALF
                    up_ref[:, lane : lane + HALF] = row(ROW_UP + 4 * layer + 2 * core + side, z)

    for core in range(2):
        pl.when(at[CORE] == core)(functools.partial(by_core, core))
    for layer in range(LAYERS):
        gain_ref, offset_ref, _, rest_ref, _ = outs[5 * layer : 5 * layer + 5]
        for z in range(2):
            lanes = slice(z * HALF, (z + 1) * HALF)
            for index in range(2):
                gain_ref[index : index + 1, lanes] = row(ROW_GAIN + 2 * layer + index, z)
                offset_ref[index : index + 1, lanes] = row(ROW_OFFSET + 2 * layer + index, z)
            rest_ref[:, lanes] = row(ROW_OUT + layer, z) + row(ROW_DOWN + layer, z)


def spread_small(at, rows, other):
    outs = [shape((2, D), F32), shape((2, D), F32), shape((8, QKV), F32), shape((1, D), F32), shape((1, CORE_FF), F32)]
    spec = block((SMALL_ROWS, HALF), lambda s: (QKV_ROWS // SMALL_ROWS, 0))
    values = run(spread_small_kernel, at, [(rows, spec), (other, spec)], outs * LAYERS, "small_spread", 0, 0)
    return zip(values[:5], values[5:])


EVERY = ("zh", "xh", "xl", "y", "zl")
ACROSS = ("xh", "xl", "y")
CHIPS = ("xl", "zl", "y")


def exchange(values):
    return lax.ppermute(values, "core", SWAP)


def scatter_sum(grads):
    parts = grads.reshape(64, -1, HALF)
    parts = lax.all_to_all(parts, EVERY, 0, 0, tiled=True)
    return jnp.sum(parts.astype(F32), axis=0).astype(BF16)


def add_from(part, other):
    return (part.astype(F32) + other.astype(F32)).astype(BF16)


def ring(values, axis, by):
    return lax.ppermute(values, axis, [(place, (place + by) % 4) for place in range(4)])


X_RING, Y_RING = ("xh", "xl"), "y"


def around(pieces, first, second):
    return [
        (ring(piece, first if index < 4 else second, index % 4) if index % 4 else piece)
        for index, piece in enumerate(pieces)
    ]


def sum_x(grads):
    return lax.psum_scatter(grads.reshape(-1, HALF), X_RING, scatter_dimension=0, tiled=True)


def sum_y(part):
    return lax.psum_scatter(part, Y_RING, scatter_dimension=0, tiled=True)


def sum_grid(grads):
    parts = lax.all_to_all(grads, ACROSS, 0, 0, tiled=True)
    return jnp.sum(parts.astype(F32), axis=0).astype(BF16)


def sum_near(part):
    return add_from(part, lax.ppermute(part, "zl", SWAP))


def sum_depth(zh, part):
    part = part.reshape(2, -1, HALF)
    keep = jnp.where(zh == 0, part[0], part[1])
    give = jnp.where(zh == 0, part[1], part[0])
    near = lax.ppermute(keep, "zl", SWAP)
    far = lax.ppermute(give, "zh", SWAP)
    across = lax.ppermute(give, ("zl", "zh"), [(0, 3), (3, 0), (1, 2), (2, 1)])
    total = (keep.astype(F32) + near.astype(F32)) + (far.astype(F32) + across.astype(F32))
    return total.astype(BF16)


def gather_short(part):
    copies = jnp.broadcast_to(part[None], (32,) + part.shape)
    return lax.all_to_all(copies, EVERY[1:], 0, 0, tiled=True).reshape(-1, HALF)


def token_places(offsets, lengths):
    ends = jnp.cumsum(lengths)
    before = ends[:, None] <= offsets[None, :]
    start = jnp.max(jnp.where(before, ends[:, None], 0), axis=0)
    return start, offsets >= ends[DOCS - 2]


def rotary(places):
    frequency = 1.0 / 10000.0 ** (jnp.arange(0, ROT, 2).astype(F32) / ROT)
    angles = frequency[:, None] * places.astype(F32)[None, :]
    return jnp.cos(angles), jnp.sin(angles)


def local(
    hidden_in,
    doc_lengths,
    norm_gain,
    norm_bias,
    qkv_weight,
    qkv_bias,
    out_weight,
    out_bias,
    up_weight,
    up_bias,
    down_weight,
    down_bias,
    cotangent,
):
    LATEST.clear()
    zh, core, xh, xl, zl, y = (lax.axis_index(name) for name in ("zh", "core", "xh", "xl", "zl", "y"))
    chip = (xl * 2 + zl) * 4 + y
    x = xh * 2 + xl
    lengths = doc_lengths[0]

    unit_seq = xl
    unit_half = jnp.where(unit_seq == 0, xh, 1 - xh)
    unit_swap = jnp.where(unit_seq == core, 0, TILE // 2)
    last_chip = jnp.where(unit_seq == 0, TILES - 1, 0)
    at = jnp.stack(
        [core, zh, unit_seq, unit_swap, 1 - unit_half, last_chip, x, y, x * 4 + y]
    ).astype(jnp.int32)

    lane = jnp.arange(TILE, dtype=jnp.int32)
    seq0_tile = xh * TILES + chip
    places = []
    for seq, tile in ((0, seq0_tile), (1, 2 * TILES - 1 - seq0_tile)):
        offsets = tile * TILE + (lane ^ jnp.where(seq == core, 0, TILE // 2))
        places.append(offsets - token_places(offsets, lengths[seq])[0])
    own_tables = rotary(jnp.concatenate(places))
    unit_lengths = lax.dynamic_index_in_dim(lengths, unit_seq, 0, keepdims=False)
    relative = (jnp.arange(TILES, dtype=jnp.int32)[:, None] * TILE + (lane ^ unit_swap)[None, :]).reshape(-1)
    offsets = unit_half * UNIT + relative
    start, padding = token_places(offsets, unit_lengths)
    unit_tables = rotary(offsets - start)
    low = jnp.where(padding, offsets, jnp.maximum(start, offsets - (WINDOW - 1)))
    low = (low - unit_half * UNIT).reshape(1, UNIT)
    pos = relative.reshape(1, UNIT)

    def to_units(values):
        return lax.all_to_all(values.reshape(TILES, -1, TILE), CHIPS, 0, 0, tiled=True)

    def halo_of(got):
        last = lax.dynamic_index_in_dim(got, last_chip, 0, keepdims=False)
        return lax.ppermute(last[HEAD:QKV], "xh", SWAP)

    def finish_attention(packed, edge, tail):
        edge = lax.ppermute(edge, "xh", SWAP)
        return to_units(add_edge(at, packed, tail, edge, *unit_tables))

    small = (norm_gain, norm_bias, qkv_bias, out_bias, up_bias, down_bias)

    def gather_chunks(chunk):
        return lax.all_gather(chunk, ACROSS, axis=0, tiled=True).reshape(16, CHUNK, HALF)

    weights = begin(at, qkv_weight, up_weight, down_weight, small)
    own_qkv, other_qkv = [weights], [lax.ppermute(weights, "zh", SWAP)]
    rest = [gather_chunks(other_qkv[0][CHUNK_AT:])]
    tokens = cotangent[0]
    dhid1 = (tokens, exchange(tokens))
    gain, offset, b_qkv, b_rest, b_up = spread_small(at, weights, other_qkv[0])
    _, hat0, inverse0, act = norms(at, hidden_in[0], None, gain[0], offset[0])
    acts0 = (act, exchange(act))
    got0 = to_units(project_qkv(at, *acts0, own_qkv[0], other_qkv[0], b_qkv[0], *own_tables))
    rows, weights = begin_rest(at, qkv_weight, up_weight, down_weight, out_weight)
    rows, weights = held(at, [rows, weights], (got0,))
    rows = lax.ppermute(rows, "zh", SWAP)
    own_qkv.append(weights)
    other_qkv.append(lax.ppermute(weights, "zh", SWAP))
    outs = (out_weight, rows)
    halo0 = halo_of(got0)
    ctx0, *saved0 = attention(at, got0, halo0, low, pos)
    rest.append(gather_chunks(held(at, [rows[REST_CHUNK:]])[0]))
    ctx0 = to_units(ctx0)
    gate0, slope0, total = feed_forward(at, *acts0, b_up[0], up_weight, down_weight, rest, 0)
    dctx1 = grad_ctx(at, *dhid1, outs, 1)
    keep, give = attention_out(at, ctx0, outs, total, 0)
    added = (keep, exchange(give), b_rest[0])

    stream, hat1, inverse1, act = norms(at, hidden_in[0], added, gain[1], offset[1])
    acts1 = (act, exchange(act))
    got1 = to_units(project_qkv(at, *acts1, own_qkv[1], other_qkv[1], b_qkv[1], *own_tables, dctx1))
    gate1, slope1, mlp1 = feed_forward(at, *acts1, b_up[1], up_weight, down_weight, rest, 1)
    dup1, keep, give, sum_up1, sent = mlp_back(
        at, *dhid1, slope1, up_weight, down_weight, rest, 1, (*acts1, gate1)
    )
    second1 = (keep, exchange(give))
    late1 = lax.ppermute(held(at, [sent], (got1,))[0], "zh", SWAP)
    halo1 = halo_of(got1)
    packed = attention(at, got1, halo1, low, pos, unit_tables)
    dqkv1 = finish_attention(*packed)
    grads1 = own_grads(at, *acts1, *dhid1, gate1, dup1, late1)
    part1 = sum_x(held(at, [grads1], (dqkv1,))[0])
    keep, give, sum_qkv1 = qkv_back(at, dqkv1, own_qkv[1], other_qkv[1])
    first1 = (keep, exchange(give))
    early0 = lax.ppermute(pack_early(at, *acts0, gate0, ctx0), "zh", SWAP)
    dstream, low_stream, sum_norm1 = norm_back(at, first1, second1, hat1, inverse1, gain[1], tokens)

    dhid0 = (low_stream, exchange(low_stream))
    dctx0 = to_units(grad_ctx(at, *dhid0, outs, 0))
    dup0, keep, give, sum_up0, sent = mlp_back(at, *dhid0, slope0, up_weight, down_weight, rest, 0)
    second0 = (keep, exchange(give))
    gradsq = grads_qkv(at, dqkv1, *acts1, *dhid1)
    gradsq, sent, part1 = held(at, [gradsq, sent, part1], (dctx0, early0))
    late0 = lax.ppermute(sent, "zh", SWAP)
    part1 = sum_y(part1)
    partq = sum_x(gradsq)
    packed = attention(at, got0, halo0, low, pos, unit_tables, dctx0, saved0)
    dqkv0 = finish_attention(*packed)
    grads0 = own_grads(at, *acts0, *dhid0, gate0, dup0, late0, early0, ctx0)
    part0 = sum_grid(held(at, [grads0], (dqkv0,))[0])
    keep, give, sum_qkv0 = qkv_back(at, dqkv0, own_qkv[0], other_qkv[0])
    first0 = (keep, exchange(give))
    dstream, _, sum_norm0 = norm_back(at, first0, second0, hat0, inverse0, gain[0], dstream)
    hidden_grad = dstream[None]
    partq, part1 = held(at, [partq, part1])
    partq = sum_y(partq)

    sums = (sum_norm0, sum_up0, sum_qkv0, sum_norm1, sum_up1, sum_qkv1)
    part_qkv = scatter_sum(qkv_grads_first(at, dqkv0, *acts0, sums, (part0,)))
    part0, partq, part1 = held(at, [part0, partq, part1])
    total = [sum_near(part0), sum_depth(zh, partq), sum_near(part1)]
    (total,) = held(at, [jnp.concatenate(total)])
    long = lax.all_gather(total, ACROSS, axis=0, tiled=True)
    keep, give = attention_out(at, dqkv1, outs, mlp1, 1, (part_qkv,))
    hidden_out = (stream + (keep + exchange(give) + b_rest[1])).astype(BF16)[None]
    qkv0 = gather_short(part_qkv)
    g_qkv, g_gain, g_offset, g_hidden, g_again, g_bqkv, g_bup = place_qkv(at, qkv0, exchange(qkv0))
    (long,) = held(at, [long])
    g_up, g_down, g_out, g_qkv = place_long(at, long, exchange(long), g_qkv)
    return (
        hidden_out,
        hidden_grad,
        g_gain,
        g_offset,
        g_qkv,
        g_bqkv,
        g_out,
        g_hidden,
        g_up,
        g_bup,
        g_down,
        g_again,
    )


def solution(mesh):
    fine = Mesh(
        mesh.devices.reshape(2, 2, 2, 4, 2, 2), ("xh", "xl", "zl", "y", "core", "zh")
    )
    ctx = ("xh", "xl", "zl", "y", "core")
    rows = P(None, "zh", None)
    tokens = P("zh", ctx, None)
    last = P(None, None, "zh")
    bias = P(None, "zh")
    return jax.shard_map(
        local,
        mesh=fine,
        in_specs=(tokens, P("zh", None, None), last, last, rows, bias, rows, bias, rows, bias, rows, bias, tokens),
        out_specs=(tokens, tokens, last, last, rows, bias, rows, bias, rows, bias, rows, bias),
        check_vma=False,
    )
```

```python
import functools

import jax
import jax.numpy as jnp
from jax import lax
from jax.experimental import pallas as pl
from jax.experimental.pallas import tpu as pltpu
from jax.sharding import Mesh
from jax.sharding import PartitionSpec as P

D = 768
HALF = D // 2
HEADS = 12
HEAD = 64
FF = 3072
ROT = 16
LAYERS = 2
WINDOW = 1024
DOCS = 8
TILE = 128
TILES = 16
UNIT = TILE * TILES
SLOTS = 8
CORE_HEADS = HEADS // 2
QKV = 3 * HEAD
QKV_ROWS = CORE_HEADS * QKV
CORE_FF = FF // 2
QUARTER = FF // 4

CHUNK_UP = 96
CHUNK_DOWN = 48
CHUNK = CHUNK_UP + 2 * CHUNK_DOWN
QKV_PART = QKV_ROWS // 4
OUT_PART = QKV // 2
PART_SECOND = 2 * HALF
PART_FIRST = 2 * HALF + OUT_PART + 32
PART_QKV = QKV_PART + OUT_PART
CHUNK_SECOND, CHUNK_FIRST, CHUNK_QKV = PART_SECOND // 4, PART_FIRST // 4, PART_QKV // 4
SENT_GATE, SENT_CTX = HALF, HALF + QUARTER
SENT_EARLY = SENT_CTX + QKV + HEAD
SENT_LATE = CORE_FF + D
QKV_FIRST = 32 * 40
SMALL = 12

BLOCKED = -1e30
EPSILON = 1e-05
SWAP = [(0, 1), (1, 0)]
F32 = jnp.float32
BF16 = jnp.bfloat16

NN = (((1,), (0,)), ((), ()))
NT = (((1,), (1,)), ((), ()))
TN = (((0,), (0,)), ((), ()))


def dot(left, right, dims=NN):
    return lax.dot_general(left, right, dims, preferred_element_type=F32)


def shape(dims, kind):
    return jax.ShapeDtypeStruct(dims, kind)


def block(dims, *at):
    place = at[0] if at else (lambda s: (0,) * len(dims))
    return pl.BlockSpec(dims, lambda i, s: place(s))


def whole(array):
    return block(array.shape)


LATEST = []


def run(
    kernel, scalars, inputs, outs, name, flops, moved, scratch=(), limit=40, aliases=None, exps=0, out_specs=None, after=(), token=False
):
    after = list(after) + LATEST
    arrays = [item[0] if isinstance(item, tuple) else item for item in inputs] + after
    specs = [item[1] if isinstance(item, tuple) else whole(item) for item in inputs]
    specs += [pl.BlockSpec(memory_space=pl.ANY)] * len(after)
    if out_specs is None:
        out_specs = [block(out.shape) for out in outs]
    count = len(inputs)

    def body(at, *refs):
        kernel(at, *refs[:count], *refs[count + len(after) :])

    results = pl.pallas_call(
        body,
        grid_spec=pltpu.PrefetchScalarGridSpec(
            num_scalar_prefetch=1,
            grid=(1,),
            in_specs=specs,
            out_specs=out_specs,
            scratch_shapes=list(scratch),
        ),
        out_shape=outs,
        input_output_aliases=aliases or {},
        compiler_params=pltpu.CompilerParams(vmem_limit_bytes=60 * 1024 * 1024),
        cost_estimate=pl.CostEstimate(flops=1, bytes_accessed=1, transcendentals=0),
        name=name,
    )(scalars, *arrays)
    LATEST[:] = [results[-1] if token else min(results, key=lambda result: result.size)]
    return results


def held(at, values, after=()):
    anywhere = pl.BlockSpec(memory_space=pl.ANY)

    def kernel(at, *refs):
        refs[-1][0] = 0

    outs = [shape(value.shape, value.dtype) for value in values] + [shape((1,), jnp.int32)]
    specs = [anywhere] * len(values) + [pl.BlockSpec(memory_space=pltpu.SMEM)]
    aliases = {1 + index: index for index in range(len(values))}
    inputs = [(value, anywhere) for value in values]
    return run(kernel, at, inputs, outs, "held", 0, 0, aliases=aliases, out_specs=specs, after=after, token=True)[:-1]


CORE, ZH, REVERSE, SWAPPED, FIRST_HALF, LAST_CHIP, RING_X, RING_Y, SPOT = range(9)


def half_at(index):
    return pl.ds(pl.multiple_of(index * HALF, HALF), HALF)


def turn(at, raw_ref, out_ref):
    def by_core(core):
        for part in range(3):
            for z in range(2):
                start = part * D + z * HALF + core * QKV
                piece = raw_ref[0, :, start : start + QKV].T
                for head in range(3):
                    row = (z * 3 + head) * QKV + part * HEAD
                    out_ref[row : row + HEAD, :] = piece[head * HEAD : (head + 1) * HEAD]

    for core in range(2):
        pl.when(at[CORE] == core)(functools.partial(by_core, core))


def put_chunk(up_ref, down_ref, out_ref):
    out_ref[0:CHUNK_UP] = up_ref[0]
    out_ref[CHUNK_UP : CHUNK_UP + CHUNK_DOWN] = down_ref[0, :, :HALF]
    out_ref[CHUNK_UP + CHUNK_DOWN :] = down_ref[0, :, HALF:]


SMALL_AT, CHUNK_AT = QKV_ROWS, QKV_ROWS + 32


def begin_kernel(at, qkv_ref, up_ref, down_ref, *refs):
    small, out_ref = refs[:-1], refs[-1]
    turn(at, qkv_ref, out_ref)
    out_ref[SMALL_AT:CHUNK_AT] = gather_small(small).astype(BF16)
    put_chunk(up_ref, down_ref, out_ref.at[CHUNK_AT:])


def begin(at, qkv_weight, up_weight, down_weight, small):
    return run(
        begin_kernel,
        at,
        [
            (qkv_weight, block((1, HALF, 3 * D), lambda s: (0, 0, 0))),
            *chunk_inputs(up_weight, down_weight, 0),
            *small,
        ],
        [shape((CHUNK_AT + CHUNK, HALF), BF16)],
        "begin",
        0,
        2700000,
    )[0]


def chunk_inputs(up_weight, down_weight, layer):
    column = lambda s: (s[RING_Y] // 2) * 4 + s[CORE] * 2 + s[RING_Y] % 2
    return [
        (up_weight, block((1, CHUNK_UP, HALF), lambda s: (layer, s[RING_X], column(s)))),
        (down_weight, block((1, CHUNK_DOWN, D), lambda s: (layer, s[CORE] * 16 + s[SPOT], 0))),
    ]


REST_CHUNK = LAYERS * HALF


def begin_rest_kernel(at, qkv_ref, up_ref, down_ref, out_ref, rows_ref, turned_ref):
    for layer in range(LAYERS):
        for side in range(2):
            row = layer * HALF + side * QKV
            rows_ref[row : row + QKV] = out_ref[layer, :, side * HALF : (side + 1) * HALF]
    put_chunk(up_ref, down_ref, rows_ref.at[REST_CHUNK:])
    turn(at, qkv_ref, turned_ref)


def begin_rest(at, qkv_weight, up_weight, down_weight, out_weight):
    return run(
        begin_rest_kernel,
        at,
        [
            (qkv_weight, block((1, HALF, 3 * D), lambda s: (1, 0, 0))),
            *chunk_inputs(up_weight, down_weight, 1),
            (out_weight, block((LAYERS, QKV, D), lambda s: (0, s[CORE], 0))),
        ],
        [shape((REST_CHUNK + CHUNK, HALF), BF16), shape((QKV_ROWS, HALF), BF16)],
        "begin_rest",
        0,
        1500000,
    )


def fill_up(z, up_ref, own0_ref, own1_ref, rest_ref):
    up_ref[half_at(z), 0:QUARTER] = own0_ref[0]
    up_ref[half_at(z), QUARTER:] = own1_ref[0]
    for chunk in range(16):
        x, y = chunk // 4, chunk % 4
        rows = pl.ds(pl.multiple_of((1 - z) * HALF + CHUNK_UP * x, 32), CHUNK_UP)
        up_ref[rows, y * HALF : (y + 1) * HALF] = rest_ref[chunk]


def fill_down(z, down_ref, own_ref, rest_ref):
    down_ref[pl.ds(pl.multiple_of(z * QUARTER, QUARTER), QUARTER), :] = own_ref[0]
    for chunk in range(16):
        rows = pl.ds(pl.multiple_of((1 - z) * QUARTER + CHUNK_DOWN * chunk, 16), CHUNK_DOWN)
        down_ref[rows, 0:HALF] = rest_ref[chunk, 0:CHUNK_DOWN]
        down_ref[rows, HALF:] = rest_ref[chunk, CHUNK_DOWN:]


def fill_out(z, out_ref, own_ref, other_ref):
    out_ref[pl.ds(pl.multiple_of(z * QKV, QKV), QKV), :] = own_ref[0]
    for side in range(2):
        rows = slice(side * QKV, (side + 1) * QKV)
        out_ref[pl.ds(pl.multiple_of((1 - z) * QKV, QKV), QKV), side * HALF : (side + 1) * HALF] = other_ref[rows, :]


def up_inputs(weights, rest, layer):
    own = [
        (weights, block((1, HALF, QUARTER), lambda s, z=z: (layer, 0, 2 * z + s[CORE]))) for z in range(2)
    ]
    return own + [(rest[layer], block((16, CHUNK_UP, HALF), lambda s: (0, 0, 0)))]


def down_inputs(weights, rest, layer):
    return [
        (weights, block((1, QUARTER, D), lambda s: (layer, s[CORE], 0))),
        (rest[layer], block((16, 2 * CHUNK_DOWN, HALF), lambda s: (0, 1, 0))),
    ]


def out_inputs(own, other, layer):
    return [
        (own, block((1, QKV, D), lambda s: (layer, s[CORE], 0))),
        (other, block((HALF, HALF), lambda s: (layer, 0))),
    ]


def norm_kernel(at, *refs, first):
    if first:
        stream_ref, gain_ref, offset_ref, hat_ref, inverse_ref, act_ref = refs
        stream = stream_ref[...].astype(F32)
    else:
        stream_ref, keep_ref, got_ref, bias_ref, gain_ref, offset_ref, next_ref, hat_ref, inverse_ref, act_ref = refs
        stream = stream_ref[...].astype(F32) + (keep_ref[...] + got_ref[...] + bias_ref[...])
        next_ref[...] = stream
    centered = stream - jnp.mean(stream, axis=-1, keepdims=True)
    inverse = lax.rsqrt(jnp.mean(centered * centered, axis=-1, keepdims=True) + EPSILON)
    hat = centered * inverse
    hat_ref[...] = hat
    inverse_ref[...] = inverse
    act_ref[:, 0:D] = (hat * gain_ref[0:1] + offset_ref[0:1]).astype(BF16)
    act_ref[:, D:] = (hat * gain_ref[1:2] + offset_ref[1:2]).astype(BF16)


def norms(at, stream, added, gain, offset):
    outs = [shape((TILE, D), F32), shape((TILE, 1), F32), shape((TILE, 2 * D), BF16)]
    if added is None:
        kernel = functools.partial(norm_kernel, first=True)
        return [None, *run(kernel, at, [stream, gain, offset], outs, "norms", 1000000, 1200000)]
    kernel = functools.partial(norm_kernel, first=False)
    outs = [shape((TILE, D), F32)] + outs
    return run(kernel, at, [stream, *added, gain, offset], outs, "norms", 1000000, 2400000)


def assemble(target_ref, mine, theirs):
    rows = TILE // 2
    target_ref[0:rows] = mine[:rows]
    target_ref[rows : 2 * rows] = theirs[:rows]
    target_ref[2 * rows : 3 * rows] = mine[rows:]
    target_ref[3 * rows :] = theirs[rows:]


def qkv_kernel(at, mine_ref, theirs_ref, own_ref, other_ref, bias_ref, cos_ref, sin_ref, *refs):
    along, (out_ref, tok_ref, act_t) = refs[:-3], refs[-3:]
    z = at[ZH]
    assemble(tok_ref, mine_ref[...], theirs_ref[...])
    act_t[...] = tok_ref[...].T
    cosine, sine = cos_ref[...], sin_ref[...]

    def rotated(part):
        low, high = part[:8], part[8:ROT]
        return jnp.concatenate(
            [low * cosine - high * sine, high * cosine + low * sine, part[ROT:]], axis=0
        )

    own_act, other_act = act_t[half_at(z), :], act_t[half_at(1 - z), :]
    for head in range(CORE_HEADS):
        rows = slice(head * QKV, (head + 1) * QKV)
        value = dot(own_ref[rows, :], own_act) + dot(other_ref[rows, :], other_act)
        bias = jnp.broadcast_to(bias_ref[head : head + 1, :], (8, QKV)).T
        value = value + bias[:, 0:1]
        query = (rotated(value[:HEAD]).astype(BF16).astype(F32) * 0.125).astype(BF16)
        key = rotated(value[HEAD : 2 * HEAD]).astype(BF16)
        val = value[2 * HEAD :].astype(BF16)
        for seq in range(2):
            lanes = slice(seq * TILE, (seq + 1) * TILE)
            out_ref[seq, head, 0:HEAD, :] = query[:, lanes]
            out_ref[seq, head, HEAD : 2 * HEAD, :] = key[:, lanes]
            out_ref[seq, head, 2 * HEAD : QKV, :] = val[:, lanes]
    for seq in range(2):
        out_ref[seq, CORE_HEADS:, 0:QKV, :] = jnp.zeros((SLOTS - CORE_HEADS, QKV, TILE), BF16)
        if along:
            out_ref[seq, :, QKV:, :] = along[0][seq * SLOTS : (seq + 1) * SLOTS]


def turned(weights):
    return weights, block((QKV_ROWS, HALF), lambda s: (0, 0))


def project_qkv(at, mine, theirs, own, other, bias, cosine, sine, along=None):
    left = block((TILE, D), lambda s: (0, 0))
    return run(
        qkv_kernel,
        at,
        [(mine, left), (theirs, left), turned(own), turned(other), bias, cosine, sine]
        + ([] if along is None else [along]),
        [shape((2, SLOTS, QKV if along is None else QKV + HEAD, TILE), BF16)],
        "qkv",
        4 * TILE * D * QKV_ROWS,
        3500000,
        [pltpu.VMEM((2 * TILE, D), BF16), pltpu.VMEM((D, 2 * TILE), BF16)],
        limit=24,
    )[0]


def mlp_kernel(
    at, mine_ref, theirs_ref, bias_ref, up0_ref, up1_ref, up_rest, down_own, down_rest, gate_ref, slope_ref, sum_ref, act, up, down
):
    z = at[ZH]
    act[0:TILE] = mine_ref[...]
    act[TILE:] = theirs_ref[...]
    fill_up(z, up, up0_ref, up1_ref, up_rest)
    fill_down(z, down, down_own, down_rest)
    total = jnp.zeros((2 * TILE, D), F32)
    for part in range(4):
        lanes = slice(part * HALF, (part + 1) * HALF)
        value = dot(act[...], up[:, lanes]) + bias_ref[:, lanes]
        normal = 0.5 * (1.0 + lax.erf(value * 0.7071067811865476))
        gate = (value * normal).astype(BF16)
        gate_ref[:, lanes] = gate
        slope_ref[:, lanes] = normal + value * (jnp.exp(-0.5 * value * value) * 0.3989422804014327)
        total = total + dot(gate, down[lanes, :])
    sum_ref[...] = total


def feed_forward(at, mine, theirs, bias, up, down, rest, layer, after=()):
    right = block((TILE, D), lambda s: (0, 1))
    tokens = 2 * TILE
    return run(
        mlp_kernel,
        at,
        [(mine, right), (theirs, right), bias, *up_inputs(up, rest, layer), *down_inputs(down, rest, layer)],
        [shape((tokens, CORE_FF), BF16), shape((tokens, CORE_FF), F32), shape((tokens, D), F32)],
        "mlp",
        4 * tokens * D * CORE_FF,
        8500000,
        [pltpu.VMEM((tokens, D), BF16), pltpu.VMEM((D, CORE_FF), BF16), pltpu.VMEM((CORE_FF, D), BF16)],
        limit=40,
        exps=2 * tokens * CORE_FF,
        after=after,
    )


def key_range(pair):
    first = max(-1, 2 * pair - WINDOW // TILE)
    return first, 2 * pair + 2


PAIRS_OF_TILES = sum(2 * (key_range(pair)[1] - key_range(pair)[0]) for pair in range(TILES // 2))


def allowed_mask(pair, first, last, low_row, pos_row, place):
    parts = []
    for tile in range(first, last):
        ok = place >= low_row - TILE * tile
        if tile >= 2 * pair:
            ok = ok & (place <= pos_row - TILE * tile)
        parts.append(ok)
    return jnp.concatenate(parts, axis=0)


def unturned(grads, cosine, sine):
    low, high = grads[:8], grads[8:ROT]
    return jnp.concatenate(
        [low * cosine + high * sine, high * cosine - low * sine, grads[ROT:]], axis=0
    ).astype(BF16)


def attention_kernel(at, *refs, forward, backward):
    refs = list(refs)
    take = lambda count: [refs.pop(0) for _ in range(count)]
    got_ref, halo_ref, low_ref, pos_ref = take(4)
    if backward:
        cos_ref, sin_ref = take(2)
        if not forward:
            dctx_ref, saved_ctx, saved_lse = take(3)
    if forward and not backward:
        out_ref, ctx_ref, lse_ref = take(3)
    if backward:
        packed_ref, edge_ref, tail_ref = take(3)
    key_tok, query_t = take(2)
    if forward:
        (val_t,) = take(1)
    if backward:
        val_tok, key_t, query_tok, dctx_t, dctx_tok, dkv = take(6)

    reverse = at[REVERSE]
    place = lax.broadcasted_iota(jnp.int32, (TILE, 2 * TILE), 0) ^ at[SWAPPED]

    def chip(tile):
        return jnp.where(reverse == 1, TILES - 1 - tile, tile)

    for tile in range(-1, TILES):
        here = slice(tile * TILE, (tile + 1) * TILE)
        after = slice((tile + 1) * TILE, (tile + 2) * TILE)
        if tile < 0:
            key, val = halo_ref[0:HEAD, :], halo_ref[HEAD:, :]
        else:
            source = chip(tile)
            query, key, val = (got_ref[source, part * HEAD : (part + 1) * HEAD, :] for part in range(3))
            query_t[:, here] = query
            if backward:
                query_tok[here, :] = query.T
                dctx = got_ref[source, QKV:, :] if forward else dctx_ref[source]
                dctx_t[:, here] = dctx
                dctx_tok[here, :] = dctx.T
        key_tok[after, :] = key.T
        if forward:
            val_t[:, after] = val
        if backward:
            key_t[:, after] = key
            val_tok[after, :] = val.T
    if backward:
        dkv[...] = jnp.zeros_like(dkv)
    for pair in range(TILES // 2):
        first, last = key_range(pair)
        rows = slice((first + 1) * TILE, (last + 1) * TILE)
        lanes = slice(pair * 2 * TILE, (pair + 1) * 2 * TILE)
        places = chip(2 * pair), chip(2 * pair + 1)
        scores = dot(key_tok[rows, :], query_t[:, lanes])
        ok = allowed_mask(pair, first, last, low_ref[:, lanes], pos_ref[:, lanes], place)
        scores = jnp.where(ok, scores, BLOCKED)
        if forward:
            peak = jnp.max(scores, axis=0, keepdims=True)
            probs = jnp.exp(scores - peak)
            total = jnp.sum(probs, axis=0, keepdims=True)
            inverse = 1.0 / total
            ctx = dot(val_t[:, rows], probs.astype(BF16)) * inverse
            low_ctx = ctx.astype(BF16)
            for index in range(2):
                lanes_here = slice(index * TILE, (index + 1) * TILE)
                if backward:
                    packed_ref[places[index], QKV:, :] = low_ctx[:, lanes_here]
                else:
                    out_ref[places[index]] = low_ctx[:, lanes_here]
            if backward:
                probs = probs * inverse
            else:
                ctx_ref[:, lanes] = ctx
                lse_ref[:, lanes] = peak + jnp.log(total)
        else:
            probs = jnp.exp(scores - saved_lse[:, lanes])
            ctx = saved_ctx[:, lanes]
        if backward:
            dctx = dctx_t[:, lanes]
            dprobs = dot(val_tok[rows, :], dctx)
            delta = jnp.sum(ctx * dctx.astype(F32), axis=0, keepdims=True)
            dscores = (probs * (dprobs - delta)).astype(BF16)
            dquery = dot(key_t[:, rows], dscores) * 0.125
            dquery = unturned(dquery, cos_ref[:, lanes], sin_ref[:, lanes])
            packed_ref[places[0], 0:HEAD, :] = dquery[:, :TILE]
            packed_ref[places[1], 0:HEAD, :] = dquery[:, TILE:]
            dkv[rows, 0:HEAD] += dot(dscores, query_tok[lanes, :])
            dkv[rows, HEAD:] += dot(probs.astype(BF16), dctx_tok[lanes, :])
    if backward:
        edge_ref[...] = dkv[0:TILE, :]
        tail_ref[...] = dkv[TILES * TILE :, :]
        for tile in range(TILES - 1):
            lanes = slice(tile * TILE, (tile + 1) * TILE)
            grads = dkv[(tile + 1) * TILE : (tile + 2) * TILE, :].T
            packed_ref[chip(tile), HEAD:QKV, :] = unturned(grads, cos_ref[:, lanes], sin_ref[:, lanes])
        packed_ref[chip(TILES - 1), HEAD:QKV, :] = jnp.zeros((2 * HEAD, TILE), BF16)


def attention(at, got, halo, low, pos, tables=None, dctx=None, saved=None):
    forward, backward = saved is None, tables is not None
    keys = UNIT + TILE
    inputs = [got, halo, low, pos]
    outs = []
    scratch = [pltpu.VMEM((keys, HEAD), BF16), pltpu.VMEM((HEAD, UNIT), BF16)]
    if forward:
        scratch.append(pltpu.VMEM((HEAD, keys), BF16))
        if not backward:
            outs += [shape((TILES, HEAD, TILE), BF16), shape((HEAD, UNIT), F32), shape((1, UNIT), F32)]
    if backward:
        inputs += list(tables)
        if saved is not None:
            inputs += [dctx, *saved]
        rows = QKV + HEAD if forward else QKV
        outs += [shape((TILES, rows, TILE), BF16), shape((TILE, 2 * HEAD), F32), shape((TILE, 2 * HEAD), F32)]
        scratch += [
            pltpu.VMEM((keys, HEAD), BF16),
            pltpu.VMEM((HEAD, keys), BF16),
            pltpu.VMEM((UNIT, HEAD), BF16),
            pltpu.VMEM((HEAD, UNIT), BF16),
            pltpu.VMEM((UNIT, HEAD), BF16),
            pltpu.VMEM((keys, 2 * HEAD), F32),
        ]
    products = (2 if forward else 1) + (4 if backward else 0)
    return run(
        functools.partial(attention_kernel, forward=forward, backward=backward),
        at,
        inputs,
        outs,
        "attention" + ("_forward" if forward else "") + ("_backward" if backward else ""),
        2 * products * PAIRS_OF_TILES * TILE * TILE * HEAD * 4,
        4000000,
        scratch,
        exps=PAIRS_OF_TILES * TILE * TILE,
    )


def edge_kernel(at, packed_ref, tail_ref, edge_ref, cos_ref, sin_ref, out_ref):
    grads = tail_ref[...] + jnp.where(at[FIRST_HALF] == 1, edge_ref[...], 0.0)
    out_ref[0, 0:HEAD, :] = packed_ref[0, 0:HEAD, :]
    out_ref[0, HEAD:QKV, :] = unturned(grads.T, cos_ref[...], sin_ref[...])
    if out_ref.shape[1] > QKV:
        out_ref[0, QKV:, :] = packed_ref[0, QKV:, :]


def add_edge(at, packed, tail, edge, cosine, sine):
    spec = block((1,) + packed.shape[1:], lambda s: (s[LAST_CHIP], 0, 0))
    last = block((8, TILE), lambda s: (0, TILES - 1))
    return run(
        edge_kernel,
        at,
        [(packed, spec), tail, edge, (cosine, last), (sine, last)],
        [shape(packed.shape, BF16)],
        "attention_edge",
        100000,
        300000,
        limit=8,
        aliases={1: 0},
        out_specs=[spec],
    )[0]


def out_kernel(at, got_ref, own_ref, other_ref, sum_ref, keep_ref, give_ref, weights):
    fill_out(at[ZH], weights, own_ref, other_ref)
    rows = TILE // 2
    for seq in range(2):
        ctx = got_ref[seq * SLOTS : seq * SLOTS + CORE_HEADS].reshape(HALF, TILE)
        value = dot(ctx, weights[...], TN)
        here = slice(seq * rows, (seq + 1) * rows)
        there = slice(TILE + seq * rows, TILE + (seq + 1) * rows)
        keep_ref[here, :] = value[:rows] + sum_ref[here, :]
        give_ref[here, :] = value[rows:] + sum_ref[there, :]


def ctx_of(got):
    return got, block((TILES, HEAD, TILE), lambda s: (0, got.shape[1] // HEAD - 1, 0))


def attention_out(at, got, outs, total, layer, after=()):
    return run(
        out_kernel,
        at,
        [ctx_of(got), *out_inputs(*outs, layer), total],
        [shape((TILE, D), F32), shape((TILE, D), F32)],
        "attention_out",
        4 * TILE * HALF * D,
        2700000,
        [pltpu.VMEM((HALF, D), BF16)],
        after=after,
    )


def dctx_kernel(at, mine_ref, theirs_ref, own_ref, other_ref, out_ref, weights, tok):
    fill_out(at[ZH], weights, own_ref, other_ref)
    assemble(tok, mine_ref[...], theirs_ref[...])
    value = dot(weights[...], tok[...], NT).astype(BF16)
    for seq in range(2):
        part = value[:, seq * TILE : (seq + 1) * TILE].reshape(CORE_HEADS, HEAD, TILE)
        start = seq * SLOTS
        out_ref[start : start + CORE_HEADS] = part
        out_ref[start + CORE_HEADS : start + SLOTS] = jnp.zeros((SLOTS - CORE_HEADS, HEAD, TILE), BF16)


def grad_ctx(at, mine, theirs, outs, layer):
    return run(
        dctx_kernel,
        at,
        [mine, theirs, *out_inputs(*outs, layer)],
        [shape((TILES, HEAD, TILE), BF16)],
        "grad_ctx",
        4 * TILE * HALF * D,
        1300000,
        [pltpu.VMEM((HALF, D), BF16), pltpu.VMEM((2 * TILE, D), BF16)],
    )[0]


def put_early(z, act_mine, act_theirs, gate_ref, sent_ref):
    sent_ref[0:TILE, 0:HALF] = act_mine[:, half_at(1 - z)]
    sent_ref[TILE:, 0:HALF] = act_theirs[:, half_at(1 - z)]
    lanes = pl.ds(pl.multiple_of((1 - z) * QUARTER, QUARTER), QUARTER)
    sent_ref[:, SENT_GATE:SENT_CTX] = gate_ref[:, lanes]


def mlp_back_kernel(at, *refs, early):
    refs = list(refs)
    take = lambda count: [refs.pop(0) for _ in range(count)]
    mine_ref, theirs_ref, slope_ref, up0_ref, up1_ref, up_rest, down_own, down_rest = take(8)
    if early:
        act_mine, act_theirs, gate_ref = take(3)
    dup_ref, keep_ref, give_ref, bias_ref, sent_ref, dhid, up, down = refs
    z = at[ZH]
    dhid[0:TILE] = mine_ref[...]
    dhid[TILE:] = theirs_ref[...]
    fill_up(z, up, up0_ref, up1_ref, up_rest)
    fill_down(z, down, down_own, down_rest)
    total = jnp.zeros((2 * TILE, D), F32)
    start = SENT_CTX if early else 0
    for part in range(4):
        lanes = slice(part * HALF, (part + 1) * HALF)
        value = dot(dhid[...], down[lanes, :], NT) * slope_ref[:, lanes]
        dup = value.astype(BF16)
        dup_ref[:, lanes] = dup
        sent_ref[:, start + part * HALF : start + (part + 1) * HALF] = dup
        bias_ref[part : part + 1, :] = jnp.sum(dup.astype(F32), axis=0, keepdims=True)
        total = total + dot(dup, up[:, lanes], NT)
    keep_ref[...] = total[:TILE]
    give_ref[...] = total[TILE:]
    sent_ref[:, start + CORE_FF :] = dhid[...]
    if early:
        put_early(z, act_mine, act_theirs, gate_ref, sent_ref)


def mlp_back(at, mine, theirs, slope, up, down, rest, layer, early=None):
    right = block((TILE, D), lambda s: (0, 1))
    tokens = 2 * TILE
    extra = [] if early is None else [(early[0], right), (early[1], right), early[2]]
    width = SENT_LATE + (0 if early is None else SENT_CTX)
    return run(
        functools.partial(mlp_back_kernel, early=early is not None),
        at,
        [mine, theirs, slope, *up_inputs(up, rest, layer), *down_inputs(down, rest, layer), *extra],
        [
            shape((tokens, CORE_FF), BF16),
            shape((TILE, D), F32),
            shape((TILE, D), F32),
            shape((4, HALF), F32),
            shape((tokens, width), BF16),
        ],
        "mlp_back",
        4 * tokens * D * CORE_FF,
        8500000,
        [pltpu.VMEM((tokens, D), BF16), pltpu.VMEM((D, CORE_FF), BF16), pltpu.VMEM((CORE_FF, D), BF16)],
    )


def early_kernel(at, act_mine, act_theirs, gate_ref, ctx_ref, sent_ref):
    z = at[ZH]
    put_early(z, act_mine, act_theirs, gate_ref, sent_ref)
    for seq in range(2):
        ctx = ctx_ref[pl.ds(seq * SLOTS + 3 * (1 - z), 3)].reshape(QKV, TILE)
        sent_ref[seq * TILE : (seq + 1) * TILE, SENT_CTX : SENT_CTX + QKV] = ctx.T
    sent_ref[:, SENT_CTX + QKV :] = jnp.zeros((2 * TILE, HEAD), BF16)


def pack_early(at, mine, theirs, gate, ctx):
    right = block((TILE, D), lambda s: (0, 1))
    outs = [shape((2 * TILE, SENT_EARLY), BF16)]
    return run(early_kernel, at, [(mine, right), (theirs, right), gate, ctx], outs, "pack_early", 0, 0)[0]


def put_out_grads(grads, ctx_ref, tok, z, offset, length):
    for side in range(2):
        lanes = slice(side * HALF, (side + 1) * HALF)
        value = jnp.zeros((QKV, HALF), F32)
        for seq in range(2):
            ctx = ctx_ref[seq * SLOTS + 3 * z : seq * SLOTS + 3 * z + 3].reshape(QKV, TILE)
            value = value + dot(ctx, tok[seq * TILE : (seq + 1) * TILE, lanes])
        value = value.astype(BF16)
        for index in range(2):
            start = (2 * side + index) * length + offset
            grads[start : start + OUT_PART, :] = value[index * OUT_PART : (index + 1) * OUT_PART]


def by_chunks(grads, out_ref, length):
    out_ref[...] = grads[...].reshape(16, length // 4, HALF)


def own_grads_kernel(at, act_mine, act_theirs, mine_ref, theirs_ref, gate_ref, dup_ref, *refs, with_ctx):
    refs = list(refs)
    if with_ctx:
        ctx_ref, early_ref, late_ref, out_ref, done_ref, act, dhid, grads, tok, tok_other = refs
        length, start = PART_FIRST, 0
    else:
        late_ref, out_ref, done_ref, act, dhid, grads = refs
        early_ref = late_ref
        length, start = PART_SECOND, SENT_CTX
    z = at[ZH]
    done_ref[...] = jnp.zeros_like(done_ref)
    act[0:TILE] = act_mine[:, half_at(z)]
    act[TILE:] = act_theirs[:, half_at(z)]
    dhid[0:TILE] = mine_ref[...]
    dhid[TILE:] = theirs_ref[...]
    act_t, act_other = act[...].T, early_ref[:, 0:HALF].T
    for part in range(4):
        lanes = slice(part * HALF, (part + 1) * HALF)
        other = slice(start + part * HALF, start + (part + 1) * HALF)
        value = dot(act_t, dup_ref[:, lanes]) + dot(act_other, late_ref[:, other])
        grads[part * length : part * length + HALF, :] = value.astype(BF16)
    start += CORE_FF
    gate_t = gate_ref[:, pl.ds(pl.multiple_of(z * QUARTER, QUARTER), QUARTER)].T
    gate_other = early_ref[:, SENT_GATE:SENT_CTX].T
    for side in range(2):
        lanes = slice(side * HALF, (side + 1) * HALF)
        other = slice(start + side * HALF, start + (side + 1) * HALF)
        value = (dot(gate_t, dhid[:, lanes]) + dot(gate_other, late_ref[:, other])).astype(BF16)
        for index in range(2):
            row = (2 * side + index) * length + HALF
            grads[row : row + HALF, :] = value[index * HALF : (index + 1) * HALF]
    if with_ctx:
        assemble(tok, mine_ref[...], theirs_ref[...])
        assemble(tok_other, late_ref[0:TILE, start:], late_ref[TILE:, start:])
        ctx_other = early_ref[:, SENT_CTX : SENT_CTX + QKV].T
        for side in range(2):
            lanes = slice(side * HALF, (side + 1) * HALF)
            value = dot(ctx_other, tok_other[:, lanes])
            for seq in range(2):
                ctx = ctx_ref[pl.ds(seq * SLOTS + 3 * z, 3)].reshape(QKV, TILE)
                value = value + dot(ctx, tok[seq * TILE : (seq + 1) * TILE, lanes])
            value = value.astype(BF16)
            for index in range(2):
                row = (2 * side + index) * length + 2 * HALF
                grads[row : row + OUT_PART, :] = value[index * OUT_PART : (index + 1) * OUT_PART]
                grads[row + OUT_PART : row + OUT_PART + 32, :] = jnp.zeros((32, HALF), BF16)
    by_chunks(grads, out_ref, length)


def own_grads(at, mine, theirs, dmine, dtheirs, gate, dup, late, early=None, ctx=None):
    right = block((TILE, D), lambda s: (0, 1))
    tokens = 2 * TILE
    length = PART_SECOND if ctx is None else PART_FIRST
    inputs = [(mine, right), (theirs, right), dmine, dtheirs, gate, dup]
    inputs += [late] if ctx is None else [ctx, early, late]
    scratch = [pltpu.VMEM((tokens, HALF), BF16), pltpu.VMEM((tokens, D), BF16), pltpu.VMEM((4 * length, HALF), BF16)]
    if ctx is not None:
        scratch += [pltpu.VMEM((tokens, D), BF16)] * 2
    return run(
        functools.partial(own_grads_kernel, with_ctx=ctx is not None),
        at,
        inputs,
        [shape((16, length // 4, HALF), BF16), shape((8, 128), F32)],
        "own_grads",
        4 * tokens * 4 * length * HALF,
        8000000,
        scratch,
        token=True,
    )[0]


def grads_qkv_kernel(
    at, got_ref, mine_ref, theirs_ref, dmine_ref, dtheirs_ref, ctx_ref, out_ref, done_ref, act, tok, grads
):
    done_ref[...] = jnp.zeros_like(done_ref)
    assemble(act, mine_ref[...], theirs_ref[...])
    assemble(tok, dmine_ref[...], dtheirs_ref[...])
    for z in range(2):
        put_out_grads(grads, ctx_ref, tok, z, QKV_PART, PART_QKV)
        lanes = slice(z * HALF, (z + 1) * HALF)
        value = jnp.zeros((QKV_ROWS, HALF), F32)
        for seq in range(2):
            rows = got_ref[seq * SLOTS : seq * SLOTS + CORE_HEADS, 0:QKV, :].reshape(QKV_ROWS, TILE)
            value = value + dot(rows, act[seq * TILE : (seq + 1) * TILE, lanes])
        value = value.astype(BF16)
        for part in range(4):
            start = part * PART_QKV
            grads[start : start + QKV_PART, :] = value[part * QKV_PART : (part + 1) * QKV_PART]
        out_ref[:, z] = grads[...].reshape(16, CHUNK_QKV, HALF)


def grads_qkv(at, got, mine, theirs, dmine, dtheirs):
    left = block((TILE, D), lambda s: (0, 0))
    return run(
        grads_qkv_kernel,
        at,
        [got, (mine, left), (theirs, left), dmine, dtheirs, ctx_of(got)],
        [shape((16, 2, CHUNK_QKV, HALF), BF16), shape((8, 128), F32)],
        "grads_qkv",
        4 * TILE * D * 4 * PART_QKV,
        3800000,
        [pltpu.VMEM((2 * TILE, D), BF16)] * 2 + [pltpu.VMEM((4 * PART_QKV, HALF), BF16)],
        token=True,
    )[0]


def qkv_back_kernel(at, got_ref, own_ref, other_ref, keep_ref, give_ref, bias_ref):
    z = at[ZH]
    rows = TILE // 2
    sums = jnp.zeros((8, QKV_ROWS), F32)
    for seq in range(2):
        tok = got_ref[seq * SLOTS : seq * SLOTS + CORE_HEADS, 0:QKV, :].reshape(QKV_ROWS, TILE).T
        sums = sums + dot(jnp.ones((8, TILE), BF16), tok)
        here = slice(seq * rows, (seq + 1) * rows)
        for weights, at_z in ((own_ref, z), (other_ref, 1 - z)):
            value = dot(tok, weights[...])
            keep_ref[here, half_at(at_z)] = value[:rows]
            give_ref[here, half_at(at_z)] = value[rows:]
    bias_ref[...] = sums


def qkv_back(at, got, own, other):
    return run(
        qkv_back_kernel,
        at,
        [got, turned(own), turned(other)],
        [shape((TILE, D), F32), shape((TILE, D), F32), shape((8, QKV_ROWS), F32)],
        "qkv_back",
        4 * TILE * D * QKV_ROWS,
        3500000,
        limit=24,
    )


def qkv_rows(got_ref, tok, out_ref):
    for z in range(2):
        lanes = slice(z * HALF, (z + 1) * HALF)
        value = jnp.zeros((QKV_ROWS, HALF), F32)
        for seq in range(2):
            grads = got_ref[seq * SLOTS : seq * SLOTS + CORE_HEADS].reshape(QKV_ROWS, TILE)
            value = value + dot(grads, tok[seq * TILE : (seq + 1) * TILE, lanes])
        out_ref[z, 0:QKV_ROWS, :] = value.astype(BF16)


def qkv_grads_first_kernel(at, got_ref, mine_ref, theirs_ref, *refs):
    sums, (out_ref, tok, small) = refs[:6], refs[6:]
    assemble(tok, mine_ref[...], theirs_ref[...])
    qkv_rows(got_ref, tok, out_ref)

    def by_core(core):
        for z in range(2):
            small[...] = jnp.zeros((4 * SMALL, HALF), F32)
            for layer in range(LAYERS):
                norm_ref, up_ref, qkv_ref = sums[3 * layer : 3 * layer + 3]
                start = layer * SMALL
                for index in range(5):
                    small[start + index : start + index + 1] = norm_ref[2 * index + z : 2 * index + z + 1]
                for index in range(3):
                    part, half = (3 * z + index) // 2, (3 * z + index) % 2
                    for head in range(3):
                        lane = core * QKV + head * HEAD
                        source = (3 * half + head) * QKV + part * HEAD
                        small[start + 5 + index : start + 6 + index, lane : lane + HEAD] = qkv_ref[
                            0:1, source : source + HEAD
                        ]
                for side in range(2):
                    row = start + 8 + 2 * core + side
                    small[row : row + 1] = up_ref[2 * z + side : 2 * z + side + 1]
            out_ref[z, QKV_ROWS : QKV_ROWS + 4 * SMALL, :] = small[...].astype(BF16)
            used = QKV_ROWS + 4 * SMALL
            out_ref[z, used:, :] = jnp.zeros((QKV_FIRST - used, HALF), BF16)

    for core in range(2):
        pl.when(at[CORE] == core)(functools.partial(by_core, core))


def qkv_grads_first(at, got, mine, theirs, sums, after):
    left = block((TILE, D), lambda s: (0, 0))
    return run(
        qkv_grads_first_kernel,
        at,
        [got, (mine, left), (theirs, left), *sums],
        [shape((2, QKV_FIRST, HALF), BF16)],
        "qkv_grads_first",
        4 * TILE * D * QKV_ROWS,
        3300000,
        [pltpu.VMEM((2 * TILE, D), BF16), pltpu.VMEM((4 * SMALL, HALF), F32)],
        after=after,
    )[0]


def norm_back_kernel(
    at, keep0, got0, keep1, got1, hat_ref, inverse_ref, gain_ref, dstream_ref, next_ref, low_ref, sums_ref
):
    first, second = keep0[...] + got0[...], keep1[...] + got1[...]
    hat = hat_ref[...]
    dstream = dstream_ref[...].astype(F32)
    dhat = first * gain_ref[0:1] + second * gain_ref[1:2]
    grad = inverse_ref[...] * (
        dhat
        - jnp.mean(dhat, axis=-1, keepdims=True)
        - hat * jnp.mean(dhat * hat, axis=-1, keepdims=True)
    )
    total = dstream + grad
    next_ref[...] = total
    low_ref[...] = total.astype(BF16)
    rows = (first * hat, second * hat, first, second, dstream.astype(BF16).astype(F32))
    for index, value in enumerate(rows):
        row = jnp.sum(value, axis=0, keepdims=True)
        sums_ref[2 * index : 2 * index + 1, :] = row[:, :HALF]
        sums_ref[2 * index + 1 : 2 * index + 2, :] = row[:, HALF:]


def norm_back(at, first, second, hat, inverse, gain, dstream):
    return run(
        norm_back_kernel,
        at,
        [*first, *second, hat, inverse, gain, dstream],
        [shape((TILE, D), F32), shape((TILE, D), BF16), shape((10, HALF), F32)],
        "norm_back",
        2000000,
        3400000,
        limit=24,
    )


def rows_of(part, start, count, chunk, length, offset=0):
    at = start
    while at < start + count:
        step = min(chunk - at % chunk, start + count - at)
        yield (4 * part + at // chunk) * length + offset + at % chunk, at - start, step
        at += step


def place_mlp(source, core, up_ref, down_ref, chunk, length, offset=0):
    for part in range(4):
        z, side = part // 2, part % 2
        column = z * CORE_FF + core * QUARTER + side * HALF
        for source_row, row, count in rows_of(part, 0, HALF, chunk, length, offset):
            up_ref[0, row : row + count, column : column + HALF] = source[source_row : source_row + count, :].astype(F32)
        side, index = part // 2, part % 2
        lanes = slice(side * HALF, (side + 1) * HALF)
        first = core * QUARTER + index * HALF
        for source_row, row, count in rows_of(part, HALF, HALF, chunk, length, offset):
            row += first
            down_ref[0, row : row + count, lanes] = source[source_row : source_row + count, :].astype(F32)


def for_cores(at, mine, theirs, put):
    for here, source in ((True, mine), (False, theirs)):
        for core in range(2):
            pl.when((at[CORE] == core) == here)(functools.partial(put, core, source))


UP_SHAPE, DOWN_SHAPE, OUT_SHAPE = (LAYERS, HALF, FF), (LAYERS, FF // 2, D), (LAYERS, HALF, D)
QKV_SHAPE = (LAYERS, HALF, 3 * D)
PLACED = (UP_SHAPE, DOWN_SHAPE, OUT_SHAPE)


def place_out(source, core, out_ref, first, chunk, length, offset):
    for part in range(4):
        lanes = slice((part // 2) * HALF, (part // 2 + 1) * HALF)
        start = core * QKV + (part % 2) * OUT_PART
        for source_row, row, count in rows_of(part, first, OUT_PART, chunk, length, offset):
            row += start
            out_ref[0, row : row + count, lanes] = source[source_row : source_row + count, :].astype(F32)


def place_turned(rows_ref, out_ref, part, z):
    column = part * D + z * HALF
    out_ref[0, :, column : column + HALF] = rows_ref[...].T


LENGTH = CHUNK_FIRST + CHUNK_QKV + CHUNK_SECOND


def place_part(source, layer, z, up_ref, down_ref, out_ref):
    if layer == 0:
        main = CHUNK_FIRST, LENGTH, 0
        outs = 2 * HALF, CHUNK_FIRST, LENGTH, 0
    else:
        main = CHUNK_SECOND, LENGTH, CHUNK_FIRST + CHUNK_QKV
        outs = QKV_PART, CHUNK_QKV, LENGTH, CHUNK_FIRST
    half = slice(z * HALF, (z + 1) * HALF)
    for index in range(2):
        part = 2 * z + index
        lanes = slice(index * HALF, (index + 1) * HALF)
        for start, row, count in rows_of(part, 0, HALF, *main):
            up_ref[0, row : row + count, lanes] = source[start : start + count, :].astype(F32)
        for start, row, count in rows_of(part, HALF, HALF, *main):
            row += index * HALF
            down_ref[0, row : row + count, half] = source[start : start + count, :].astype(F32)
        for start, row, count in rows_of(part, outs[0], OUT_PART, *outs[1:]):
            row += index * OUT_PART
            out_ref[0, row : row + count, half] = source[start : start + count, :].astype(F32)


def place_long_kernel(at, *refs, mine):
    if mine:
        source, _, up_ref, down_ref, out_ref = refs
    else:
        mine_ref, source, _, _, _, _, _, up_ref, down_ref, out_ref, qkv_ref, rows_ref = refs
    for layer in range(LAYERS):
        for z in range(2):
            here = (pl.program_id(0) == layer) & (pl.program_id(1) == z)
            pl.when(here)(functools.partial(place_part, source, layer, z, up_ref, down_ref, out_ref))
    if mine:
        return

    @pl.when((pl.program_id(0) == 0) & (pl.program_id(1) == 0))
    def _():
        for part in range(3):
            for z in range(2):

                def put_rows(core, source):
                    for head in range(3):
                        row = (z * 3 + head) * QKV + part * HEAD
                        to = core * QKV + head * HEAD
                        for start in range(row, row + HEAD, 32):
                            pieces = rows_of(start // QKV_PART, start % QKV_PART, 32, CHUNK_QKV, LENGTH, CHUNK_FIRST)
                            for source_row, more, count in pieces:
                                here = to + start - row + more
                                rows_ref[here : here + count, :] = source[source_row : source_row + count, :].astype(F32)

                for_cores(at, mine_ref, source, put_rows)
                place_turned(rows_ref, qkv_ref, part, z)


def place_long(at, sources, filled):
    mine = len(sources) == 1
    anywhere = pl.BlockSpec(memory_space=pl.ANY)
    once = pl.BlockSpec(sources[0].shape, lambda i, z, s: (0, 0), pipeline_mode=pl.Buffered(1))
    core = (lambda s: s[CORE]) if mine else (lambda s: 1 - s[CORE])
    specs = [
        pl.BlockSpec((1, HALF, QUARTER), lambda i, z, s: (i, 0, 2 * z + core(s))),
        pl.BlockSpec((1, QUARTER, D), lambda i, z, s: (i, core(s), 0)),
        pl.BlockSpec((1, QKV, D), lambda i, z, s: (i, core(s), 0)),
    ]
    outs = list(PLACED)
    scratch = []
    if not mine:
        specs.append(pl.BlockSpec((1,) + QKV_SHAPE[1:], lambda i, z, s: (1, 0, 0)))
        outs.append(QKV_SHAPE)
        scratch.append(pltpu.VMEM((HALF, HALF), F32))
    count = len(sources)
    return pl.pallas_call(
        functools.partial(place_long_kernel, mine=mine),
        grid_spec=pltpu.PrefetchScalarGridSpec(
            num_scalar_prefetch=1,
            grid=(LAYERS, 2),
            in_specs=[once] * count + [anywhere] * (len(filled) + 1),
            out_specs=specs,
            scratch_shapes=scratch,
        ),
        out_shape=[shape(dims, F32) for dims in outs],
        input_output_aliases={1 + count + index: index for index in range(len(filled))},
        compiler_params=pltpu.CompilerParams(vmem_limit_bytes=60 * 1024 * 1024),
        cost_estimate=pl.CostEstimate(flops=1, bytes_accessed=1, transcendentals=0),
        name="place_mine" if mine else "place_theirs",
    )(at, *sources, *filled, *LATEST)


def place_qkv_kernel(
    at, mine_ref, theirs_ref, out_ref, gain_ref, offset_ref, hidden_ref, again_ref, qkv_ref, up_ref, rows_ref
):
    for part in range(3):
        for z in range(2):

            def put(core, source):
                for head in range(3):
                    row = (z * 3 + head) * QKV + part * HEAD
                    to = core * QKV + head * HEAD
                    rows_ref[to : to + HEAD, :] = source[row : row + HEAD, :].astype(F32)

            for_cores(at, mine_ref, theirs_ref, put)
            place_turned(rows_ref, out_ref, part, z)
    rows = slice(QKV_ROWS, QKV_ROWS + 2 * SMALL + 8)
    small = mine_ref[rows, :].astype(F32) + theirs_ref[rows, :].astype(F32)
    for layer in range(LAYERS):
        start = layer * SMALL
        gain_ref[layer] = small[start : start + 2]
        offset_ref[layer] = small[start + 2 : start + 4]
        hidden_ref[layer : layer + 1] = small[start + 4 : start + 5]
        again_ref[layer : layer + 1] = small[start + 4 : start + 5]
        for index in range(3):
            lanes = slice(index * HALF, (index + 1) * HALF)
            qkv_ref[layer : layer + 1, lanes] = small[start + 5 + index : start + 6 + index]
        for index in range(4):
            lanes = slice(index * HALF, (index + 1) * HALF)
            up_ref[layer : layer + 1, lanes] = small[start + 8 + index : start + 9 + index]


def place_qkv(at, mine, theirs):
    outs = [shape((LAYERS, HALF, 3 * D), F32)]
    specs = [block((1, HALF, 3 * D), lambda s: (0, 0, 0))]
    for dims in ((2, HALF), (2, HALF), (HALF,), (HALF,), (3 * HALF,), (4 * HALF,)):
        outs.append(shape((LAYERS,) + dims, F32))
        specs.append(block((LAYERS,) + dims))
    return run(
        place_qkv_kernel,
        at,
        [mine, theirs],
        outs,
        "place_qkv",
        0,
        6000000,
        [pltpu.VMEM((HALF, HALF), F32)],
        limit=40,
        out_specs=specs,
    )


ROW_GAIN, ROW_OFFSET, ROW_QKV, ROW_OUT, ROW_UP, ROW_DOWN, SMALL_ROWS = 0, 4, 8, 14, 16, 24, 32


def gather_small(refs):
    gain, offset, qkv, out, up, down = (ref[...].astype(F32) for ref in refs)
    rows = [gain.reshape(4, HALF), offset.reshape(4, HALF)]
    rows += [qkv[layer : layer + 1, part * HALF : (part + 1) * HALF] for layer in range(LAYERS) for part in range(3)]
    rows.append(out)
    rows += [up[layer : layer + 1, part * HALF : (part + 1) * HALF] for layer in range(LAYERS) for part in range(4)]
    rows += [down, jnp.zeros((SMALL_ROWS - ROW_DOWN - LAYERS, HALF), F32)]
    return jnp.concatenate(rows, axis=0)


def spread_small_kernel(at, own_ref, other_ref, *outs):
    own, other = own_ref[...].astype(F32), other_ref[...].astype(F32)
    swap = at[ZH] == 1
    halves = jnp.where(swap, other, own), jnp.where(swap, own, other)

    def row(index, z):
        return halves[z][index : index + 1]

    def by_core(core):
        for layer in range(LAYERS):
            qkv_ref, up_ref = outs[5 * layer + 2], outs[5 * layer + 4]
            for part in range(3):
                for z in range(2):
                    place = part * 2 + z
                    values = row(ROW_QKV + layer * 3 + place % 3, place // 3)
                    for head in range(3):
                        lane = core * QKV + head * HEAD
                        qkv_ref[3 * z + head : 3 * z + head + 1, part * HEAD : (part + 1) * HEAD] = values[
                            :, lane : lane + HEAD
                        ]
            for z in range(2):
                for side in range(2):
                    lane = z * QUARTER + side * HALF
                    up_ref[:, lane : lane + HALF] = row(ROW_UP + 4 * layer + 2 * core + side, z)

    for core in range(2):
        pl.when(at[CORE] == core)(functools.partial(by_core, core))
    for layer in range(LAYERS):
        gain_ref, offset_ref, _, rest_ref, _ = outs[5 * layer : 5 * layer + 5]
        for z in range(2):
            lanes = slice(z * HALF, (z + 1) * HALF)
            for index in range(2):
                gain_ref[index : index + 1, lanes] = row(ROW_GAIN + 2 * layer + index, z)
                offset_ref[index : index + 1, lanes] = row(ROW_OFFSET + 2 * layer + index, z)
            rest_ref[:, lanes] = row(ROW_OUT + layer, z) + row(ROW_DOWN + layer, z)


def spread_small(at, rows, other):
    outs = [shape((2, D), F32), shape((2, D), F32), shape((8, QKV), F32), shape((1, D), F32), shape((1, CORE_FF), F32)]
    spec = block((SMALL_ROWS, HALF), lambda s: (QKV_ROWS // SMALL_ROWS, 0))
    values = run(spread_small_kernel, at, [(rows, spec), (other, spec)], outs * LAYERS, "small_spread", 0, 0)
    return zip(values[:5], values[5:])


EVERY = ("zh", "xh", "xl", "y", "zl")
ACROSS = ("xh", "xl", "y")
CHIPS = ("xl", "zl", "y")


def exchange(values):
    return lax.ppermute(values, "core", SWAP)


def scatter_sum(grads):
    parts = grads.reshape(64, -1, HALF)
    parts = lax.all_to_all(parts, EVERY, 0, 0, tiled=True)
    return jnp.sum(parts.astype(F32), axis=0).astype(BF16)


def add_from(part, other):
    return (part.astype(F32) + other.astype(F32)).astype(BF16)


def ring(values, axis, by):
    return lax.ppermute(values, axis, [(place, (place + by) % 4) for place in range(4)])


X_RING, Y_RING = ("xh", "xl"), "y"


def around(pieces, first, second):
    return [
        (ring(piece, first if index < 4 else second, index % 4) if index % 4 else piece)
        for index, piece in enumerate(pieces)
    ]


def sum_x(grads):
    return lax.psum_scatter(grads.reshape(-1, HALF), X_RING, scatter_dimension=0, tiled=True)


def sum_y(part):
    return lax.psum_scatter(part, Y_RING, scatter_dimension=0, tiled=True)


def sum_grid(grads):
    parts = lax.all_to_all(grads, ACROSS, 0, 0, tiled=True)
    return jnp.sum(parts.astype(F32), axis=0).astype(BF16)


def sum_near(part):
    return add_from(part, lax.ppermute(part, "zl", SWAP))


def sum_depth(zh, part):
    part = part.reshape(2, -1, HALF)
    keep = jnp.where(zh == 0, part[0], part[1])
    give = jnp.where(zh == 0, part[1], part[0])
    near = lax.ppermute(keep, "zl", SWAP)
    far = lax.ppermute(give, "zh", SWAP)
    across = lax.ppermute(give, ("zl", "zh"), [(0, 3), (3, 0), (1, 2), (2, 1)])
    total = (keep.astype(F32) + near.astype(F32)) + (far.astype(F32) + across.astype(F32))
    return total.astype(BF16)


def gather_short(part):
    copies = jnp.broadcast_to(part[None], (32,) + part.shape)
    return lax.all_to_all(copies, EVERY[1:], 0, 0, tiled=True).reshape(-1, HALF)


def token_places(offsets, lengths):
    ends = jnp.cumsum(lengths)
    before = ends[:, None] <= offsets[None, :]
    start = jnp.max(jnp.where(before, ends[:, None], 0), axis=0)
    return start, offsets >= ends[DOCS - 2]


def rotary(places):
    frequency = 1.0 / 10000.0 ** (jnp.arange(0, ROT, 2).astype(F32) / ROT)
    angles = frequency[:, None] * places.astype(F32)[None, :]
    return jnp.cos(angles), jnp.sin(angles)


def local(
    hidden_in,
    doc_lengths,
    norm_gain,
    norm_bias,
    qkv_weight,
    qkv_bias,
    out_weight,
    out_bias,
    up_weight,
    up_bias,
    down_weight,
    down_bias,
    cotangent,
):
    LATEST.clear()
    zh, core, xh, xl, zl, y = (lax.axis_index(name) for name in ("zh", "core", "xh", "xl", "zl", "y"))
    chip = (xl * 2 + zl) * 4 + y
    x = xh * 2 + xl
    lengths = doc_lengths[0]

    unit_seq = xl
    unit_half = jnp.where(unit_seq == 0, xh, 1 - xh)
    unit_swap = jnp.where(unit_seq == core, 0, TILE // 2)
    last_chip = jnp.where(unit_seq == 0, TILES - 1, 0)
    at = jnp.stack(
        [core, zh, unit_seq, unit_swap, 1 - unit_half, last_chip, x, y, x * 4 + y]
    ).astype(jnp.int32)

    lane = jnp.arange(TILE, dtype=jnp.int32)
    seq0_tile = xh * TILES + chip
    places = []
    for seq, tile in ((0, seq0_tile), (1, 2 * TILES - 1 - seq0_tile)):
        offsets = tile * TILE + (lane ^ jnp.where(seq == core, 0, TILE // 2))
        places.append(offsets - token_places(offsets, lengths[seq])[0])
    own_tables = rotary(jnp.concatenate(places))
    unit_lengths = lax.dynamic_index_in_dim(lengths, unit_seq, 0, keepdims=False)
    relative = (jnp.arange(TILES, dtype=jnp.int32)[:, None] * TILE + (lane ^ unit_swap)[None, :]).reshape(-1)
    offsets = unit_half * UNIT + relative
    start, padding = token_places(offsets, unit_lengths)
    unit_tables = rotary(offsets - start)
    low = jnp.where(padding, offsets, jnp.maximum(start, offsets - (WINDOW - 1)))
    low = (low - unit_half * UNIT).reshape(1, UNIT)
    pos = relative.reshape(1, UNIT)

    def to_units(values):
        return lax.all_to_all(values.reshape(TILES, -1, TILE), CHIPS, 0, 0, tiled=True)

    def halo_of(got):
        last = lax.dynamic_index_in_dim(got, last_chip, 0, keepdims=False)
        return lax.ppermute(last[HEAD:QKV], "xh", SWAP)

    def finish_attention(packed, edge, tail):
        edge = lax.ppermute(edge, "xh", SWAP)
        return to_units(add_edge(at, packed, tail, edge, *unit_tables))

    small = (norm_gain, norm_bias, qkv_bias, out_bias, up_bias, down_bias)

    def gather_chunks(chunk):
        return lax.all_gather(chunk, ACROSS, axis=0, tiled=True).reshape(16, CHUNK, HALF)

    weights = begin(at, qkv_weight, up_weight, down_weight, small)
    own_qkv, other_qkv = [weights], [lax.ppermute(weights, "zh", SWAP)]
    rest = [gather_chunks(other_qkv[0][CHUNK_AT:])]
    tokens = cotangent[0]
    dhid1 = (tokens, exchange(tokens))
    gain, offset, b_qkv, b_rest, b_up = spread_small(at, weights, other_qkv[0])
    _, hat0, inverse0, act = norms(at, hidden_in[0], None, gain[0], offset[0])
    acts0 = (act, exchange(act))
    got0 = to_units(project_qkv(at, *acts0, own_qkv[0], other_qkv[0], b_qkv[0], *own_tables))
    rows, weights = begin_rest(at, qkv_weight, up_weight, down_weight, out_weight)
    rows, weights = held(at, [rows, weights], (got0,))
    rows = lax.ppermute(rows, "zh", SWAP)
    own_qkv.append(weights)
    other_qkv.append(lax.ppermute(weights, "zh", SWAP))
    outs = (out_weight, rows)
    halo0 = halo_of(got0)
    ctx0, *saved0 = attention(at, got0, halo0, low, pos)
    rest.append(gather_chunks(held(at, [rows[REST_CHUNK:]])[0]))
    ctx0 = to_units(ctx0)
    gate0, slope0, total = feed_forward(at, *acts0, b_up[0], up_weight, down_weight, rest, 0)
    dctx1 = grad_ctx(at, *dhid1, outs, 1)
    keep, give = attention_out(at, ctx0, outs, total, 0)
    added = (keep, exchange(give), b_rest[0])

    stream, hat1, inverse1, act = norms(at, hidden_in[0], added, gain[1], offset[1])
    acts1 = (act, exchange(act))
    got1 = to_units(project_qkv(at, *acts1, own_qkv[1], other_qkv[1], b_qkv[1], *own_tables, dctx1))
    gate1, slope1, mlp1 = feed_forward(at, *acts1, b_up[1], up_weight, down_weight, rest, 1)
    dup1, keep, give, sum_up1, sent = mlp_back(
        at, *dhid1, slope1, up_weight, down_weight, rest, 1, (*acts1, gate1)
    )
    second1 = (keep, exchange(give))
    late1 = lax.ppermute(held(at, [sent], (got1,))[0], "zh", SWAP)
    halo1 = halo_of(got1)
    packed = attention(at, got1, halo1, low, pos, unit_tables)
    dqkv1 = finish_attention(*packed)
    grads1 = own_grads(at, *acts1, *dhid1, gate1, dup1, late1)
    part1 = sum_x(held(at, [grads1], (dqkv1,))[0])
    keep, give, sum_qkv1 = qkv_back(at, dqkv1, own_qkv[1], other_qkv[1])
    first1 = (keep, exchange(give))
    early0 = lax.ppermute(pack_early(at, *acts0, gate0, ctx0), "zh", SWAP)
    dstream, low_stream, sum_norm1 = norm_back(at, first1, second1, hat1, inverse1, gain[1], tokens)

    dhid0 = (low_stream, exchange(low_stream))
    dctx0 = to_units(grad_ctx(at, *dhid0, outs, 0))
    dup0, keep, give, sum_up0, sent = mlp_back(at, *dhid0, slope0, up_weight, down_weight, rest, 0)
    second0 = (keep, exchange(give))
    gradsq = grads_qkv(at, dqkv1, *acts1, *dhid1)
    gradsq, sent, part1 = held(at, [gradsq, sent, part1], (dctx0, early0))
    late0 = lax.ppermute(sent, "zh", SWAP)
    part1 = sum_y(part1)
    partq = sum_x(gradsq)
    packed = attention(at, got0, halo0, low, pos, unit_tables, dctx0, saved0)
    dqkv0 = finish_attention(*packed)
    grads0 = own_grads(at, *acts0, *dhid0, gate0, dup0, late0, early0, ctx0)
    part0 = sum_grid(held(at, [grads0], (dqkv0,))[0])
    keep, give, sum_qkv0 = qkv_back(at, dqkv0, own_qkv[0], other_qkv[0])
    first0 = (keep, exchange(give))
    dstream, _, sum_norm0 = norm_back(at, first0, second0, hat0, inverse0, gain[0], dstream)
    hidden_grad = dstream[None]
    partq, part1 = held(at, [partq, part1])
    partq = sum_y(partq)

    sums = (sum_norm0, sum_up0, sum_qkv0, sum_norm1, sum_up1, sum_qkv1)
    part_qkv = scatter_sum(qkv_grads_first(at, dqkv0, *acts0, sums, (part0,)))
    part0, partq, near1 = held(at, [part0, partq, sum_near(part1)])
    total = [sum_near(part0), sum_depth(zh, partq), near1]
    (total,) = held(at, [jnp.concatenate(total)])
    long = lax.all_gather(total, ACROSS, axis=0, tiled=True)
    keep, give = attention_out(at, dqkv1, outs, mlp1, 1, (part_qkv,))
    given = exchange(give)
    hidden_out = (stream + (keep + given + b_rest[1])).astype(BF16)[None]
    qkv0 = gather_short(part_qkv)
    g_qkv, g_gain, g_offset, g_hidden, g_again, g_bqkv, g_bup = place_qkv(at, qkv0, exchange(qkv0))
    (long,) = held(at, [long], (given,))
    filled = place_long(at, (long,), ())
    g_up, g_down, g_out, g_qkv = place_long(at, (long, exchange(long)), (*filled, g_qkv))
    return (
        hidden_out,
        hidden_grad,
        g_gain,
        g_offset,
        g_qkv,
        g_bqkv,
        g_out,
        g_hidden,
        g_up,
        g_bup,
        g_down,
        g_again,
    )


def solution(mesh):
    fine = Mesh(
        mesh.devices.reshape(2, 2, 2, 4, 2, 2), ("xh", "xl", "zl", "y", "core", "zh")
    )
    ctx = ("xh", "xl", "zl", "y", "core")
    rows = P(None, "zh", None)
    tokens = P("zh", ctx, None)
    last = P(None, None, "zh")
    bias = P(None, "zh")
    return jax.shard_map(
        local,
        mesh=fine,
        in_specs=(tokens, P("zh", None, None), last, last, rows, bias, rows, bias, rows, bias, rows, bias, tokens),
        out_specs=(tokens, tokens, last, last, rows, bias, rows, bias, rows, bias, rows, bias),
        check_vma=False,
    )
```

```python
import functools

import jax
import jax.numpy as jnp
from jax import lax
from jax.experimental import pallas as pl
from jax.experimental.pallas import tpu as pltpu
from jax.sharding import Mesh
from jax.sharding import PartitionSpec as P

D = 768
HALF = D // 2
HEADS = 12
HEAD = 64
FF = 3072
ROT = 16
LAYERS = 2
WINDOW = 1024
DOCS = 8
TILE = 128
TILES = 16
UNIT = TILE * TILES
SLOTS = 8
CORE_HEADS = HEADS // 2
QKV = 3 * HEAD
QKV_ROWS = CORE_HEADS * QKV
CORE_FF = FF // 2
QUARTER = FF // 4

CHUNK_UP = 96
CHUNK_DOWN = 48
CHUNK = CHUNK_UP + 2 * CHUNK_DOWN
QKV_PART = QKV_ROWS // 4
OUT_PART = QKV // 2
PART_SECOND = 2 * HALF
PART_FIRST = 2 * HALF + OUT_PART + 32
PART_QKV = QKV_PART + OUT_PART
CHUNK_SECOND, CHUNK_FIRST, CHUNK_QKV = PART_SECOND // 4, PART_FIRST // 4, PART_QKV // 4
SENT_GATE, SENT_CTX = HALF, HALF + QUARTER
SENT_EARLY = SENT_CTX + QKV + HEAD
SENT_LATE = CORE_FF + D
QKV_FIRST = 32 * 40
SMALL = 12

BLOCKED = -1e30
EPSILON = 1e-05
SWAP = [(0, 1), (1, 0)]
F32 = jnp.float32
BF16 = jnp.bfloat16

NN = (((1,), (0,)), ((), ()))
NT = (((1,), (1,)), ((), ()))
TN = (((0,), (0,)), ((), ()))


def dot(left, right, dims=NN):
    return lax.dot_general(left, right, dims, preferred_element_type=F32)


def shape(dims, kind):
    return jax.ShapeDtypeStruct(dims, kind)


def block(dims, *at):
    place = at[0] if at else (lambda s: (0,) * len(dims))
    return pl.BlockSpec(dims, lambda i, s: place(s))


def whole(array):
    return block(array.shape)


LATEST = []


def run(
    kernel, scalars, inputs, outs, name, flops, moved, scratch=(), limit=40, aliases=None, exps=0, out_specs=None, after=(), token=False
):
    after = list(after) + LATEST
    arrays = [item[0] if isinstance(item, tuple) else item for item in inputs] + after
    specs = [item[1] if isinstance(item, tuple) else whole(item) for item in inputs]
    specs += [pl.BlockSpec(memory_space=pl.ANY)] * len(after)
    if out_specs is None:
        out_specs = [block(out.shape) for out in outs]
    count = len(inputs)

    def body(at, *refs):
        kernel(at, *refs[:count], *refs[count + len(after) :])

    results = pl.pallas_call(
        body,
        grid_spec=pltpu.PrefetchScalarGridSpec(
            num_scalar_prefetch=1,
            grid=(1,),
            in_specs=specs,
            out_specs=out_specs,
            scratch_shapes=list(scratch),
        ),
        out_shape=outs,
        input_output_aliases=aliases or {},
        compiler_params=pltpu.CompilerParams(vmem_limit_bytes=60 * 1024 * 1024),
        cost_estimate=pl.CostEstimate(flops=1, bytes_accessed=1, transcendentals=0),
        name=name,
    )(scalars, *arrays)
    LATEST[:] = [results[-1] if token else min(results, key=lambda result: result.size)]
    return results


def held(at, values, after=()):
    anywhere = pl.BlockSpec(memory_space=pl.ANY)

    def kernel(at, *refs):
        refs[-1][0] = 0

    outs = [shape(value.shape, value.dtype) for value in values] + [shape((1,), jnp.int32)]
    specs = [anywhere] * len(values) + [pl.BlockSpec(memory_space=pltpu.SMEM)]
    aliases = {1 + index: index for index in range(len(values))}
    inputs = [(value, anywhere) for value in values]
    return run(kernel, at, inputs, outs, "held", 0, 0, aliases=aliases, out_specs=specs, after=after, token=True)[:-1]


CORE, ZH, REVERSE, SWAPPED, FIRST_HALF, LAST_CHIP, RING_X, RING_Y, SPOT = range(9)


def half_at(index):
    return pl.ds(pl.multiple_of(index * HALF, HALF), HALF)


def turn(at, raw_ref, out_ref):
    def by_core(core):
        for part in range(3):
            for z in range(2):
                start = part * D + z * HALF + core * QKV
                piece = raw_ref[0, :, start : start + QKV].T
                for head in range(3):
                    row = (z * 3 + head) * QKV + part * HEAD
                    out_ref[row : row + HEAD, :] = piece[head * HEAD : (head + 1) * HEAD]

    for core in range(2):
        pl.when(at[CORE] == core)(functools.partial(by_core, core))


def put_chunk(up_ref, down_ref, out_ref):
    out_ref[0:CHUNK_UP] = up_ref[0]
    out_ref[CHUNK_UP : CHUNK_UP + CHUNK_DOWN] = down_ref[0, :, :HALF]
    out_ref[CHUNK_UP + CHUNK_DOWN :] = down_ref[0, :, HALF:]


SMALL_AT, CHUNK_AT = QKV_ROWS, QKV_ROWS + 32


def begin_kernel(at, qkv_ref, up_ref, down_ref, *refs):
    small, out_ref = refs[:-1], refs[-1]
    turn(at, qkv_ref, out_ref)
    out_ref[SMALL_AT:CHUNK_AT] = gather_small(small).astype(BF16)
    put_chunk(up_ref, down_ref, out_ref.at[CHUNK_AT:])


def begin(at, qkv_weight, up_weight, down_weight, small):
    return run(
        begin_kernel,
        at,
        [
            (qkv_weight, block((1, HALF, 3 * D), lambda s: (0, 0, 0))),
            *chunk_inputs(up_weight, down_weight, 0),
            *small,
        ],
        [shape((CHUNK_AT + CHUNK, HALF), BF16)],
        "begin",
        0,
        2700000,
    )[0]


def chunk_inputs(up_weight, down_weight, layer):
    column = lambda s: (s[RING_Y] // 2) * 4 + s[CORE] * 2 + s[RING_Y] % 2
    return [
        (up_weight, block((1, CHUNK_UP, HALF), lambda s: (layer, s[RING_X], column(s)))),
        (down_weight, block((1, CHUNK_DOWN, D), lambda s: (layer, s[CORE] * 16 + s[SPOT], 0))),
    ]


REST_CHUNK = LAYERS * HALF


def begin_rest_kernel(at, qkv_ref, up_ref, down_ref, out_ref, rows_ref, turned_ref):
    for layer in range(LAYERS):
        for side in range(2):
            row = layer * HALF + side * QKV
            rows_ref[row : row + QKV] = out_ref[layer, :, side * HALF : (side + 1) * HALF]
    put_chunk(up_ref, down_ref, rows_ref.at[REST_CHUNK:])
    turn(at, qkv_ref, turned_ref)


def begin_rest(at, qkv_weight, up_weight, down_weight, out_weight):
    return run(
        begin_rest_kernel,
        at,
        [
            (qkv_weight, block((1, HALF, 3 * D), lambda s: (1, 0, 0))),
            *chunk_inputs(up_weight, down_weight, 1),
            (out_weight, block((LAYERS, QKV, D), lambda s: (0, s[CORE], 0))),
        ],
        [shape((REST_CHUNK + CHUNK, HALF), BF16), shape((QKV_ROWS, HALF), BF16)],
        "begin_rest",
        0,
        1500000,
    )


def fill_up(z, up_ref, own0_ref, own1_ref, rest_ref):
    up_ref[half_at(z), 0:QUARTER] = own0_ref[0]
    up_ref[half_at(z), QUARTER:] = own1_ref[0]
    for chunk in range(16):
        x, y = chunk // 4, chunk % 4
        rows = pl.ds(pl.multiple_of((1 - z) * HALF + CHUNK_UP * x, 32), CHUNK_UP)
        up_ref[rows, y * HALF : (y + 1) * HALF] = rest_ref[chunk]


def fill_down(z, down_ref, own_ref, rest_ref):
    down_ref[pl.ds(pl.multiple_of(z * QUARTER, QUARTER), QUARTER), :] = own_ref[0]
    for chunk in range(16):
        rows = pl.ds(pl.multiple_of((1 - z) * QUARTER + CHUNK_DOWN * chunk, 16), CHUNK_DOWN)
        down_ref[rows, 0:HALF] = rest_ref[chunk, 0:CHUNK_DOWN]
        down_ref[rows, HALF:] = rest_ref[chunk, CHUNK_DOWN:]


def fill_out(z, out_ref, own_ref, other_ref):
    out_ref[pl.ds(pl.multiple_of(z * QKV, QKV), QKV), :] = own_ref[0]
    for side in range(2):
        rows = slice(side * QKV, (side + 1) * QKV)
        out_ref[pl.ds(pl.multiple_of((1 - z) * QKV, QKV), QKV), side * HALF : (side + 1) * HALF] = other_ref[rows, :]


def up_inputs(weights, rest, layer):
    own = [
        (weights, block((1, HALF, QUARTER), lambda s, z=z: (layer, 0, 2 * z + s[CORE]))) for z in range(2)
    ]
    return own + [(rest[layer], block((16, CHUNK_UP, HALF), lambda s: (0, 0, 0)))]


def down_inputs(weights, rest, layer):
    return [
        (weights, block((1, QUARTER, D), lambda s: (layer, s[CORE], 0))),
        (rest[layer], block((16, 2 * CHUNK_DOWN, HALF), lambda s: (0, 1, 0))),
    ]


def out_inputs(own, other, layer):
    return [
        (own, block((1, QKV, D), lambda s: (layer, s[CORE], 0))),
        (other, block((HALF, HALF), lambda s: (layer, 0))),
    ]


def norm_kernel(at, *refs, first):
    if first:
        stream_ref, gain_ref, offset_ref, hat_ref, inverse_ref, act_ref = refs
        stream = stream_ref[...].astype(F32)
    else:
        stream_ref, keep_ref, got_ref, bias_ref, gain_ref, offset_ref, next_ref, hat_ref, inverse_ref, act_ref = refs
        stream = stream_ref[...].astype(F32) + (keep_ref[...] + got_ref[...] + bias_ref[...])
        next_ref[...] = stream
    centered = stream - jnp.mean(stream, axis=-1, keepdims=True)
    inverse = lax.rsqrt(jnp.mean(centered * centered, axis=-1, keepdims=True) + EPSILON)
    hat = centered * inverse
    hat_ref[...] = hat
    inverse_ref[...] = inverse
    act_ref[:, 0:D] = (hat * gain_ref[0:1] + offset_ref[0:1]).astype(BF16)
    act_ref[:, D:] = (hat * gain_ref[1:2] + offset_ref[1:2]).astype(BF16)


def norms(at, stream, added, gain, offset):
    outs = [shape((TILE, D), F32), shape((TILE, 1), F32), shape((TILE, 2 * D), BF16)]
    if added is None:
        kernel = functools.partial(norm_kernel, first=True)
        return [None, *run(kernel, at, [stream, gain, offset], outs, "norms", 1000000, 1200000)]
    kernel = functools.partial(norm_kernel, first=False)
    outs = [shape((TILE, D), F32)] + outs
    return run(kernel, at, [stream, *added, gain, offset], outs, "norms", 1000000, 2400000)


def assemble(target_ref, mine, theirs):
    rows = TILE // 2
    target_ref[0:rows] = mine[:rows]
    target_ref[rows : 2 * rows] = theirs[:rows]
    target_ref[2 * rows : 3 * rows] = mine[rows:]
    target_ref[3 * rows :] = theirs[rows:]


def qkv_kernel(at, mine_ref, theirs_ref, own_ref, other_ref, bias_ref, cos_ref, sin_ref, *refs):
    along, (out_ref, tok_ref, act_t) = refs[:-3], refs[-3:]
    z = at[ZH]
    assemble(tok_ref, mine_ref[...], theirs_ref[...])
    act_t[...] = tok_ref[...].T
    cosine, sine = cos_ref[...], sin_ref[...]

    def rotated(part):
        low, high = part[:8], part[8:ROT]
        return jnp.concatenate(
            [low * cosine - high * sine, high * cosine + low * sine, part[ROT:]], axis=0
        )

    own_act, other_act = act_t[half_at(z), :], act_t[half_at(1 - z), :]
    for head in range(CORE_HEADS):
        rows = slice(head * QKV, (head + 1) * QKV)
        value = dot(own_ref[rows, :], own_act) + dot(other_ref[rows, :], other_act)
        bias = jnp.broadcast_to(bias_ref[head : head + 1, :], (8, QKV)).T
        value = value + bias[:, 0:1]
        query = (rotated(value[:HEAD]).astype(BF16).astype(F32) * 0.125).astype(BF16)
        key = rotated(value[HEAD : 2 * HEAD]).astype(BF16)
        val = value[2 * HEAD :].astype(BF16)
        for seq in range(2):
            lanes = slice(seq * TILE, (seq + 1) * TILE)
            out_ref[seq, head, 0:HEAD, :] = query[:, lanes]
            out_ref[seq, head, HEAD : 2 * HEAD, :] = key[:, lanes]
            out_ref[seq, head, 2 * HEAD : QKV, :] = val[:, lanes]
    for seq in range(2):
        out_ref[seq, CORE_HEADS:, 0:QKV, :] = jnp.zeros((SLOTS - CORE_HEADS, QKV, TILE), BF16)
        if along:
            out_ref[seq, :, QKV:, :] = along[0][seq * SLOTS : (seq + 1) * SLOTS]


def turned(weights):
    return weights, block((QKV_ROWS, HALF), lambda s: (0, 0))


def project_qkv(at, mine, theirs, own, other, bias, cosine, sine, along=None):
    left = block((TILE, D), lambda s: (0, 0))
    return run(
        qkv_kernel,
        at,
        [(mine, left), (theirs, left), turned(own), turned(other), bias, cosine, sine]
        + ([] if along is None else [along]),
        [shape((2, SLOTS, QKV if along is None else QKV + HEAD, TILE), BF16)],
        "qkv",
        4 * TILE * D * QKV_ROWS,
        3500000,
        [pltpu.VMEM((2 * TILE, D), BF16), pltpu.VMEM((D, 2 * TILE), BF16)],
        limit=24,
    )[0]


def mlp_kernel(
    at, mine_ref, theirs_ref, bias_ref, up0_ref, up1_ref, up_rest, down_own, down_rest, gate_ref, slope_ref, sum_ref, act, up, down
):
    z = at[ZH]
    act[0:TILE] = mine_ref[...]
    act[TILE:] = theirs_ref[...]
    fill_up(z, up, up0_ref, up1_ref, up_rest)
    fill_down(z, down, down_own, down_rest)
    total = jnp.zeros((2 * TILE, D), F32)
    for part in range(4):
        lanes = slice(part * HALF, (part + 1) * HALF)
        value = dot(act[...], up[:, lanes]) + bias_ref[:, lanes]
        normal = 0.5 * (1.0 + lax.erf(value * 0.7071067811865476))
        gate = (value * normal).astype(BF16)
        gate_ref[:, lanes] = gate
        slope_ref[:, lanes] = normal + value * (jnp.exp(-0.5 * value * value) * 0.3989422804014327)
        total = total + dot(gate, down[lanes, :])
    sum_ref[...] = total


def feed_forward(at, mine, theirs, bias, up, down, rest, layer, after=()):
    right = block((TILE, D), lambda s: (0, 1))
    tokens = 2 * TILE
    return run(
        mlp_kernel,
        at,
        [(mine, right), (theirs, right), bias, *up_inputs(up, rest, layer), *down_inputs(down, rest, layer)],
        [shape((tokens, CORE_FF), BF16), shape((tokens, CORE_FF), F32), shape((tokens, D), F32)],
        "mlp",
        4 * tokens * D * CORE_FF,
        8500000,
        [pltpu.VMEM((tokens, D), BF16), pltpu.VMEM((D, CORE_FF), BF16), pltpu.VMEM((CORE_FF, D), BF16)],
        limit=40,
        exps=2 * tokens * CORE_FF,
        after=after,
    )


def key_range(pair):
    first = max(-1, 2 * pair - WINDOW // TILE)
    return first, 2 * pair + 2


PAIRS_OF_TILES = sum(2 * (key_range(pair)[1] - key_range(pair)[0]) for pair in range(TILES // 2))


def allowed_mask(pair, first, last, low_row, pos_row, place):
    parts = []
    for tile in range(first, last):
        ok = place >= low_row - TILE * tile
        if tile >= 2 * pair:
            ok = ok & (place <= pos_row - TILE * tile)
        parts.append(ok)
    return jnp.concatenate(parts, axis=0)


def unturned(grads, cosine, sine):
    low, high = grads[:8], grads[8:ROT]
    return jnp.concatenate(
        [low * cosine + high * sine, high * cosine - low * sine, grads[ROT:]], axis=0
    ).astype(BF16)


def attention_kernel(at, *refs, forward, backward):
    refs = list(refs)
    take = lambda count: [refs.pop(0) for _ in range(count)]
    got_ref, halo_ref, low_ref, pos_ref = take(4)
    if backward:
        cos_ref, sin_ref = take(2)
        if not forward:
            dctx_ref, saved_ctx, saved_lse = take(3)
    if forward and not backward:
        out_ref, ctx_ref, lse_ref = take(3)
    if backward:
        packed_ref, edge_ref, tail_ref = take(3)
    key_tok, query_t = take(2)
    if forward:
        (val_t,) = take(1)
    if backward:
        val_tok, key_t, query_tok, dctx_t, dctx_tok, dkv = take(6)

    reverse = at[REVERSE]
    place = lax.broadcasted_iota(jnp.int32, (TILE, 2 * TILE), 0) ^ at[SWAPPED]

    def chip(tile):
        return jnp.where(reverse == 1, TILES - 1 - tile, tile)

    for tile in range(-1, TILES):
        here = slice(tile * TILE, (tile + 1) * TILE)
        after = slice((tile + 1) * TILE, (tile + 2) * TILE)
        if tile < 0:
            key, val = halo_ref[0:HEAD, :], halo_ref[HEAD:, :]
        else:
            source = chip(tile)
            query, key, val = (got_ref[source, part * HEAD : (part + 1) * HEAD, :] for part in range(3))
            query_t[:, here] = query
            if backward:
                query_tok[here, :] = query.T
                dctx = got_ref[source, QKV:, :] if forward else dctx_ref[source]
                dctx_t[:, here] = dctx
                dctx_tok[here, :] = dctx.T
        key_tok[after, :] = key.T
        if forward:
            val_t[:, after] = val
        if backward:
            key_t[:, after] = key
            val_tok[after, :] = val.T
    if backward:
        dkv[...] = jnp.zeros_like(dkv)
    for pair in range(TILES // 2):
        first, last = key_range(pair)
        rows = slice((first + 1) * TILE, (last + 1) * TILE)
        lanes = slice(pair * 2 * TILE, (pair + 1) * 2 * TILE)
        places = chip(2 * pair), chip(2 * pair + 1)
        scores = dot(key_tok[rows, :], query_t[:, lanes])
        ok = allowed_mask(pair, first, last, low_ref[:, lanes], pos_ref[:, lanes], place)
        scores = jnp.where(ok, scores, BLOCKED)
        if forward:
            peak = jnp.max(scores, axis=0, keepdims=True)
            probs = jnp.exp(scores - peak)
            total = jnp.sum(probs, axis=0, keepdims=True)
            inverse = 1.0 / total
            ctx = dot(val_t[:, rows], probs.astype(BF16)) * inverse
            low_ctx = ctx.astype(BF16)
            for index in range(2):
                lanes_here = slice(index * TILE, (index + 1) * TILE)
                if backward:
                    packed_ref[places[index], QKV:, :] = low_ctx[:, lanes_here]
                else:
                    out_ref[places[index]] = low_ctx[:, lanes_here]
            if backward:
                probs = probs * inverse
            else:
                ctx_ref[:, lanes] = ctx
                lse_ref[:, lanes] = peak + jnp.log(total)
        else:
            probs = jnp.exp(scores - saved_lse[:, lanes])
            ctx = saved_ctx[:, lanes]
        if backward:
            dctx = dctx_t[:, lanes]
            dprobs = dot(val_tok[rows, :], dctx)
            delta = jnp.sum(ctx * dctx.astype(F32), axis=0, keepdims=True)
            dscores = (probs * (dprobs - delta)).astype(BF16)
            dquery = dot(key_t[:, rows], dscores) * 0.125
            dquery = unturned(dquery, cos_ref[:, lanes], sin_ref[:, lanes])
            packed_ref[places[0], 0:HEAD, :] = dquery[:, :TILE]
            packed_ref[places[1], 0:HEAD, :] = dquery[:, TILE:]
            dkv[rows, 0:HEAD] += dot(dscores, query_tok[lanes, :])
            dkv[rows, HEAD:] += dot(probs.astype(BF16), dctx_tok[lanes, :])
    if backward:
        edge_ref[...] = dkv[0:TILE, :]
        tail_ref[...] = dkv[TILES * TILE :, :]
        for tile in range(TILES - 1):
            lanes = slice(tile * TILE, (tile + 1) * TILE)
            grads = dkv[(tile + 1) * TILE : (tile + 2) * TILE, :].T
            packed_ref[chip(tile), HEAD:QKV, :] = unturned(grads, cos_ref[:, lanes], sin_ref[:, lanes])
        packed_ref[chip(TILES - 1), HEAD:QKV, :] = jnp.zeros((2 * HEAD, TILE), BF16)


def attention(at, got, halo, low, pos, tables=None, dctx=None, saved=None):
    forward, backward = saved is None, tables is not None
    keys = UNIT + TILE
    inputs = [got, halo, low, pos]
    outs = []
    scratch = [pltpu.VMEM((keys, HEAD), BF16), pltpu.VMEM((HEAD, UNIT), BF16)]
    if forward:
        scratch.append(pltpu.VMEM((HEAD, keys), BF16))
        if not backward:
            outs += [shape((TILES, HEAD, TILE), BF16), shape((HEAD, UNIT), F32), shape((1, UNIT), F32)]
    if backward:
        inputs += list(tables)
        if saved is not None:
            inputs += [dctx, *saved]
        rows = QKV + HEAD if forward else QKV
        outs += [shape((TILES, rows, TILE), BF16), shape((TILE, 2 * HEAD), F32), shape((TILE, 2 * HEAD), F32)]
        scratch += [
            pltpu.VMEM((keys, HEAD), BF16),
            pltpu.VMEM((HEAD, keys), BF16),
            pltpu.VMEM((UNIT, HEAD), BF16),
            pltpu.VMEM((HEAD, UNIT), BF16),
            pltpu.VMEM((UNIT, HEAD), BF16),
            pltpu.VMEM((keys, 2 * HEAD), F32),
        ]
    products = (2 if forward else 1) + (4 if backward else 0)
    return run(
        functools.partial(attention_kernel, forward=forward, backward=backward),
        at,
        inputs,
        outs,
        "attention" + ("_forward" if forward else "") + ("_backward" if backward else ""),
        2 * products * PAIRS_OF_TILES * TILE * TILE * HEAD * 4,
        4000000,
        scratch,
        exps=PAIRS_OF_TILES * TILE * TILE,
    )


def edge_kernel(at, packed_ref, tail_ref, edge_ref, cos_ref, sin_ref, out_ref):
    grads = tail_ref[...] + jnp.where(at[FIRST_HALF] == 1, edge_ref[...], 0.0)
    out_ref[0, 0:HEAD, :] = packed_ref[0, 0:HEAD, :]
    out_ref[0, HEAD:QKV, :] = unturned(grads.T, cos_ref[...], sin_ref[...])
    if out_ref.shape[1] > QKV:
        out_ref[0, QKV:, :] = packed_ref[0, QKV:, :]


def add_edge(at, packed, tail, edge, cosine, sine):
    spec = block((1,) + packed.shape[1:], lambda s: (s[LAST_CHIP], 0, 0))
    last = block((8, TILE), lambda s: (0, TILES - 1))
    return run(
        edge_kernel,
        at,
        [(packed, spec), tail, edge, (cosine, last), (sine, last)],
        [shape(packed.shape, BF16)],
        "attention_edge",
        100000,
        300000,
        limit=8,
        aliases={1: 0},
        out_specs=[spec],
    )[0]


def out_kernel(at, got_ref, own_ref, other_ref, sum_ref, keep_ref, give_ref, weights):
    fill_out(at[ZH], weights, own_ref, other_ref)
    rows = TILE // 2
    for seq in range(2):
        ctx = got_ref[seq * SLOTS : seq * SLOTS + CORE_HEADS].reshape(HALF, TILE)
        value = dot(ctx, weights[...], TN)
        here = slice(seq * rows, (seq + 1) * rows)
        there = slice(TILE + seq * rows, TILE + (seq + 1) * rows)
        keep_ref[here, :] = value[:rows] + sum_ref[here, :]
        give_ref[here, :] = value[rows:] + sum_ref[there, :]


def ctx_of(got):
    return got, block((TILES, HEAD, TILE), lambda s: (0, got.shape[1] // HEAD - 1, 0))


def attention_out(at, got, outs, total, layer, after=()):
    return run(
        out_kernel,
        at,
        [ctx_of(got), *out_inputs(*outs, layer), total],
        [shape((TILE, D), F32), shape((TILE, D), F32)],
        "attention_out",
        4 * TILE * HALF * D,
        2700000,
        [pltpu.VMEM((HALF, D), BF16)],
        after=after,
    )


def dctx_kernel(at, mine_ref, theirs_ref, own_ref, other_ref, out_ref, weights, tok):
    fill_out(at[ZH], weights, own_ref, other_ref)
    assemble(tok, mine_ref[...], theirs_ref[...])
    value = dot(weights[...], tok[...], NT).astype(BF16)
    for seq in range(2):
        part = value[:, seq * TILE : (seq + 1) * TILE].reshape(CORE_HEADS, HEAD, TILE)
        start = seq * SLOTS
        out_ref[start : start + CORE_HEADS] = part
        out_ref[start + CORE_HEADS : start + SLOTS] = jnp.zeros((SLOTS - CORE_HEADS, HEAD, TILE), BF16)


def grad_ctx(at, mine, theirs, outs, layer):
    return run(
        dctx_kernel,
        at,
        [mine, theirs, *out_inputs(*outs, layer)],
        [shape((TILES, HEAD, TILE), BF16)],
        "grad_ctx",
        4 * TILE * HALF * D,
        1300000,
        [pltpu.VMEM((HALF, D), BF16), pltpu.VMEM((2 * TILE, D), BF16)],
    )[0]


def put_early(z, act_mine, act_theirs, gate_ref, sent_ref):
    sent_ref[0:TILE, 0:HALF] = act_mine[:, half_at(1 - z)]
    sent_ref[TILE:, 0:HALF] = act_theirs[:, half_at(1 - z)]
    lanes = pl.ds(pl.multiple_of((1 - z) * QUARTER, QUARTER), QUARTER)
    sent_ref[:, SENT_GATE:SENT_CTX] = gate_ref[:, lanes]


def mlp_back_kernel(at, *refs, early):
    refs = list(refs)
    take = lambda count: [refs.pop(0) for _ in range(count)]
    mine_ref, theirs_ref, slope_ref, up0_ref, up1_ref, up_rest, down_own, down_rest = take(8)
    if early:
        act_mine, act_theirs, gate_ref = take(3)
    dup_ref, keep_ref, give_ref, bias_ref, sent_ref, dhid, up, down = refs
    z = at[ZH]
    dhid[0:TILE] = mine_ref[...]
    dhid[TILE:] = theirs_ref[...]
    fill_up(z, up, up0_ref, up1_ref, up_rest)
    fill_down(z, down, down_own, down_rest)
    total = jnp.zeros((2 * TILE, D), F32)
    start = SENT_CTX if early else 0
    for part in range(4):
        lanes = slice(part * HALF, (part + 1) * HALF)
        value = dot(dhid[...], down[lanes, :], NT) * slope_ref[:, lanes]
        dup = value.astype(BF16)
        dup_ref[:, lanes] = dup
        sent_ref[:, start + part * HALF : start + (part + 1) * HALF] = dup
        bias_ref[part : part + 1, :] = jnp.sum(dup.astype(F32), axis=0, keepdims=True)
        total = total + dot(dup, up[:, lanes], NT)
    keep_ref[...] = total[:TILE]
    give_ref[...] = total[TILE:]
    sent_ref[:, start + CORE_FF :] = dhid[...]
    if early:
        put_early(z, act_mine, act_theirs, gate_ref, sent_ref)


def mlp_back(at, mine, theirs, slope, up, down, rest, layer, early=None):
    right = block((TILE, D), lambda s: (0, 1))
    tokens = 2 * TILE
    extra = [] if early is None else [(early[0], right), (early[1], right), early[2]]
    width = SENT_LATE + (0 if early is None else SENT_CTX)
    return run(
        functools.partial(mlp_back_kernel, early=early is not None),
        at,
        [mine, theirs, slope, *up_inputs(up, rest, layer), *down_inputs(down, rest, layer), *extra],
        [
            shape((tokens, CORE_FF), BF16),
            shape((TILE, D), F32),
            shape((TILE, D), F32),
            shape((4, HALF), F32),
            shape((tokens, width), BF16),
        ],
        "mlp_back",
        4 * tokens * D * CORE_FF,
        8500000,
        [pltpu.VMEM((tokens, D), BF16), pltpu.VMEM((D, CORE_FF), BF16), pltpu.VMEM((CORE_FF, D), BF16)],
    )


def early_kernel(at, act_mine, act_theirs, gate_ref, ctx_ref, sent_ref):
    z = at[ZH]
    put_early(z, act_mine, act_theirs, gate_ref, sent_ref)
    for seq in range(2):
        ctx = ctx_ref[pl.ds(seq * SLOTS + 3 * (1 - z), 3)].reshape(QKV, TILE)
        sent_ref[seq * TILE : (seq + 1) * TILE, SENT_CTX : SENT_CTX + QKV] = ctx.T
    sent_ref[:, SENT_CTX + QKV :] = jnp.zeros((2 * TILE, HEAD), BF16)


def pack_early(at, mine, theirs, gate, ctx):
    right = block((TILE, D), lambda s: (0, 1))
    outs = [shape((2 * TILE, SENT_EARLY), BF16)]
    return run(early_kernel, at, [(mine, right), (theirs, right), gate, ctx], outs, "pack_early", 0, 0)[0]


def put_out_grads(grads, ctx_ref, tok, z, offset, length):
    for side in range(2):
        lanes = slice(side * HALF, (side + 1) * HALF)
        value = jnp.zeros((QKV, HALF), F32)
        for seq in range(2):
            ctx = ctx_ref[seq * SLOTS + 3 * z : seq * SLOTS + 3 * z + 3].reshape(QKV, TILE)
            value = value + dot(ctx, tok[seq * TILE : (seq + 1) * TILE, lanes])
        value = value.astype(BF16)
        for index in range(2):
            start = (2 * side + index) * length + offset
            grads[start : start + OUT_PART, :] = value[index * OUT_PART : (index + 1) * OUT_PART]


def by_chunks(grads, out_ref, length):
    out_ref[...] = grads[...].reshape(16, length // 4, HALF)


def own_grads_kernel(at, act_mine, act_theirs, mine_ref, theirs_ref, gate_ref, dup_ref, *refs, with_ctx):
    refs = list(refs)
    if with_ctx:
        ctx_ref, early_ref, late_ref, out_ref, done_ref, act, dhid, grads, tok, tok_other = refs
        length, start = PART_FIRST, 0
    else:
        late_ref, out_ref, done_ref, act, dhid, grads = refs
        early_ref = late_ref
        length, start = PART_SECOND, SENT_CTX
    z = at[ZH]
    done_ref[...] = jnp.zeros_like(done_ref)
    act[0:TILE] = act_mine[:, half_at(z)]
    act[TILE:] = act_theirs[:, half_at(z)]
    dhid[0:TILE] = mine_ref[...]
    dhid[TILE:] = theirs_ref[...]
    act_t, act_other = act[...].T, early_ref[:, 0:HALF].T
    for part in range(4):
        lanes = slice(part * HALF, (part + 1) * HALF)
        other = slice(start + part * HALF, start + (part + 1) * HALF)
        value = dot(act_t, dup_ref[:, lanes]) + dot(act_other, late_ref[:, other])
        grads[part * length : part * length + HALF, :] = value.astype(BF16)
    start += CORE_FF
    gate_t = gate_ref[:, pl.ds(pl.multiple_of(z * QUARTER, QUARTER), QUARTER)].T
    gate_other = early_ref[:, SENT_GATE:SENT_CTX].T
    for side in range(2):
        lanes = slice(side * HALF, (side + 1) * HALF)
        other = slice(start + side * HALF, start + (side + 1) * HALF)
        value = (dot(gate_t, dhid[:, lanes]) + dot(gate_other, late_ref[:, other])).astype(BF16)
        for index in range(2):
            row = (2 * side + index) * length + HALF
            grads[row : row + HALF, :] = value[index * HALF : (index + 1) * HALF]
    if with_ctx:
        assemble(tok, mine_ref[...], theirs_ref[...])
        assemble(tok_other, late_ref[0:TILE, start:], late_ref[TILE:, start:])
        ctx_other = early_ref[:, SENT_CTX : SENT_CTX + QKV].T
        for side in range(2):
            lanes = slice(side * HALF, (side + 1) * HALF)
            value = dot(ctx_other, tok_other[:, lanes])
            for seq in range(2):
                ctx = ctx_ref[pl.ds(seq * SLOTS + 3 * z, 3)].reshape(QKV, TILE)
                value = value + dot(ctx, tok[seq * TILE : (seq + 1) * TILE, lanes])
            value = value.astype(BF16)
            for index in range(2):
                row = (2 * side + index) * length + 2 * HALF
                grads[row : row + OUT_PART, :] = value[index * OUT_PART : (index + 1) * OUT_PART]
                grads[row + OUT_PART : row + OUT_PART + 32, :] = jnp.zeros((32, HALF), BF16)
    by_chunks(grads, out_ref, length)


def own_grads(at, mine, theirs, dmine, dtheirs, gate, dup, late, early=None, ctx=None):
    right = block((TILE, D), lambda s: (0, 1))
    tokens = 2 * TILE
    length = PART_SECOND if ctx is None else PART_FIRST
    inputs = [(mine, right), (theirs, right), dmine, dtheirs, gate, dup]
    inputs += [late] if ctx is None else [ctx, early, late]
    scratch = [pltpu.VMEM((tokens, HALF), BF16), pltpu.VMEM((tokens, D), BF16), pltpu.VMEM((4 * length, HALF), BF16)]
    if ctx is not None:
        scratch += [pltpu.VMEM((tokens, D), BF16)] * 2
    return run(
        functools.partial(own_grads_kernel, with_ctx=ctx is not None),
        at,
        inputs,
        [shape((16, length // 4, HALF), BF16), shape((8, 128), F32)],
        "own_grads",
        4 * tokens * 4 * length * HALF,
        8000000,
        scratch,
        token=True,
    )[0]


def grads_qkv_kernel(
    at, got_ref, mine_ref, theirs_ref, dmine_ref, dtheirs_ref, ctx_ref, out_ref, done_ref, act, tok, grads
):
    done_ref[...] = jnp.zeros_like(done_ref)
    assemble(act, mine_ref[...], theirs_ref[...])
    assemble(tok, dmine_ref[...], dtheirs_ref[...])
    for z in range(2):
        put_out_grads(grads, ctx_ref, tok, z, QKV_PART, PART_QKV)
        lanes = slice(z * HALF, (z + 1) * HALF)
        value = jnp.zeros((QKV_ROWS, HALF), F32)
        for seq in range(2):
            rows = got_ref[seq * SLOTS : seq * SLOTS + CORE_HEADS, 0:QKV, :].reshape(QKV_ROWS, TILE)
            value = value + dot(rows, act[seq * TILE : (seq + 1) * TILE, lanes])
        value = value.astype(BF16)
        for part in range(4):
            start = part * PART_QKV
            grads[start : start + QKV_PART, :] = value[part * QKV_PART : (part + 1) * QKV_PART]
        out_ref[:, z] = grads[...].reshape(16, CHUNK_QKV, HALF)


def grads_qkv(at, got, mine, theirs, dmine, dtheirs):
    left = block((TILE, D), lambda s: (0, 0))
    return run(
        grads_qkv_kernel,
        at,
        [got, (mine, left), (theirs, left), dmine, dtheirs, ctx_of(got)],
        [shape((16, 2, CHUNK_QKV, HALF), BF16), shape((8, 128), F32)],
        "grads_qkv",
        4 * TILE * D * 4 * PART_QKV,
        3800000,
        [pltpu.VMEM((2 * TILE, D), BF16)] * 2 + [pltpu.VMEM((4 * PART_QKV, HALF), BF16)],
        token=True,
    )[0]


def qkv_back_kernel(at, got_ref, own_ref, other_ref, keep_ref, give_ref, bias_ref):
    z = at[ZH]
    rows = TILE // 2
    sums = jnp.zeros((8, QKV_ROWS), F32)
    for seq in range(2):
        tok = got_ref[seq * SLOTS : seq * SLOTS + CORE_HEADS, 0:QKV, :].reshape(QKV_ROWS, TILE).T
        sums = sums + dot(jnp.ones((8, TILE), BF16), tok)
        here = slice(seq * rows, (seq + 1) * rows)
        for weights, at_z in ((own_ref, z), (other_ref, 1 - z)):
            value = dot(tok, weights[...])
            keep_ref[here, half_at(at_z)] = value[:rows]
            give_ref[here, half_at(at_z)] = value[rows:]
    bias_ref[...] = sums


def qkv_back(at, got, own, other):
    return run(
        qkv_back_kernel,
        at,
        [got, turned(own), turned(other)],
        [shape((TILE, D), F32), shape((TILE, D), F32), shape((8, QKV_ROWS), F32)],
        "qkv_back",
        4 * TILE * D * QKV_ROWS,
        3500000,
        limit=24,
    )


def qkv_rows(got_ref, tok, out_ref):
    for z in range(2):
        lanes = slice(z * HALF, (z + 1) * HALF)
        value = jnp.zeros((QKV_ROWS, HALF), F32)
        for seq in range(2):
            grads = got_ref[seq * SLOTS : seq * SLOTS + CORE_HEADS].reshape(QKV_ROWS, TILE)
            value = value + dot(grads, tok[seq * TILE : (seq + 1) * TILE, lanes])
        out_ref[z, 0:QKV_ROWS, :] = value.astype(BF16)


def qkv_grads_first_kernel(at, got_ref, mine_ref, theirs_ref, *refs):
    sums, (out_ref, tok, small) = refs[:6], refs[6:]
    assemble(tok, mine_ref[...], theirs_ref[...])
    qkv_rows(got_ref, tok, out_ref)

    def by_core(core):
        for z in range(2):
            small[...] = jnp.zeros((4 * SMALL, HALF), F32)
            for layer in range(LAYERS):
                norm_ref, up_ref, qkv_ref = sums[3 * layer : 3 * layer + 3]
                start = layer * SMALL
                for index in range(5):
                    small[start + index : start + index + 1] = norm_ref[2 * index + z : 2 * index + z + 1]
                for index in range(3):
                    part, half = (3 * z + index) // 2, (3 * z + index) % 2
                    for head in range(3):
                        lane = core * QKV + head * HEAD
                        source = (3 * half + head) * QKV + part * HEAD
                        small[start + 5 + index : start + 6 + index, lane : lane + HEAD] = qkv_ref[
                            0:1, source : source + HEAD
                        ]
                for side in range(2):
                    row = start + 8 + 2 * core + side
                    small[row : row + 1] = up_ref[2 * z + side : 2 * z + side + 1]
            out_ref[z, QKV_ROWS : QKV_ROWS + 4 * SMALL, :] = small[...].astype(BF16)
            used = QKV_ROWS + 4 * SMALL
            out_ref[z, used:, :] = jnp.zeros((QKV_FIRST - used, HALF), BF16)

    for core in range(2):
        pl.when(at[CORE] == core)(functools.partial(by_core, core))


def qkv_grads_first(at, got, mine, theirs, sums, after):
    left = block((TILE, D), lambda s: (0, 0))
    return run(
        qkv_grads_first_kernel,
        at,
        [got, (mine, left), (theirs, left), *sums],
        [shape((2, QKV_FIRST, HALF), BF16)],
        "qkv_grads_first",
        4 * TILE * D * QKV_ROWS,
        3300000,
        [pltpu.VMEM((2 * TILE, D), BF16), pltpu.VMEM((4 * SMALL, HALF), F32)],
        after=after,
    )[0]


def norm_back_kernel(
    at, keep0, got0, keep1, got1, hat_ref, inverse_ref, gain_ref, dstream_ref, next_ref, low_ref, sums_ref
):
    first, second = keep0[...] + got0[...], keep1[...] + got1[...]
    hat = hat_ref[...]
    dstream = dstream_ref[...].astype(F32)
    dhat = first * gain_ref[0:1] + second * gain_ref[1:2]
    grad = inverse_ref[...] * (
        dhat
        - jnp.mean(dhat, axis=-1, keepdims=True)
        - hat * jnp.mean(dhat * hat, axis=-1, keepdims=True)
    )
    total = dstream + grad
    next_ref[...] = total
    low_ref[...] = total.astype(BF16)
    rows = (first * hat, second * hat, first, second, dstream.astype(BF16).astype(F32))
    for index, value in enumerate(rows):
        row = jnp.sum(value, axis=0, keepdims=True)
        sums_ref[2 * index : 2 * index + 1, :] = row[:, :HALF]
        sums_ref[2 * index + 1 : 2 * index + 2, :] = row[:, HALF:]


def norm_back(at, first, second, hat, inverse, gain, dstream):
    return run(
        norm_back_kernel,
        at,
        [*first, *second, hat, inverse, gain, dstream],
        [shape((TILE, D), F32), shape((TILE, D), BF16), shape((10, HALF), F32)],
        "norm_back",
        2000000,
        3400000,
        limit=24,
    )


def rows_of(part, start, count, chunk, length, offset=0):
    at = start
    while at < start + count:
        step = min(chunk - at % chunk, start + count - at)
        yield (4 * part + at // chunk) * length + offset + at % chunk, at - start, step
        at += step


def place_mlp(source, core, up_ref, down_ref, chunk, length, offset=0):
    for part in range(4):
        z, side = part // 2, part % 2
        column = z * CORE_FF + core * QUARTER + side * HALF
        for source_row, row, count in rows_of(part, 0, HALF, chunk, length, offset):
            up_ref[0, row : row + count, column : column + HALF] = source[source_row : source_row + count, :].astype(F32)
        side, index = part // 2, part % 2
        lanes = slice(side * HALF, (side + 1) * HALF)
        first = core * QUARTER + index * HALF
        for source_row, row, count in rows_of(part, HALF, HALF, chunk, length, offset):
            row += first
            down_ref[0, row : row + count, lanes] = source[source_row : source_row + count, :].astype(F32)


def for_cores(at, mine, theirs, put):
    for here, source in ((True, mine), (False, theirs)):
        for core in range(2):
            pl.when((at[CORE] == core) == here)(functools.partial(put, core, source))


UP_SHAPE, DOWN_SHAPE, OUT_SHAPE = (LAYERS, HALF, FF), (LAYERS, FF // 2, D), (LAYERS, HALF, D)
QKV_SHAPE = (LAYERS, HALF, 3 * D)
PLACED = (UP_SHAPE, DOWN_SHAPE, OUT_SHAPE)


def place_out(source, core, out_ref, first, chunk, length, offset):
    for part in range(4):
        lanes = slice((part // 2) * HALF, (part // 2 + 1) * HALF)
        start = core * QKV + (part % 2) * OUT_PART
        for source_row, row, count in rows_of(part, first, OUT_PART, chunk, length, offset):
            row += start
            out_ref[0, row : row + count, lanes] = source[source_row : source_row + count, :].astype(F32)


def place_turned(rows_ref, out_ref, part, z):
    column = part * D + z * HALF
    out_ref[0, :, column : column + HALF] = rows_ref[...].T


LENGTH = CHUNK_FIRST + CHUNK_QKV + CHUNK_SECOND


def place_part(source, layer, z, up_ref, down_ref, out_ref):
    if layer == 0:
        main = CHUNK_FIRST, LENGTH, 0
        outs = 2 * HALF, CHUNK_FIRST, LENGTH, 0
    else:
        main = CHUNK_SECOND, LENGTH, CHUNK_FIRST + CHUNK_QKV
        outs = QKV_PART, CHUNK_QKV, LENGTH, CHUNK_FIRST
    half = slice(z * HALF, (z + 1) * HALF)
    for index in range(2):
        part = 2 * z + index
        lanes = slice(index * HALF, (index + 1) * HALF)
        for start, row, count in rows_of(part, 0, HALF, *main):
            up_ref[0, row : row + count, lanes] = source[start : start + count, :].astype(F32)
        for start, row, count in rows_of(part, HALF, HALF, *main):
            row += index * HALF
            down_ref[0, row : row + count, half] = source[start : start + count, :].astype(F32)
        for start, row, count in rows_of(part, outs[0], OUT_PART, *outs[1:]):
            row += index * OUT_PART
            out_ref[0, row : row + count, half] = source[start : start + count, :].astype(F32)


def place_long_kernel(at, *refs, mine):
    if mine:
        source, _, up_ref, down_ref, out_ref = refs
    else:
        mine_ref, source, _, _, _, _, _, up_ref, down_ref, out_ref, qkv_ref, rows_ref = refs
    for layer in range(LAYERS):
        for z in range(2):
            here = (pl.program_id(0) == layer) & (pl.program_id(1) == z)
            pl.when(here)(functools.partial(place_part, source, layer, z, up_ref, down_ref, out_ref))
    if mine:
        return

    @pl.when((pl.program_id(0) == 0) & (pl.program_id(1) == 0))
    def _():
        for part in range(3):
            for z in range(2):

                def put_rows(core, source):
                    for head in range(3):
                        row = (z * 3 + head) * QKV + part * HEAD
                        to = core * QKV + head * HEAD
                        for start in range(row, row + HEAD, 32):
                            pieces = rows_of(start // QKV_PART, start % QKV_PART, 32, CHUNK_QKV, LENGTH, CHUNK_FIRST)
                            for source_row, more, count in pieces:
                                here = to + start - row + more
                                rows_ref[here : here + count, :] = source[source_row : source_row + count, :].astype(F32)

                for_cores(at, mine_ref, source, put_rows)
                place_turned(rows_ref, qkv_ref, part, z)


def place_long(at, sources, filled):
    mine = len(sources) == 1
    anywhere = pl.BlockSpec(memory_space=pl.ANY)
    once = pl.BlockSpec(sources[0].shape, lambda i, z, s: (0, 0), pipeline_mode=pl.Buffered(1))
    core = (lambda s: s[CORE]) if mine else (lambda s: 1 - s[CORE])
    specs = [
        pl.BlockSpec((1, HALF, QUARTER), lambda i, z, s: (i, 0, 2 * z + core(s))),
        pl.BlockSpec((1, QUARTER, D), lambda i, z, s: (i, core(s), 0)),
        pl.BlockSpec((1, QKV, D), lambda i, z, s: (i, core(s), 0)),
    ]
    outs = list(PLACED)
    scratch = []
    if not mine:
        specs.append(pl.BlockSpec((1,) + QKV_SHAPE[1:], lambda i, z, s: (1, 0, 0)))
        outs.append(QKV_SHAPE)
        scratch.append(pltpu.VMEM((HALF, HALF), F32))
    count = len(sources)
    return pl.pallas_call(
        functools.partial(place_long_kernel, mine=mine),
        grid_spec=pltpu.PrefetchScalarGridSpec(
            num_scalar_prefetch=1,
            grid=(LAYERS, 2),
            in_specs=[once] * count + [anywhere] * (len(filled) + 1),
            out_specs=specs,
            scratch_shapes=scratch,
        ),
        out_shape=[shape(dims, F32) for dims in outs],
        input_output_aliases={1 + count + index: index for index in range(len(filled))},
        compiler_params=pltpu.CompilerParams(vmem_limit_bytes=60 * 1024 * 1024),
        cost_estimate=pl.CostEstimate(flops=1, bytes_accessed=1, transcendentals=0),
        name="place_mine" if mine else "place_theirs",
    )(at, *sources, *filled, *LATEST)


def place_qkv_kernel(
    at, mine_ref, theirs_ref, out_ref, gain_ref, offset_ref, hidden_ref, again_ref, qkv_ref, up_ref, rows_ref
):
    for part in range(3):
        for z in range(2):

            def put(core, source):
                for head in range(3):
                    row = (z * 3 + head) * QKV + part * HEAD
                    to = core * QKV + head * HEAD
                    rows_ref[to : to + HEAD, :] = source[row : row + HEAD, :].astype(F32)

            for_cores(at, mine_ref, theirs_ref, put)
            place_turned(rows_ref, out_ref, part, z)
    rows = slice(QKV_ROWS, QKV_ROWS + 2 * SMALL + 8)
    small = mine_ref[rows, :].astype(F32) + theirs_ref[rows, :].astype(F32)
    for layer in range(LAYERS):
        start = layer * SMALL
        gain_ref[layer] = small[start : start + 2]
        offset_ref[layer] = small[start + 2 : start + 4]
        hidden_ref[layer : layer + 1] = small[start + 4 : start + 5]
        again_ref[layer : layer + 1] = small[start + 4 : start + 5]
        for index in range(3):
            lanes = slice(index * HALF, (index + 1) * HALF)
            qkv_ref[layer : layer + 1, lanes] = small[start + 5 + index : start + 6 + index]
        for index in range(4):
            lanes = slice(index * HALF, (index + 1) * HALF)
            up_ref[layer : layer + 1, lanes] = small[start + 8 + index : start + 9 + index]


def place_qkv(at, mine, theirs):
    outs = [shape((LAYERS, HALF, 3 * D), F32)]
    specs = [block((1, HALF, 3 * D), lambda s: (0, 0, 0))]
    for dims in ((2, HALF), (2, HALF), (HALF,), (HALF,), (3 * HALF,), (4 * HALF,)):
        outs.append(shape((LAYERS,) + dims, F32))
        specs.append(block((LAYERS,) + dims))
    return run(
        place_qkv_kernel,
        at,
        [mine, theirs],
        outs,
        "place_qkv",
        0,
        6000000,
        [pltpu.VMEM((HALF, HALF), F32)],
        limit=40,
        out_specs=specs,
    )


ROW_GAIN, ROW_OFFSET, ROW_QKV, ROW_OUT, ROW_UP, ROW_DOWN, SMALL_ROWS = 0, 4, 8, 14, 16, 24, 32


def gather_small(refs):
    gain, offset, qkv, out, up, down = (ref[...].astype(F32) for ref in refs)
    rows = [gain.reshape(4, HALF), offset.reshape(4, HALF)]
    rows += [qkv[layer : layer + 1, part * HALF : (part + 1) * HALF] for layer in range(LAYERS) for part in range(3)]
    rows.append(out)
    rows += [up[layer : layer + 1, part * HALF : (part + 1) * HALF] for layer in range(LAYERS) for part in range(4)]
    rows += [down, jnp.zeros((SMALL_ROWS - ROW_DOWN - LAYERS, HALF), F32)]
    return jnp.concatenate(rows, axis=0)


def spread_small_kernel(at, own_ref, other_ref, *outs):
    own, other = own_ref[...].astype(F32), other_ref[...].astype(F32)
    swap = at[ZH] == 1
    halves = jnp.where(swap, other, own), jnp.where(swap, own, other)

    def row(index, z):
        return halves[z][index : index + 1]

    def by_core(core):
        for layer in range(LAYERS):
            qkv_ref, up_ref = outs[5 * layer + 2], outs[5 * layer + 4]
            for part in range(3):
                for z in range(2):
                    place = part * 2 + z
                    values = row(ROW_QKV + layer * 3 + place % 3, place // 3)
                    for head in range(3):
                        lane = core * QKV + head * HEAD
                        qkv_ref[3 * z + head : 3 * z + head + 1, part * HEAD : (part + 1) * HEAD] = values[
                            :, lane : lane + HEAD
                        ]
            for z in range(2):
                for side in range(2):
                    lane = z * QUARTER + side * HALF
                    up_ref[:, lane : lane + HALF] = row(ROW_UP + 4 * layer + 2 * core + side, z)

    for core in range(2):
        pl.when(at[CORE] == core)(functools.partial(by_core, core))
    for layer in range(LAYERS):
        gain_ref, offset_ref, _, rest_ref, _ = outs[5 * layer : 5 * layer + 5]
        for z in range(2):
            lanes = slice(z * HALF, (z + 1) * HALF)
            for index in range(2):
                gain_ref[index : index + 1, lanes] = row(ROW_GAIN + 2 * layer + index, z)
                offset_ref[index : index + 1, lanes] = row(ROW_OFFSET + 2 * layer + index, z)
            rest_ref[:, lanes] = row(ROW_OUT + layer, z) + row(ROW_DOWN + layer, z)


def spread_small(at, rows, other):
    outs = [shape((2, D), F32), shape((2, D), F32), shape((8, QKV), F32), shape((1, D), F32), shape((1, CORE_FF), F32)]
    spec = block((SMALL_ROWS, HALF), lambda s: (QKV_ROWS // SMALL_ROWS, 0))
    values = run(spread_small_kernel, at, [(rows, spec), (other, spec)], outs * LAYERS, "small_spread", 0, 0)
    return zip(values[:5], values[5:])


EVERY = ("zh", "xh", "xl", "y", "zl")
ACROSS = ("xh", "xl", "y")
CHIPS = ("xl", "zl", "y")


def exchange(values):
    return lax.ppermute(values, "core", SWAP)


def scatter_sum(grads):
    parts = grads.reshape(64, -1, HALF)
    parts = lax.all_to_all(parts, EVERY, 0, 0, tiled=True)
    return jnp.sum(parts.astype(F32), axis=0).astype(BF16)


def add_from(part, other):
    return (part.astype(F32) + other.astype(F32)).astype(BF16)


def ring(values, axis, by):
    return lax.ppermute(values, axis, [(place, (place + by) % 4) for place in range(4)])


X_RING, Y_RING = ("xh", "xl"), "y"


def around(pieces, first, second):
    return [
        (ring(piece, first if index < 4 else second, index % 4) if index % 4 else piece)
        for index, piece in enumerate(pieces)
    ]


def sum_x(grads):
    return lax.psum_scatter(grads.reshape(-1, HALF), X_RING, scatter_dimension=0, tiled=True)


def sum_y(part):
    return lax.psum_scatter(part, Y_RING, scatter_dimension=0, tiled=True)


def sum_grid(grads):
    parts = lax.all_to_all(grads, ACROSS, 0, 0, tiled=True)
    return jnp.sum(parts.astype(F32), axis=0).astype(BF16)


def sum_near(part):
    return add_from(part, lax.ppermute(part, "zl", SWAP))


def sum_depth(zh, part):
    part = part.reshape(2, -1, HALF)
    keep = jnp.where(zh == 0, part[0], part[1])
    give = jnp.where(zh == 0, part[1], part[0])
    near = lax.ppermute(keep, "zl", SWAP)
    far = lax.ppermute(give, "zh", SWAP)
    across = lax.ppermute(give, ("zl", "zh"), [(0, 3), (3, 0), (1, 2), (2, 1)])
    total = (keep.astype(F32) + near.astype(F32)) + (far.astype(F32) + across.astype(F32))
    return total.astype(BF16)


def gather_short(part):
    copies = jnp.broadcast_to(part[None], (32,) + part.shape)
    return lax.all_to_all(copies, EVERY[1:], 0, 0, tiled=True).reshape(-1, HALF)


def token_places(offsets, lengths):
    ends = jnp.cumsum(lengths)
    before = ends[:, None] <= offsets[None, :]
    start = jnp.max(jnp.where(before, ends[:, None], 0), axis=0)
    return start, offsets >= ends[DOCS - 2]


def rotary(places):
    frequency = 1.0 / 10000.0 ** (jnp.arange(0, ROT, 2).astype(F32) / ROT)
    angles = frequency[:, None] * places.astype(F32)[None, :]
    return jnp.cos(angles), jnp.sin(angles)


def local(
    hidden_in,
    doc_lengths,
    norm_gain,
    norm_bias,
    qkv_weight,
    qkv_bias,
    out_weight,
    out_bias,
    up_weight,
    up_bias,
    down_weight,
    down_bias,
    cotangent,
):
    LATEST.clear()
    zh, core, xh, xl, zl, y = (lax.axis_index(name) for name in ("zh", "core", "xh", "xl", "zl", "y"))
    chip = (xl * 2 + zl) * 4 + y
    x = xh * 2 + xl
    lengths = doc_lengths[0]

    unit_seq = xl
    unit_half = jnp.where(unit_seq == 0, xh, 1 - xh)
    unit_swap = jnp.where(unit_seq == core, 0, TILE // 2)
    last_chip = jnp.where(unit_seq == 0, TILES - 1, 0)
    at = jnp.stack(
        [core, zh, unit_seq, unit_swap, 1 - unit_half, last_chip, x, y, x * 4 + y]
    ).astype(jnp.int32)

    lane = jnp.arange(TILE, dtype=jnp.int32)
    seq0_tile = xh * TILES + chip
    places = []
    for seq, tile in ((0, seq0_tile), (1, 2 * TILES - 1 - seq0_tile)):
        offsets = tile * TILE + (lane ^ jnp.where(seq == core, 0, TILE // 2))
        places.append(offsets - token_places(offsets, lengths[seq])[0])
    own_tables = rotary(jnp.concatenate(places))
    unit_lengths = lax.dynamic_index_in_dim(lengths, unit_seq, 0, keepdims=False)
    relative = (jnp.arange(TILES, dtype=jnp.int32)[:, None] * TILE + (lane ^ unit_swap)[None, :]).reshape(-1)
    offsets = unit_half * UNIT + relative
    start, padding = token_places(offsets, unit_lengths)
    unit_tables = rotary(offsets - start)
    low = jnp.where(padding, offsets, jnp.maximum(start, offsets - (WINDOW - 1)))
    low = (low - unit_half * UNIT).reshape(1, UNIT)
    pos = relative.reshape(1, UNIT)

    def to_units(values):
        return lax.all_to_all(values.reshape(TILES, -1, TILE), CHIPS, 0, 0, tiled=True)

    def halo_of(got):
        last = lax.dynamic_index_in_dim(got, last_chip, 0, keepdims=False)
        return lax.ppermute(last[HEAD:QKV], "xh", SWAP)

    def finish_attention(packed, edge, tail):
        edge = lax.ppermute(edge, "xh", SWAP)
        return to_units(add_edge(at, packed, tail, edge, *unit_tables))

    small = (norm_gain, norm_bias, qkv_bias, out_bias, up_bias, down_bias)

    def gather_chunks(chunk):
        return lax.all_gather(chunk, ACROSS, axis=0, tiled=True).reshape(16, CHUNK, HALF)

    weights = begin(at, qkv_weight, up_weight, down_weight, small)
    own_qkv, other_qkv = [weights], [lax.ppermute(weights, "zh", SWAP)]
    rest = [gather_chunks(other_qkv[0][CHUNK_AT:])]
    tokens = cotangent[0]
    dhid1 = (tokens, exchange(tokens))
    gain, offset, b_qkv, b_rest, b_up = spread_small(at, weights, other_qkv[0])
    _, hat0, inverse0, act = norms(at, hidden_in[0], None, gain[0], offset[0])
    acts0 = (act, exchange(act))
    got0 = to_units(project_qkv(at, *acts0, own_qkv[0], other_qkv[0], b_qkv[0], *own_tables))
    rows, weights = begin_rest(at, qkv_weight, up_weight, down_weight, out_weight)
    rows, weights = held(at, [rows, weights], (got0,))
    rows = lax.ppermute(rows, "zh", SWAP)
    own_qkv.append(weights)
    other_qkv.append(lax.ppermute(weights, "zh", SWAP))
    outs = (out_weight, rows)
    halo0 = halo_of(got0)
    ctx0, *saved0 = attention(at, got0, halo0, low, pos)
    rest.append(gather_chunks(held(at, [rows[REST_CHUNK:]])[0]))
    ctx0 = to_units(ctx0)
    gate0, slope0, total = feed_forward(at, *acts0, b_up[0], up_weight, down_weight, rest, 0)
    dctx1 = grad_ctx(at, *dhid1, outs, 1)
    keep, give = attention_out(at, ctx0, outs, total, 0)
    added = (keep, exchange(give), b_rest[0])

    stream, hat1, inverse1, act = norms(at, hidden_in[0], added, gain[1], offset[1])
    acts1 = (act, exchange(act))
    got1 = to_units(project_qkv(at, *acts1, own_qkv[1], other_qkv[1], b_qkv[1], *own_tables, dctx1))
    gate1, slope1, mlp1 = feed_forward(at, *acts1, b_up[1], up_weight, down_weight, rest, 1)
    dup1, keep, give, sum_up1, sent = mlp_back(
        at, *dhid1, slope1, up_weight, down_weight, rest, 1, (*acts1, gate1)
    )
    second1 = (keep, exchange(give))
    late1 = lax.ppermute(held(at, [sent], (got1,))[0], "zh", SWAP)
    halo1 = halo_of(got1)
    packed = attention(at, got1, halo1, low, pos, unit_tables)
    dqkv1 = finish_attention(*packed)
    grads1 = own_grads(at, *acts1, *dhid1, gate1, dup1, late1)
    part1 = sum_x(held(at, [grads1], (dqkv1,))[0])
    keep, give, sum_qkv1 = qkv_back(at, dqkv1, own_qkv[1], other_qkv[1])
    first1 = (keep, exchange(give))
    early0 = lax.ppermute(pack_early(at, *acts0, gate0, ctx0), "zh", SWAP)
    dstream, low_stream, sum_norm1 = norm_back(at, first1, second1, hat1, inverse1, gain[1], tokens)

    dhid0 = (low_stream, exchange(low_stream))
    dctx0 = to_units(grad_ctx(at, *dhid0, outs, 0))
    dup0, keep, give, sum_up0, sent = mlp_back(at, *dhid0, slope0, up_weight, down_weight, rest, 0)
    second0 = (keep, exchange(give))
    gradsq = grads_qkv(at, dqkv1, *acts1, *dhid1)
    gradsq, sent, part1 = held(at, [gradsq, sent, part1], (dctx0, early0))
    late0 = lax.ppermute(sent, "zh", SWAP)
    part1 = sum_y(part1)
    partq = sum_x(gradsq)
    packed = attention(at, got0, halo0, low, pos, unit_tables, dctx0, saved0)
    dqkv0 = finish_attention(*packed)
    grads0 = own_grads(at, *acts0, *dhid0, gate0, dup0, late0, early0, ctx0)
    part0 = sum_grid(held(at, [grads0], (dqkv0,))[0])
    keep, give, sum_qkv0 = qkv_back(at, dqkv0, own_qkv[0], other_qkv[0])
    first0 = (keep, exchange(give))
    dstream, _, sum_norm0 = norm_back(at, first0, second0, hat0, inverse0, gain[0], dstream)
    hidden_grad = dstream[None]
    partq, part1 = held(at, [partq, part1])
    partq = sum_y(partq)

    sums = (sum_norm0, sum_up0, sum_qkv0, sum_norm1, sum_up1, sum_qkv1)
    part_qkv = scatter_sum(qkv_grads_first(at, dqkv0, *acts0, sums, (part0,)))
    part0, partq, near1 = held(at, [part0, partq, sum_near(part1)])
    total = [sum_near(part0), sum_depth(zh, partq), near1]
    total = jnp.concatenate(total)
    long = lax.all_gather(total, ACROSS, axis=0, tiled=True)
    keep, give = attention_out(at, dqkv1, outs, mlp1, 1, (part_qkv,))
    given = exchange(give)
    hidden_out = (stream + (keep + given + b_rest[1])).astype(BF16)[None]
    qkv0 = gather_short(part_qkv)
    g_qkv, g_gain, g_offset, g_hidden, g_again, g_bqkv, g_bup = place_qkv(at, qkv0, exchange(qkv0))
    (long,) = held(at, [long], (given,))
    filled = place_long(at, (long,), ())
    g_up, g_down, g_out, g_qkv = place_long(at, (long, exchange(long)), (*filled, g_qkv))
    return (
        hidden_out,
        hidden_grad,
        g_gain,
        g_offset,
        g_qkv,
        g_bqkv,
        g_out,
        g_hidden,
        g_up,
        g_bup,
        g_down,
        g_again,
    )


def solution(mesh):
    fine = Mesh(
        mesh.devices.reshape(2, 2, 2, 4, 2, 2), ("xh", "xl", "zl", "y", "core", "zh")
    )
    ctx = ("xh", "xl", "zl", "y", "core")
    rows = P(None, "zh", None)
    tokens = P("zh", ctx, None)
    last = P(None, None, "zh")
    bias = P(None, "zh")
    return jax.shard_map(
        local,
        mesh=fine,
        in_specs=(tokens, P("zh", None, None), last, last, rows, bias, rows, bias, rows, bias, rows, bias, tokens),
        out_specs=(tokens, tokens, last, last, rows, bias, rows, bias, rows, bias, rows, bias),
        check_vma=False,
    )
```
